32 devices in a mesh: ctx: 8 (over z, x), fsdp: 4 (over y, core).
Axes of the slice: x: 2, y: 2, z: 4, core: 2. Of those that a mesh axis runs over, the one named last changes fastest.
Arguments:
- tokens: bfloat16 [12, 1024, 576], P('fsdp', 'ctx'), may hold values from -6 to 6
- cotangent: bfloat16 [12, 1024, 576], P('fsdp', 'ctx'), may hold values from -6 to 6
- attn_gain: bfloat16 [576], P('fsdp'), may hold values from 0.5 to 1.5
- w_query: bfloat16 [576, 576], P('fsdp'), may hold values from -0.25 to 0.25
- w_key: bfloat16 [576, 192], P('fsdp'), may hold values from -0.25 to 0.25
- w_value: bfloat16 [576, 192], P('fsdp'), may hold values from -0.25 to 0.25
- w_out: bfloat16 [576, 576], P('fsdp'), may hold values from -1 to 1
- mlp_gain: bfloat16 [576], P('fsdp'), may hold values from 0.5 to 1.5
- w_gate: bfloat16 [576, 1536], P('fsdp'), may hold values from -0.25 to 0.25
- w_up: bfloat16 [576, 1536], P('fsdp'), may hold values from -0.25 to 0.25
- w_down: bfloat16 [1536, 576], P('fsdp'), may hold values from -0.15625 to 0.15625
- seq_lengths: int32 [12], P('fsdp'), may hold values from 256 to 1024, as said below
- seq_starts: int32 [12], P('fsdp'), may hold values from 0 to 768, as said below
Outputs:
- mixed_out: float32 [12, 1024, 576], P('fsdp', 'ctx')
- input_grad: float32 [12, 1024, 576], P('fsdp', 'ctx')
- grad_attn_gain: float32 [576], P('fsdp')
- grad_query: float32 [576, 576], P('fsdp')
- grad_key: float32 [576, 192], P('fsdp')
- grad_value: float32 [576, 192], P('fsdp')
- grad_out: float32 [576, 576], P('fsdp')
- grad_mlp_gain: float32 [576], P('fsdp')
- grad_gate: float32 [576, 1536], P('fsdp')
- grad_up: float32 [576, 1536], P('fsdp')
- grad_down: float32 [1536, 576], P('fsdp')
The draws below stay inside these ranges and needn't reach their ends.
Inputs may be any that keep to these rules, and one draw needn't show every extreme that they name: `seq_lengths`: in each group of 3 consecutive rows (the rows of one fsdp index) one row, chosen by the seed, holds a sequence of 1024 tokens starting at 0; every sequence ends within its row. seq_starts + seq_lengths <= 1024 in every row.
All inputs are finite; a program needn't handle non-finite values.
Results may differ from the reference program's by a relative error of at most 0.039.
Values may be sent and summed in bfloat16 or wider, within the bound.
No kernel may reach another device: no remote copies, remote signals or barrier semaphores. Data moves between devices by JAX's collectives and lax.ppermute only.
A program may use at most 192 MiB of HBM per device.

```python
import jax
import jax.numpy as jnp
from jax import lax

D = 576
HEADS = 9
KV_HEADS = 3
HEAD_DIM = 64
FF = 1536
SEQS = 3
LEN = 1024
SEQ_ALL = 12
N_FSDP = 4


def sequence_spans(key):
    pick_key, length_key, start_key = jax.random.split(key, 3)
    group_count = SEQ_ALL // SEQS
    chosen = jax.random.randint(pick_key, (group_count,), 0, SEQS)
    drawn_lengths = jax.random.randint(length_key, (SEQ_ALL,), LEN // 4, LEN + 1)
    row_number = jnp.arange(SEQ_ALL, dtype=jnp.int32)
    slot_in_group = row_number % SEQS
    full_row = slot_in_group == jnp.repeat(chosen, SEQS)
    shortest_row = row_number == (chosen[0] + 1) % SEQS
    final_lengths = jnp.where(full_row, LEN, jnp.where(shortest_row, LEN // 4, drawn_lengths)).astype(jnp.int32)
    room_left = LEN - final_lengths
    drawn_starts = jax.random.randint(start_key, (SEQ_ALL,), 0, room_left + 1)
    final_starts = jnp.where(full_row, 0, jnp.where(shortest_row, room_left, drawn_starts))
    return (final_lengths, final_starts.astype(jnp.int32))


def draw_seq_lengths(key, part):
    spans = sequence_spans(key)
    return spans[0]


def draw_seq_starts(key, part):
    spans = sequence_spans(key)
    return spans[1]


def levels(stream_key, dims, cuts, smallest, top_value):
    level, own = 1.0, jax.random.fold_in(stream_key, 6)
    for position, parts in cuts:
        draws = jnp.exp(jax.random.uniform(jax.random.fold_in(own, position), (parts,), jnp.float32, smallest / len(cuts), top_value / len(cuts)))
        level = level * jnp.repeat(draws, dims[position] // parts).reshape([-1 if axis == position else 1 for axis in range(len(dims))])
    return level


def scatter_about(key, shape, scale, limit, cuts=(), kind=jnp.bfloat16):
    gain = levels(key, shape, cuts, -0.22, 0.18) if cuts else 1.0
    drawn = jax.random.normal(key, shape, jnp.float32) * scale * gain
    return jnp.minimum(jnp.maximum(drawn, -limit), limit).astype(kind)


def setup_inputs(seed: int = 0) -> dict:
    splits = jax.random.split(jax.random.key(seed), 14)
    return {
        "tokens": scatter_about(splits[0], (SEQ_ALL, LEN, D), 1.0, 6.0, ((0, 4), (1, 8))),
        "cotangent": scatter_about(splits[1], (SEQ_ALL, LEN, D), 1.0, 6.0, ((0, 4), (1, 8))),
        "attn_gain": jnp.clip(1.0 + 0.1 * jax.random.normal(splits[2], (D,), jnp.float32), 0.5, 1.5).astype(jnp.bfloat16),
        "w_query": scatter_about(splits[3], (D, HEADS * HEAD_DIM), D ** -0.5, 0.25, ((0, 4),)),
        "w_key": scatter_about(splits[4], (D, KV_HEADS * HEAD_DIM), D ** -0.5, 0.25, ((0, 4),)),
        "w_value": scatter_about(splits[5], (D, KV_HEADS * HEAD_DIM), D ** -0.5, 0.25, ((0, 4),)),
        "w_out": scatter_about(splits[6], (HEADS * HEAD_DIM, D), (HEADS * HEAD_DIM // 16) ** -0.5, 1.0, ((0, 4),)),
        "mlp_gain": jnp.clip(1.0 + 0.1 * jax.random.normal(splits[7], (D,), jnp.float32), 0.5, 1.5).astype(jnp.bfloat16),
        "w_gate": scatter_about(splits[8], (D, FF), D ** -0.5, 0.25, ((0, 4),)),
        "w_up": scatter_about(splits[9], (D, FF), D ** -0.5, 0.25, ((0, 4),)),
        "w_down": scatter_about(splits[10], (FF, D), FF ** -0.5, 0.15625, ((0, 4),)),
        "seq_lengths": draw_seq_lengths(jax.random.fold_in(splits[13], 71), 0),
        "seq_starts": draw_seq_starts(jax.random.fold_in(splits[13], 71), 0),
    }


@jax.custom_vjp
def low(v):
    return lax.optimization_barrier(v.astype(jnp.bfloat16)).astype(jnp.float32)

@jax.custom_vjp
def low_back(v):
    return v

def low_keep(v):
    return (low(v), None)

def low_pass(kept, grad):
    return (grad,)

def back_keep(v):
    return (v, None)

def back_low(kept, grad):
    return (low(grad),)
low.defvjp(low_keep, low_pass)
low_back.defvjp(back_keep, back_low)
EPSILON = 1e-05
THETA = 100000.0
HIGHEST = lax.Precision.HIGHEST

def rounded_both(value_in):
    return low(low_back(value_in))

def rms_scale(rows, gain_row):
    return rows * lax.rsqrt(lax.optimization_barrier(jnp.mean(rows * rows, axis=-1, keepdims=True)) + EPSILON) * gain_row

def rotate(tensor, cosines, sines):
    half_dim = tensor.shape[-1] // 2
    first_half = tensor[..., :half_dim]
    second_half = tensor[..., half_dim:]
    return jnp.concatenate([first_half * cosines - second_half * sines, second_half * cosines + first_half * sines], axis=-1)

def seq_mask(query_places, key_places, starts, lengths):
    seq_ends = starts + lengths
    query_inside = (query_places[None, :] >= starts[:, None]) & (query_places[None, :] < seq_ends[:, None])
    key_inside = (key_places[None, :] >= starts[:, None]) & (key_places[None, :] < seq_ends[:, None])
    causal = key_places[None, :] <= query_places[:, None]
    diagonal = key_places[None, :] == query_places[:, None]
    return causal[None] & query_inside[:, :, None] & key_inside[:, None, :] | diagonal[None]

def attend_group(pieces):
    queries, keys_rot, values_rows, starts, lengths = pieces
    places = jnp.arange(LEN, dtype=jnp.int32)
    allowed = seq_mask(places, places, starts, lengths)
    score_scale = HEAD_DIM ** (-0.5)
    scores = low_back(jnp.einsum('sqkgd,stkd->skgqt', queries, keys_rot, precision=HIGHEST) * score_scale)
    masked = jnp.where(allowed[:, None, None], scores, -1e+30)
    weights = low(jax.nn.softmax(masked, axis=-1))
    return jnp.einsum('skgqt,stkd->sqkgd', weights, values_rows, precision=HIGHEST)

def layer_forward(tokens_in, gain_one, query_mat, key_mat, value_mat, out_mat, gain_two, gate_mat, up_mat, down_mat, starts, lengths):
    group_size = HEADS // KV_HEADS
    flat_rows = tokens_in.reshape(SEQ_ALL * LEN, D)
    normed = low(rms_scale(flat_rows, gain_one))
    q_lin = low_back(jnp.dot(normed, query_mat, precision=HIGHEST))
    k_lin = low_back(jnp.dot(normed, key_mat, precision=HIGHEST))
    values_rows = rounded_both(jnp.dot(normed, value_mat, precision=HIGHEST))
    places = jnp.arange(LEN, dtype=jnp.int32)
    positions = (places[None, :] - starts[:, None]).astype(jnp.float32)
    frequency = THETA ** (-(2.0 * jnp.arange(HEAD_DIM // 2, dtype=jnp.float32)) / HEAD_DIM)
    angles = positions[:, :, None] * frequency
    cosines = jnp.cos(angles)[:, :, None, :]
    sines = jnp.sin(angles)[:, :, None, :]
    queries = low(rotate(q_lin.reshape(SEQ_ALL, LEN, HEADS, HEAD_DIM), cosines, sines))
    keys_rot = low(rotate(k_lin.reshape(SEQ_ALL, LEN, KV_HEADS, HEAD_DIM), cosines, sines))
    queries = queries.reshape(N_FSDP, SEQS, LEN, KV_HEADS, group_size, HEAD_DIM)
    keys_rot = keys_rot.reshape(N_FSDP, SEQS, LEN, KV_HEADS, HEAD_DIM)
    values_grouped = values_rows.reshape(N_FSDP, SEQS, LEN, KV_HEADS, HEAD_DIM)
    attended = lax.map(jax.checkpoint(attend_group), (queries, keys_rot, values_grouped, starts.reshape(N_FSDP, SEQS), lengths.reshape(N_FSDP, SEQS)))
    attended = rounded_both(attended.reshape(SEQ_ALL * LEN, HEADS * HEAD_DIM))
    middle = flat_rows + low_back(jnp.dot(attended, out_mat, precision=HIGHEST))
    normed_two = low(rms_scale(middle, gain_two))
    gate_lin = low_back(jnp.dot(normed_two, gate_mat, precision=HIGHEST))
    up_lin = low_back(jnp.dot(normed_two, up_mat, precision=HIGHEST))
    hidden = low(jax.nn.silu(gate_lin) * up_lin)
    result = middle + jnp.dot(hidden, down_mat, precision=HIGHEST)
    return result.reshape(SEQ_ALL, LEN, D)

def reference(tokens, cotangent, attn_gain, w_query, w_key, w_value, w_out, mlp_gain, w_gate, w_up, w_down, seq_lengths, seq_starts):
    floats_in = tuple((item.astype(jnp.float32) for item in (tokens, attn_gain, w_query, w_key, w_value, w_out, mlp_gain, w_gate, w_up, w_down)))

    def forward_only(*values_in):
        return layer_forward(*values_in, seq_starts, seq_lengths)
    result, pullback = jax.vjp(forward_only, *floats_in)
    gradients = pullback(cotangent.astype(jnp.float32))
    return (result, gradients[0], gradients[1], gradients[2], gradients[3], gradients[4], gradients[5], gradients[6], gradients[7], gradients[8], gradients[9])
```

```python
import functools
import math

import jax
import jax.numpy as jnp
from jax import lax
from jax.experimental import pallas as pl
from jax.experimental.pallas import tpu as pltpu
from jax.sharding import PartitionSpec as P

HEADS = 9
KV_HEADS = 3
HEAD_DIM = 64
GROUP = HEADS // KV_HEADS
LANES = 128
EPSILON = 1e-05
THETA = 100000.0
SCALE = HEAD_DIM ** (-0.5)
MASKED = -2e30
LOWEST = -1e30
FAR = 1 << 29
CHUNKS = 8
SLOTS = (0, 2, 1, 3)
BF16 = jnp.bfloat16
F32 = jnp.float32
NN = (((1,), (0,)), ((), ()))
NT = (((1,), (1,)), ((), ()))
TN = (((0,), (0,)), ((), ()))
VMEM_LIMIT = 56 * 1024 * 1024


def dot(a, b, dims=NN):
    return lax.dot_general(a, b, dims, preferred_element_type=F32)


def call(kernel, out_shape, in_specs=None, cost=(0, 0, 0), **kwargs):
    return pl.pallas_call(
        kernel,
        out_shape=out_shape,
        in_specs=in_specs,
        compiler_params=pltpu.CompilerParams(vmem_limit_bytes=VMEM_LIMIT),
        cost_estimate=pl.CostEstimate(
            flops=int(cost[0]), bytes_accessed=int(cost[1]), transcendentals=int(cost[2])
        ),
        **kwargs,
    )


def sds(shape, dtype):
    return jax.ShapeDtypeStruct(shape, dtype)


def lane_of(shape):
    return lax.broadcasted_iota(jnp.int32, shape, 1)


def swap_halves(tile):
    lane = lane_of(tile.shape) % HEAD_DIM
    return jnp.where(
        lane < HEAD_DIM // 2, pltpu.roll(tile, LANES - 32, 1), pltpu.roll(tile, 32, 1)
    )


def half_roll(tile):
    return pltpu.roll(tile, HEAD_DIM, 1)


def assemble(target, index, shards, rows):
    for code, ref in zip((0, 1, 2, 3), shards):
        start = pl.multiple_of((index ^ code) * rows, 16)
        target[pl.ds(start, rows), :] = ref[...]


def inverse_rms(rows):
    return lax.rsqrt(jnp.mean(rows * rows, axis=-1, keepdims=True) + EPSILON)


def qkv_kernel(index_ref, x_ref, w0, w1, w2, w3, cos_ref, sin_ref, w_ref, normed_ref, q_ref, kv_ref):
    assemble(w_ref, index_ref[0], (w0, w1, w2, w3), w0.shape[0])
    width = w_ref.shape[1]
    gains = jnp.transpose(w_ref[:, width - LANES :].astype(F32))
    x = x_ref[...].astype(F32)
    normed = (x * inverse_rms(x) * gains[HEAD_DIM : HEAD_DIM + 1, :]).astype(BF16)
    normed_ref[...] = normed
    cosines, sines = cos_ref[...], sin_ref[...]
    lane = lane_of(cosines.shape)
    low = lane < HEAD_DIM
    cos_kv = jnp.where(low, cosines, 1.0)
    sin_kv = jnp.where(low, sines, 0.0)
    rows = kv_ref.shape[1]
    seqs = x.shape[0] // rows
    for g in range(KV_HEADS):
        tile = dot(normed, w_ref[:, g * LANES : (g + 1) * LANES])
        turned = (tile * cos_kv + swap_halves(tile) * sin_kv).astype(BF16)
        for r in range(seqs):
            kv_ref[r * KV_HEADS + g] = turned[r * rows : (r + 1) * rows]
    first = KV_HEADS * LANES
    lin = dot(normed, w_ref[:, first:])
    for p in range((HEADS + 1) // 2):
        tile = lin[:, p * LANES : (p + 1) * LANES]
        turned = (tile * cosines + swap_halves(tile) * sines) * SCALE
        for h in (2 * p, 2 * p + 1):
            if h < HEADS:
                own = turned if h % 2 == 0 else half_roll(turned)
                own = jnp.where(low, own, 0.0).astype(BF16)
                g, i = divmod(h, GROUP)
                for r in range(seqs):
                    q_ref[r * KV_HEADS + g, i * rows : (i + 1) * rows] = own[
                        r * rows : (r + 1) * rows
                    ]


def pair_places(info_ref, step, rows, axis):
    shape = (1, 2 * rows) if axis == 1 else (2 * rows, 1)
    at = lax.broadcasted_iota(jnp.int32, shape, axis)
    first, second = info_ref[1 + 2 * step], info_ref[2 + 2 * step]
    return jnp.where(at < rows, first + at, second + at - rows)


def query_places(info_ref, rows, axis):
    total = GROUP * rows
    shape = (1, total) if axis == 1 else (total, 1)
    at = lax.broadcasted_iota(jnp.int32, shape, axis)
    return info_ref[0] * rows + at % rows


def seen_of(key_places, q_places, start, end, diagonal):
    key_in = (key_places >= start) & (key_places < end)
    query_in = (q_places >= start) & (q_places < end)
    seen = jnp.where(key_in, key_places, FAR) <= jnp.where(query_in, q_places, -1)
    if diagonal:
        seen = seen | (key_places == q_places)
    return seen


def row_active(info_ref, step, rows, start, end):
    own = info_ref[0] * rows
    first, second = info_ref[1 + 2 * step], info_ref[2 + 2 * step]
    keys_in = ((first < end) & (first + rows > start)) | ((second < end) & (second + rows > start))
    return (own < end) & (own + rows > start) & keys_in & (jnp.minimum(first, second) <= own)


def attend_kernel(steps, diagonal, fresh, info_ref, q_ref, a_ref, b_ref, *refs):
    if fresh:
        max_ref, sum_ref = refs
    else:
        max_in, sum_in, max_ref, sum_ref = refs
    step = pl.program_id(0)
    rows = a_ref.shape[2]
    seqs = q_ref.shape[0] // KV_HEADS
    spans = 1 + 2 * steps

    @pl.when(step == 0)
    def _():
        if fresh:
            max_ref[...] = jnp.full_like(max_ref, LOWEST)
            sum_ref[...] = jnp.zeros_like(sum_ref)
        else:
            max_ref[...] = max_in[...]
            sum_ref[...] = sum_in[...]

    for r in range(seqs):
        start = info_ref[spans + r]
        end = info_ref[spans + seqs + r]

        def one_row(r=r, start=start, end=end):
            seen = seen_of(
                pair_places(info_ref, step, rows, 1),
                query_places(info_ref, rows, 0),
                start,
                end,
                diagonal,
            )
            for g in range(KV_HEADS):
                rg = r * KV_HEADS + g
                kv = jnp.concatenate([a_ref[0, rg], b_ref[0, rg]], axis=0)
                scores = jnp.where(seen, dot(q_ref[rg], kv, NT), MASKED)
                old = max_ref[rg]
                new = jnp.maximum(old, jnp.max(scores, axis=-1, keepdims=True))
                weights = jnp.exp(scores - jnp.concatenate([new, new], axis=1)).astype(BF16)
                ones = jnp.where(lane_of(kv.shape) < HEAD_DIM, jnp.ones_like(kv), kv)
                sum_ref[rg] = sum_ref[rg] * jnp.exp(old - new) + dot(weights, ones)
                max_ref[rg] = new

        if diagonal:
            one_row()
        else:
            pl.when(row_active(info_ref, step, rows, start, end))(one_row)


def attend(info, queries, a, b, carry, diagonal):
    steps = a.shape[0]
    tiles, total, _ = queries.shape
    rows = a.shape[2]
    whole = pl.BlockSpec((tiles, total, LANES), lambda i: (0, 0, 0))
    piece = pl.BlockSpec((1, tiles, rows, LANES), lambda i: (i, 0, 0, 0))
    work = steps * tiles * total * 2 * rows
    return call(
        functools.partial(attend_kernel, steps, diagonal, carry is None),
        (sds((tiles, total, LANES), F32),) * 2,
        [pl.BlockSpec(memory_space=pltpu.SMEM), whole, piece, piece]
        + ([] if carry is None else [whole] * 2),
        cost=(work * 4 * LANES, tiles * total * LANES * 16, work),
        out_specs=(whole, whole),
        grid=(steps,),
    )(info, queries, a, b, *(carry or ()))


def attend_back_kernel(
    steps, diagonal, fresh, info_ref, q_ref, d_ref, stat_ref, a_ref, b_ref, *refs
):
    if fresh:
        dq_ref, da_ref, db_ref = refs
    else:
        dq_in, dq_ref, da_ref, db_ref = refs
    step = pl.program_id(0)
    rows = a_ref.shape[2]
    seqs = q_ref.shape[0] // KV_HEADS
    spans = 1 + 2 * steps

    @pl.when(step == 0)
    def _():
        dq_ref[...] = jnp.zeros_like(dq_ref) if fresh else dq_in[...]

    for r in range(seqs):
        start = info_ref[spans + r]
        end = info_ref[spans + seqs + r]

        def one_row(r=r, start=start, end=end):
            seen = seen_of(
                pair_places(info_ref, step, rows, 0),
                query_places(info_ref, rows, 1),
                start,
                end,
                diagonal,
            )
            for g in range(KV_HEADS):
                rg = r * KV_HEADS + g
                kv = jnp.concatenate([a_ref[0, rg], b_ref[0, rg]], axis=0)
                q, d = q_ref[rg], d_ref[rg]
                log_sum = stat_ref[rg, 0:1, :]
                delta = stat_ref[rg, 1:2, :]
                scores = jnp.where(seen, dot(kv, q, NT), MASKED)
                probs = jnp.exp(scores - log_sum)
                d_scores = (probs * (dot(kv, d, NT) - delta)).astype(BF16)
                grad = (dot(d_scores, q) + dot(probs.astype(BF16), d)).astype(BF16)
                da_ref[0, rg] = grad[:rows]
                db_ref[0, rg] = grad[rows:]
                dq_ref[rg] = dq_ref[rg] + dot(d_scores, kv, TN)

        if diagonal:
            one_row()
        else:
            active = row_active(info_ref, step, rows, start, end)
            pl.when(active)(one_row)

            @pl.when(jnp.logical_not(active))
            def _(r=r):
                for g in range(KV_HEADS):
                    rg = r * KV_HEADS + g
                    da_ref[0, rg] = jnp.zeros((rows, LANES), BF16)
                    db_ref[0, rg] = jnp.zeros((rows, LANES), BF16)


def attend_back(info, queries, d_out, stats, a, b, carry, diagonal):
    steps = a.shape[0]
    tiles, total, _ = queries.shape
    rows = a.shape[2]
    whole = pl.BlockSpec((tiles, total, LANES), lambda i: (0, 0, 0))
    stat = pl.BlockSpec(stats.shape, lambda i: (0, 0, 0))
    piece = pl.BlockSpec((1, tiles, rows, LANES), lambda i: (i, 0, 0, 0))
    work = steps * tiles * total * 2 * rows
    return call(
        functools.partial(attend_back_kernel, steps, diagonal, carry is None),
        (sds((tiles, total, LANES), F32), sds(a.shape, BF16), sds(b.shape, BF16)),
        [pl.BlockSpec(memory_space=pltpu.SMEM), whole, whole, stat, piece, piece]
        + ([] if carry is None else [whole]),
        cost=(work * 10 * LANES, tiles * total * LANES * 16, work),
        out_specs=(whole, piece, piece),
        grid=(steps,),
    )(info, queries, d_out, stats, a, b, *(() if carry is None else (carry,)))


def middle_kernel(
    index_ref,
    x_ref,
    cot_ref,
    gain_ref,
    max_ref,
    sum_ref,
    gu0,
    gu1,
    gu2,
    gu3,
    do0,
    do1,
    do2,
    do3,
    out_ref,
    d_mid_ref,
    d_ref,
    stat_ref,
    keep_gu,
    send_gu,
    keep_do,
    send_do,
    w_gu,
    w_down,
    w_out,
    att_ref,
    n2_ref,
    dn2_ref,
    g_gu,
    g_down,
    g_out,
    slot_ref,
):
    index = index_ref[0]
    dim = x_ref.shape[1]
    ff = w_down.shape[0]
    fd, fs = ff // 4, dim // 4
    assemble(w_gu, index, (gu0, gu1, gu2, gu3), fs)
    for code, ref in zip((0, 1, 2, 3), (do0, do1, do2, do3)):
        shard = index ^ code
        w_down[pl.ds(pl.multiple_of(shard * fd, 16), fd), :] = ref[0:fd, :]
        w_out[pl.ds(pl.multiple_of(shard * fs, 16), fs), :] = ref[fd:, :]
    tiles, total, _ = max_ref.shape
    seqs = tiles // KV_HEADS
    rows = total // GROUP
    low = lane_of((total, LANES)) < HEAD_DIM
    low_rows = low[:rows]
    outs = []
    for rg in range(tiles):
        sums = sum_ref[rg]
        turned = half_roll(sums)
        both = jnp.where(low, sums, turned)
        log_sum = max_ref[rg] + jnp.log(both)
        stat_ref[rg, 0:1, :] = jnp.transpose(log_sum)[0:1, :]
        normal = jnp.where(low, 0.0, sums / both)
        sum_ref_row = normal
        outs.append(sum_ref_row)
    for r in range(seqs):
        for p in range((HEADS + 1) // 2):
            g, i = divmod(2 * p, GROUP)
            tile = half_roll(outs[r * KV_HEADS + g][i * rows : (i + 1) * rows])
            if 2 * p + 1 < HEADS:
                g, i = divmod(2 * p + 1, GROUP)
                tile = jnp.where(
                    low_rows, tile, outs[r * KV_HEADS + g][i * rows : (i + 1) * rows]
                )
                att_ref[r * rows : (r + 1) * rows, p * LANES : (p + 1) * LANES] = tile.astype(BF16)
            else:
                att_ref[r * rows : (r + 1) * rows, p * LANES :] = tile[:, :HEAD_DIM].astype(BF16)
    att = att_ref[...]
    cot = cot_ref[...]
    mid = x_ref[...].astype(F32) + dot(att, w_out[...])
    inv = inverse_rms(mid)
    gain = gain_ref[...]
    n2 = (mid * inv * gain).astype(BF16)
    n2_ref[...] = n2
    out_ref[...] = mid
    dn2_ref[...] = jnp.zeros_like(dn2_ref)
    width = ff // 2

    def ff_step(i, carry):
        at = pl.multiple_of(i * width, width)
        cols, cols_up = pl.ds(at, width), pl.ds(pl.multiple_of(at + ff, width), width)
        n2 = n2_ref[...]
        w_g, w_u, w_d = w_gu[:, cols], w_gu[:, cols_up], w_down[cols, :]
        gate = dot(n2, w_g)
        up = dot(n2, w_u)
        sig = 1.0 / (1.0 + jnp.exp(-gate))
        silu = gate * sig
        hidden = (silu * up).astype(BF16)
        out_ref[...] += dot(hidden, w_d)
        d_hidden = dot(cot_ref[...], w_d, NT)
        d_gate = (d_hidden * up * sig * (1.0 + gate * (1.0 - sig))).astype(BF16)
        d_up = (d_hidden * silu).astype(BF16)
        g_down[cols, :] = dot(hidden, cot_ref[...], TN)
        g_gu[:, cols] = dot(n2, d_gate, TN)
        g_gu[:, cols_up] = dot(n2, d_up, TN)
        dn2_ref[...] += dot(d_gate, w_g, NT) + dot(d_up, w_u, NT)
        return carry

    lax.fori_loop(0, 2, ff_step, 0)
    dn2 = dn2_ref[...]
    scaled = dn2 * gain
    gain_grad = jnp.sum(dn2 * mid * inv, axis=0, keepdims=True)
    d_mid = (
        cot.astype(F32)
        + inv * scaled
        - mid * (inv * inv * inv) * jnp.mean(scaled * mid, axis=-1, keepdims=True)
    )
    d_mid_ref[...] = d_mid
    d_low = d_mid.astype(BF16)
    g_out[...] = dot(att, d_low, TN)
    d_att = dot(d_low, w_out[...], NT)
    for r in range(seqs):
        for p in range((HEADS + 1) // 2):
            stop = min((p + 1) * LANES, dim)
            tile = d_att[r * rows : (r + 1) * rows, p * LANES : stop]
            if stop - p * LANES < LANES:
                tile = jnp.concatenate([tile, jnp.zeros_like(tile)], axis=1)
            for h in (2 * p, 2 * p + 1):
                if h < HEADS:
                    own = half_roll(tile) if h % 2 == 0 else tile
                    own = jnp.where(low_rows, 0.0, own).astype(BF16)
                    g, i = divmod(h, GROUP)
                    d_ref[r * KV_HEADS + g, i * rows : (i + 1) * rows] = own
    for rg in range(tiles):
        prod = d_ref[rg].astype(F32) * outs[rg]
        stat_ref[rg, 1:2, :] = jnp.sum(jnp.transpose(prod), axis=0, keepdims=True)
    cols = 2 * ff // CHUNKS
    part = dim // CHUNKS
    for slot in range(4):
        shard = index ^ SLOTS[slot]
        to_gu, to_do = (keep_gu, keep_do) if slot < 2 else (send_gu, send_do)
        at = pl.ds(pl.multiple_of(shard * fs, 16), fs)
        for c in range(CHUNKS):
            to_gu[slot % 2, c] = g_gu[at, c * cols : (c + 1) * cols].astype(BF16)
        slot_ref[0:fd, :] = g_down[pl.ds(pl.multiple_of(shard * fd, 16), fd), :]
        slot_ref[fd : fd + fs, :] = g_out[at, :]
        slot_ref[fd + fs :, :] = jnp.broadcast_to(gain_grad, (dim - fd - fs, dim))
        for c in range(CHUNKS):
            to_do[slot % 2, c] = slot_ref[c * part : (c + 1) * part, :].astype(BF16)


def middle(index, x, cot, gain, top, sums, gu, do):
    n, dim = x.shape
    tiles, total, _ = top.shape
    ff2 = gu[0].shape[1]
    ff = ff2 // 2
    pair_gu = sds((2, CHUNKS, dim // 4, ff2 // CHUNKS), BF16)
    pair_do = sds((2, CHUNKS, dim // CHUNKS, dim), BF16)
    vm = pl.BlockSpec(memory_space=pltpu.VMEM)
    return call(
        middle_kernel,
        (
            sds((n, dim), F32),
            sds((n, dim), F32),
            sds((tiles, total, LANES), BF16),
            sds((tiles, 8, total), F32),
            pair_gu,
            pair_gu,
            pair_do,
            pair_do,
        ),
        [pl.BlockSpec(memory_space=pltpu.SMEM)] + [vm] * 13,
        cost=(2 * n * dim * (3 * dim + 9 * ff), 20e6, 2 * n * ff),
        out_specs=(vm,) * 8,
        scratch_shapes=[
            pltpu.VMEM((dim, ff2), BF16),
            pltpu.VMEM((ff, dim), BF16),
            pltpu.VMEM((dim, dim), BF16),
            pltpu.VMEM((n, dim), BF16),
            pltpu.VMEM((n, dim), BF16),
            pltpu.VMEM((n, dim), F32),
            pltpu.VMEM((dim, ff2), F32),
            pltpu.VMEM((ff, dim), F32),
            pltpu.VMEM((dim, dim), F32),
            pltpu.VMEM((dim, dim), F32),
        ],
    )(index, x, cot, gain, top, sums, *gu, *do)


def end_kernel(
    index_ref,
    x_ref,
    normed_ref,
    w_ref,
    cos_ref,
    sin_ref,
    dq_ref,
    dkv_ref,
    d_mid_ref,
    grad_ref,
    keep,
    send,
    lin_ref,
    g_ref,
):
    index = index_ref[0]
    width = w_ref.shape[1]
    rows = dkv_ref.shape[1]
    seqs = dkv_ref.shape[0] // KV_HEADS
    low = lane_of((rows, LANES)) < HEAD_DIM
    for r in range(seqs):
        at = slice(r * rows, (r + 1) * rows)
        cosines, sines = cos_ref[at, :], sin_ref[at, :]
        cos_kv = jnp.where(low, cosines, 1.0)
        sin_kv = jnp.where(low, sines, 0.0)
        for g in range(KV_HEADS):
            tile = dkv_ref[r * KV_HEADS + g].astype(F32)
            back = tile * cos_kv - swap_halves(tile) * sin_kv
            lin_ref[at, g * LANES : (g + 1) * LANES] = back.astype(BF16)
        first = KV_HEADS * LANES
        for p in range((HEADS + 1) // 2):
            backs = []
            for h in (2 * p, 2 * p + 1):
                if h < HEADS:
                    g, i = divmod(h, GROUP)
                    tile = dq_ref[r * KV_HEADS + g, i * rows : (i + 1) * rows]
                    backs.append((tile * cosines - swap_halves(tile) * sines) * SCALE)
                else:
                    backs.append(jnp.zeros((rows, LANES), F32))
            tile = jnp.where(low, backs[0], half_roll(backs[1]))
            lin_ref[at, first + p * LANES : first + (p + 1) * LANES] = tile.astype(BF16)
    lin = lin_ref[...]
    g_ref[...] = dot(normed_ref[...], lin, TN)
    d_normed = dot(lin, w_ref[...], NT)
    gains = jnp.transpose(w_ref[:, width - LANES :].astype(F32))
    gain = gains[HEAD_DIM : HEAD_DIM + 1, :]
    x = x_ref[...].astype(F32)
    inv = inverse_rms(x)
    scaled = d_normed * gain
    grad_ref[...] = (
        d_mid_ref[...]
        + inv * scaled
        - x * (inv * inv * inv) * jnp.mean(scaled * x, axis=-1, keepdims=True)
    )
    gain_grad = jnp.sum(d_normed * x * inv, axis=0, keepdims=True)
    dim = x.shape[1]
    fs = dim // 4
    for slot in range(4):
        start = (index ^ SLOTS[slot]) * fs
        to = keep if slot < 2 else send
        for c in range(CHUNKS):
            half, quarter = divmod(c, 4)
            size, cols = fs // 2, width // 4
            at = pl.ds(pl.multiple_of(start + half * size, 8), size)
            tile = g_ref[at, quarter * cols : (quarter + 1) * cols]
            if c == 3:
                pad = jnp.concatenate(
                    [gain_grad[:, k * HEAD_DIM : (k + 1) * HEAD_DIM] for k in range(HEADS)]
                    + [jnp.zeros((size - HEADS, HEAD_DIM), F32)],
                    axis=0,
                )
                pad = jnp.concatenate([tile[:, : cols - HEAD_DIM], pad], axis=1)
                tile = pad
            to[slot % 2, c] = tile.astype(BF16)


def finish(index, x, normed, w, cosines, sines, dq, dkv, d_mid):
    n, dim = x.shape
    width = w.shape[1]
    vm = pl.BlockSpec(memory_space=pltpu.VMEM)
    pair = sds((2, CHUNKS, dim // 8, width // 4), BF16)
    return call(
        end_kernel,
        (sds((n, dim), F32), pair, pair),
        [pl.BlockSpec(memory_space=pltpu.SMEM)] + [vm] * 8,
        cost=(4 * n * dim * width, 8e6, 0),
        out_specs=(vm,) * 3,
        scratch_shapes=[pltpu.VMEM((n, width), BF16), pltpu.VMEM((dim, width), F32)],
    )(index, x, normed, w, cosines, sines, dq, dkv, d_mid)


def flip(x, axis, mask):
    n = lax.axis_size(axis)
    return lax.ppermute(x, axis, [(i, i ^ mask) for i in range(n)])


def gather_shards(own):
    across = flip(own, "fsdp", 2)
    return own, flip(own, "fsdp", 1), across, flip(across, "fsdp", 1)


def add(a, b):
    return (a.astype(F32) + b.astype(F32)).astype(BF16)


def pick(x, i):
    return lax.dynamic_index_in_dim(x, i, 0, keepdims=False)


def join(bit, mine, other):
    flag = bit == 0
    return jnp.stack([jnp.where(flag, mine, other), jnp.where(flag, other, mine)])


def reduce_all(keep, send):
    got = flip(send, "fsdp", 1)
    away = add(keep[1], got[1])
    total = add(add(keep[0], got[0]), flip(away, "fsdp", 2))
    n = lax.axis_size("ctx")
    me = lax.axis_index("ctx")
    bits = n.bit_length() - 1
    cut = min(bits, 3)
    shape = total.shape[1:]
    for b in range(cut):
        bit = (me >> b) & 1
        halves = total.reshape((2, -1) + shape)
        total = add(pick(halves, bit), flip(pick(halves, 1 - bit), "ctx", 1 << b))
    for b in range(cut, bits):
        total = add(total, flip(total, "ctx", 1 << b))
    for b in reversed(range(cut)):
        bit = (me >> b) & 1
        total = join(bit, total, flip(total, "ctx", 1 << b)).reshape((-1,) + shape)
    return total


def local(
    tokens,
    cotangent,
    attn_gain,
    w_query,
    w_key,
    w_value,
    w_out,
    mlp_gain,
    w_gate,
    w_up,
    w_down,
    seq_lengths,
    seq_starts,
):
    seqs, rows, dim = tokens.shape
    n = seqs * rows
    n_ctx = lax.axis_size("ctx")
    me = lax.axis_index("ctx")
    index = lax.axis_index("fsdp").reshape(1).astype(jnp.int32)
    fs = w_query.shape[0]
    x = tokens.reshape(n, dim)
    cot = cotangent.reshape(n, dim)

    kv_cols = []
    for g in range(KV_HEADS):
        kv_cols += [
            w_key[:, g * HEAD_DIM : (g + 1) * HEAD_DIM],
            w_value[:, g * HEAD_DIM : (g + 1) * HEAD_DIM],
        ]
    used = KV_HEADS * LANES + HEADS * HEAD_DIM + 2
    pad = -used % LANES
    first = jnp.concatenate(
        kv_cols
        + [w_query, attn_gain[:, None], mlp_gain[:, None], jnp.zeros((fs, pad), BF16)],
        axis=1,
    )
    first_shards = gather_shards(first)
    gu_shards = gather_shards(jnp.concatenate([w_gate, w_up], axis=1))
    do_shards = gather_shards(jnp.concatenate([w_down, w_out], axis=0))

    places = me * rows + jnp.arange(rows, dtype=jnp.int32)
    positions = (places[None, :] - seq_starts[:, None]).astype(F32)
    frequency = THETA ** (-(2.0 * jnp.arange(HEAD_DIM // 2, dtype=F32)) / HEAD_DIM)
    angles = (positions[:, :, None] * frequency).reshape(n, HEAD_DIM // 2)
    cos, sin = jnp.cos(angles), jnp.sin(angles)
    cosines = jnp.concatenate([cos] * 4, axis=1)
    sines = jnp.concatenate([-sin, sin] * 2, axis=1)

    width = first.shape[1]
    tiles = seqs * KV_HEADS
    vm = pl.BlockSpec(memory_space=pltpu.VMEM)
    weights, normed, queries, kv = call(
        qkv_kernel,
        (
            sds((dim, width), BF16),
            sds((n, dim), BF16),
            sds((tiles, GROUP * rows, LANES), BF16),
            sds((tiles, rows, LANES), BF16),
        ),
        [pl.BlockSpec(memory_space=pltpu.SMEM)] + [vm] * 7,
        cost=(2 * n * dim * width, 6e6, 0),
        out_specs=(vm,) * 4,
    )(index, x, *first_shards, cosines, sines)
    gain_two = weights[:, used - 1].astype(F32)[None, :]

    spans = [seq_starts.astype(jnp.int32), (seq_starts + seq_lengths).astype(jnp.int32)]

    def info_of(bases):
        return jnp.concatenate([me.reshape(1).astype(jnp.int32), bases.astype(jnp.int32)] + spans)

    x_bit = me % 2
    if n_ctx <= 8 and n_ctx % 2 == 0:
        levels = n_ctx // 2
        up = [(i, i + 2) for i in range(n_ctx - 2)]
        down = [(i + 2, i) for i in range(n_ctx - 2)]
        pieces = []
        piece = kv
        for k in range(levels):
            other = flip(piece, "ctx", 1)
            pair = (me // 2 - k) * 2
            bases = jnp.stack([pair + x_bit, pair + 1 - x_bit]) * rows
            bases = jnp.where(pair >= 0, bases, FAR)
            pieces.append((info_of(bases), piece[None], other[None]))
            if k + 1 < levels:
                piece = lax.ppermute(piece, "ctx", up)
        carry = None
        for k in range(levels):
            info, a, b = pieces[k]
            carry = attend(info, queries, a, b, carry, k == 0)
    else:
        every = lax.all_gather(kv, "ctx", axis=0)
        info = info_of(jnp.arange(n_ctx, dtype=jnp.int32) * rows)
        carry = attend(info, queries, every[0::2], every[1::2], None, True)

    result, d_mid, d_out, stats, keep_gu, send_gu, keep_do, send_do = middle(
        index, x, cot, gain_two, carry[0], carry[1], gu_shards, do_shards
    )

    if n_ctx <= 8 and n_ctx % 2 == 0:
        dq = None
        total = None
        for k in reversed(range(levels)):
            info, a, b = pieces[k]
            dq, da, db = attend_back(info, queries, d_out, stats, a, b, dq, k == 0)
            total_k = add(da[0], flip(db[0], "ctx", 1))
            if total is not None:
                total_k = add(total_k, lax.ppermute(total, "ctx", down))
            total = total_k
        dkv = total
    else:
        dq, da, db = attend_back(
            info, queries, d_out, stats, every[0::2], every[1::2], None, True
        )
        partial = jnp.stack([da, db], axis=1).reshape((n_ctx,) + da.shape[1:])
        dkv = lax.psum_scatter(partial, "ctx", scatter_dimension=0, tiled=False)

    do_sum = reduce_all(keep_do, send_do)
    gu_sum = reduce_all(keep_gu, send_gu)
    input_grad, keep_q, send_q = finish(
        index, x, normed, weights, cosines, sines, dq, dkv, d_mid
    )
    q_sum = reduce_all(keep_q, send_q)

    ff = w_gate.shape[1]
    fd = w_down.shape[0]
    do_rows = do_sum.reshape(dim, dim)
    start = index[0] * fs
    grad_down = do_rows[:fd].astype(F32)
    grad_out = do_rows[fd : fd + fs].astype(F32)
    grad_mlp_gain = lax.dynamic_slice(do_rows[fd + fs], (start,), (fs,)).astype(F32)
    gu_cols = jnp.transpose(gu_sum, (1, 0, 2)).reshape(fs, 2 * ff).astype(F32)
    grad_gate, grad_up = gu_cols[:, :ff], gu_cols[:, ff:]
    q_cols = jnp.transpose(q_sum.reshape(2, 4, fs // 2, width // 4), (0, 2, 1, 3))
    q_cols = q_cols.reshape(fs, width).astype(F32)
    kv_grad = q_cols[:, : KV_HEADS * LANES].reshape(fs, KV_HEADS, 2, HEAD_DIM)
    grad_key = kv_grad[:, :, 0].reshape(fs, KV_HEADS * HEAD_DIM)
    grad_value = kv_grad[:, :, 1].reshape(fs, KV_HEADS * HEAD_DIM)
    grad_query = q_cols[:, KV_HEADS * LANES : used - 2]
    gain_rows = q_cols[:HEADS, width - HEAD_DIM :].reshape(dim)
    grad_attn_gain = lax.dynamic_slice(gain_rows, (start,), (fs,))
    return (
        result.reshape(seqs, rows, dim),
        input_grad.reshape(seqs, rows, dim),
        grad_attn_gain,
        grad_query,
        grad_key,
        grad_value,
        grad_out,
        grad_mlp_gain,
        grad_gate,
        grad_up,
        grad_down,
    )


def solution(mesh):
    rows3 = P("fsdp", "ctx", None)
    mat = P("fsdp", None)
    vec = P("fsdp")
    return jax.shard_map(
        local,
        mesh=mesh,
        in_specs=(rows3, rows3, vec, mat, mat, mat, mat, vec, mat, mat, mat, vec, vec),
        out_specs=(rows3, rows3, vec, mat, mat, mat, mat, vec, mat, mat, mat),
        check_vma=False,
    )
```

```python
import functools
import math

import jax
import jax.numpy as jnp
from jax import lax
from jax.experimental import pallas as pl
from jax.experimental.pallas import tpu as pltpu
from jax.sharding import PartitionSpec as P

HEADS = 9
KV_HEADS = 3
HEAD_DIM = 64
GROUP = HEADS // KV_HEADS
LANES = 128
EPSILON = 1e-05
THETA = 100000.0
SCALE = HEAD_DIM ** (-0.5)
MASKED = -2e30
LOWEST = -1e30
FAR = 1 << 29
CHUNKS = 8
SLOTS = (0, 2, 1, 3)
TOP = 40
BF16 = jnp.bfloat16
F32 = jnp.float32
NN = (((1,), (0,)), ((), ()))
NT = (((1,), (1,)), ((), ()))
TN = (((0,), (0,)), ((), ()))
VMEM_LIMIT = 63 * 1024 * 1024
PER_US = 1.0e9


def dot(a, b, dims=NN):
    return lax.dot_general(a, b, dims, preferred_element_type=F32)


def call(kernel, out_shape, in_specs=None, cost=1.0, **kwargs):
    return pl.pallas_call(
        kernel,
        out_shape=out_shape,
        in_specs=in_specs,
        compiler_params=pltpu.CompilerParams(vmem_limit_bytes=VMEM_LIMIT),
        cost_estimate=pl.CostEstimate(
            flops=int(cost * PER_US), bytes_accessed=0, transcendentals=0
        ),
        **kwargs,
    )


def sds(shape, dtype):
    return jax.ShapeDtypeStruct(shape, dtype)


def lane_of(shape):
    return lax.broadcasted_iota(jnp.int32, shape, 1)


def swap_halves(tile):
    lane = lane_of(tile.shape) % HEAD_DIM
    return jnp.where(
        lane < HEAD_DIM // 2, pltpu.roll(tile, LANES - 32, 1), pltpu.roll(tile, 32, 1)
    )


def half_roll(tile):
    return pltpu.roll(tile, HEAD_DIM, 1)


def assemble(target, index, shards, rows):
    for code, ref in zip((0, 1, 2, 3), shards):
        start = pl.multiple_of((index ^ code) * rows, 16)
        target[pl.ds(start, rows), :] = ref[...]


def inverse_rms(rows):
    return lax.rsqrt(jnp.mean(rows * rows, axis=-1, keepdims=True) + EPSILON)


def qkv_kernel(index_ref, x_ref, w0, w1, w2, w3, cos_ref, sin_ref, w_ref, normed_ref, q_ref, kv_ref, two_ref):
    assemble(w_ref, index_ref[0], (w0, w1, w2, w3), w0.shape[0])
    width = w_ref.shape[1]
    gains = jnp.transpose(w_ref[:, width - LANES :].astype(F32))
    x = x_ref[...].astype(F32)
    normed = (x * inverse_rms(x) * gains[HEAD_DIM : HEAD_DIM + 1, :]).astype(BF16)
    normed_ref[...] = normed
    two_ref[...] = gains[HEAD_DIM + 1 : HEAD_DIM + 2, :]
    cosines, sines = cos_ref[...], sin_ref[...]
    lane = lane_of(cosines.shape)
    low = lane < HEAD_DIM
    cos_kv = jnp.where(low, cosines, 1.0)
    sin_kv = jnp.where(low, sines, 0.0)
    rows = kv_ref.shape[1]
    seqs = x.shape[0] // rows
    for g in range(KV_HEADS):
        tile = dot(normed, w_ref[:, g * LANES : (g + 1) * LANES])
        turned = (tile * cos_kv + swap_halves(tile) * sin_kv).astype(BF16)
        for r in range(seqs):
            kv_ref[r * KV_HEADS + g] = turned[r * rows : (r + 1) * rows]
    first = KV_HEADS * LANES
    lin = dot(normed, w_ref[:, first:])
    for p in range((HEADS + 1) // 2):
        tile = lin[:, p * LANES : (p + 1) * LANES]
        turned = (tile * cosines + swap_halves(tile) * sines) * SCALE
        for h in (2 * p, 2 * p + 1):
            if h < HEADS:
                own = turned if h % 2 == 0 else half_roll(turned)
                own = jnp.where(low, own, 0.0).astype(BF16)
                g, i = divmod(h, GROUP)
                for r in range(seqs):
                    q_ref[r * KV_HEADS + g, i * rows : (i + 1) * rows] = own[
                        r * rows : (r + 1) * rows
                    ]


def pair_places(info_ref, step, rows, axis):
    shape = (1, 2 * rows) if axis == 1 else (2 * rows, 1)
    at = lax.broadcasted_iota(jnp.int32, shape, axis)
    first, second = info_ref[1 + 2 * step], info_ref[2 + 2 * step]
    return jnp.where(at < rows, first + at, second + at - rows)


def query_places(info_ref, rows, axis):
    total = GROUP * rows
    shape = (1, total) if axis == 1 else (total, 1)
    at = lax.broadcasted_iota(jnp.int32, shape, axis)
    return info_ref[0] * rows + at % rows


def seen_of(key_places, q_places, start, end, diagonal):
    key_in = (key_places >= start) & (key_places < end)
    query_in = (q_places >= start) & (q_places < end)
    seen = jnp.where(key_in, key_places, FAR) <= jnp.where(query_in, q_places, -1)
    if diagonal:
        seen = seen | (key_places == q_places)
    return seen


def row_active(info_ref, step, rows, start, end):
    own = info_ref[0] * rows
    first, second = info_ref[1 + 2 * step], info_ref[2 + 2 * step]
    keys_in = ((first < end) & (first + rows > start)) | ((second < end) & (second + rows > start))
    return (own < end) & (own + rows > start) & keys_in & (jnp.minimum(first, second) <= own)


def attend_kernel(steps, diagonal, fresh, info_ref, q_ref, a_ref, b_ref, *refs):
    if fresh:
        max_ref, sum_ref = refs
    else:
        max_in, sum_in, max_ref, sum_ref = refs
    step = pl.program_id(0)
    rows = a_ref.shape[2]
    seqs = q_ref.shape[0] // KV_HEADS
    spans = 1 + 2 * steps

    @pl.when(step == 0)
    def _():
        if fresh:
            max_ref[...] = jnp.full_like(max_ref, LOWEST)
            sum_ref[...] = jnp.zeros_like(sum_ref)
        else:
            max_ref[...] = max_in[...]
            sum_ref[...] = sum_in[...]

    def one_seq(r, unused):
        start = info_ref[spans + r]
        end = info_ref[spans + seqs + r]

        def one_row():
            seen = seen_of(
                pair_places(info_ref, step, rows, 1),
                query_places(info_ref, rows, 0),
                start,
                end,
                diagonal,
            )
            for g in range(KV_HEADS):
                rg = r * KV_HEADS + g
                kv = jnp.concatenate([a_ref[0, rg], b_ref[0, rg]], axis=0)
                scores = jnp.where(seen, dot(q_ref[rg], kv, NT), MASKED)
                old = max_ref[rg]
                new = jnp.maximum(old, jnp.max(scores, axis=-1, keepdims=True))
                weights = jnp.exp(scores - jnp.concatenate([new, new], axis=1)).astype(BF16)
                ones = jnp.where(lane_of(kv.shape) < HEAD_DIM, jnp.ones_like(kv), kv)
                sum_ref[rg] = sum_ref[rg] * jnp.exp(old - new) + dot(weights, ones)
                max_ref[rg] = new

        if diagonal:
            one_row()
        else:
            pl.when(row_active(info_ref, step, rows, start, end))(one_row)
        return unused

    lax.fori_loop(0, seqs, one_seq, 0)


def attend(info, queries, a, b, carry, diagonal):
    steps = a.shape[0]
    tiles, total, _ = queries.shape
    rows = a.shape[2]
    whole = pl.BlockSpec((tiles, total, LANES), lambda i: (0, 0, 0))
    piece = pl.BlockSpec((1, tiles, rows, LANES), lambda i: (i, 0, 0, 0))
    return call(
        functools.partial(attend_kernel, steps, diagonal, carry is None),
        (sds((tiles, total, LANES), F32),) * 2,
        [pl.BlockSpec(memory_space=pltpu.SMEM), whole, piece, piece]
        + ([] if carry is None else [whole] * 2),
        cost=4.0 + 2.0 * steps,
        out_specs=(whole, whole),
        grid=(steps,),
    )(info, queries, a, b, *(carry or ()))


def attend_back_kernel(
    steps, diagonal, fresh, extra, info_ref, q_ref, d_ref, stat_ref, a_ref, b_ref, *refs
):
    if extra:
        refs[-1][...] = total_of(refs[-6][...], refs[-5][...])
        dq_ref, da_ref, db_ref = refs[-4:-1]
    else:
        dq_ref, da_ref, db_ref = refs[-3:]
    dq_in = refs[0]
    step = pl.program_id(0)
    rows = a_ref.shape[2]
    seqs = q_ref.shape[0] // KV_HEADS
    spans = 1 + 2 * steps

    @pl.when(step == 0)
    def _():
        dq_ref[...] = jnp.zeros_like(dq_ref) if fresh else dq_in[...]

    def one_seq(r, unused):
        start = info_ref[spans + r]
        end = info_ref[spans + seqs + r]

        def one_row():
            seen = seen_of(
                pair_places(info_ref, step, rows, 0),
                query_places(info_ref, rows, 1),
                start,
                end,
                diagonal,
            )
            for g in range(KV_HEADS):
                rg = r * KV_HEADS + g
                kv = jnp.concatenate([a_ref[0, rg], b_ref[0, rg]], axis=0)
                q, d = q_ref[rg], d_ref[rg]
                log_sum = stat_ref[rg, 0:1, :]
                delta = stat_ref[rg, 1:2, :]
                scores = jnp.where(seen, dot(kv, q, NT), MASKED)
                probs = jnp.exp(scores - log_sum)
                d_scores = (probs * (dot(kv, d, NT) - delta)).astype(BF16)
                grad = (dot(d_scores, q) + dot(probs.astype(BF16), d)).astype(BF16)
                da_ref[0, rg] = grad[:rows]
                db_ref[0, rg] = grad[rows:]
                dq_ref[rg] = dq_ref[rg] + dot(d_scores, kv, TN)

        if diagonal:
            one_row()
        else:
            active = row_active(info_ref, step, rows, start, end)
            pl.when(active)(one_row)

            @pl.when(jnp.logical_not(active))
            def _():
                for g in range(KV_HEADS):
                    rg = r * KV_HEADS + g
                    da_ref[0, rg] = jnp.zeros((rows, LANES), BF16)
                    db_ref[0, rg] = jnp.zeros((rows, LANES), BF16)

        return unused

    lax.fori_loop(0, seqs, one_seq, 0)


def attend_back(info, queries, d_out, stats, a, b, carry, diagonal, after=(), slow=True, extra=()):
    steps = a.shape[0]
    tiles, total, _ = queries.shape
    rows = a.shape[2]
    whole = pl.BlockSpec((tiles, total, LANES), lambda i: (0, 0, 0))
    stat = pl.BlockSpec(stats.shape, lambda i: (0, 0, 0))
    one = pl.BlockSpec(a.shape[1:], lambda i: (0, 0, 0))
    piece = pl.BlockSpec((1, tiles, rows, LANES), lambda i: (i, 0, 0, 0))
    return call(
        functools.partial(attend_back_kernel, steps, diagonal, carry is None, bool(extra)),
        (sds((tiles, total, LANES), F32), sds(a.shape, BF16), sds(b.shape, BF16))
        + ((sds(a.shape[1:], BF16),) if extra else ()),
        [pl.BlockSpec(memory_space=pltpu.SMEM), whole, whole, stat, piece, piece]
        + ([] if carry is None else [whole])
        + [pl.BlockSpec(memory_space=pl.ANY)] * len(after)
        + [one] * len(extra),
        cost=3.0 + 3.0 * steps if slow else 1.0,
        out_specs=(whole, piece, piece) + ((one,) if extra else ()),
        grid=(steps,),
    )(info, queries, d_out, stats, a, b, *(() if carry is None else (carry,)), *after, *extra)


def middle_kernel(
    index_ref,
    x_ref,
    cot_ref,
    gain_ref,
    max_ref,
    sum_ref,
    gu0,
    gu1,
    gu2,
    gu3,
    do0,
    do1,
    do2,
    do3,
    turned_ref,
    d_mid_ref,
    d_ref,
    stat_ref,
    keep_ref,
    send_ref,
    out_ref,
    w_gu,
    w_down,
    w_out,
    att_ref,
    n2_ref,
    dn2_ref,
    g_gu,
    g_down,
    g_out,
    slot_ref,
    chunk_ref,
):
    index = index_ref[0]
    dim = x_ref.shape[1]
    ff = w_down.shape[0]
    fd, fs = ff // 4, dim // 4
    assemble(w_gu, index, (gu0, gu1, gu2, gu3), fs)
    for code, ref in zip((0, 1, 2, 3), (do0, do1, do2, do3)):
        shard = index ^ code
        w_down[pl.ds(pl.multiple_of(shard * fd, 16), fd), :] = ref[0:fd, :]
        w_out[pl.ds(pl.multiple_of(shard * fs, 16), fs), :] = ref[fd:, :]
    tiles, total, _ = max_ref.shape
    seqs = tiles // KV_HEADS
    rows = total // GROUP
    low = lane_of((total, LANES)) < HEAD_DIM
    low_rows = low[:rows]
    outs = []
    for rg in range(tiles):
        sums = sum_ref[rg]
        turned = half_roll(sums)
        both = jnp.where(low, sums, turned)
        log_sum = max_ref[rg] + jnp.log(both)
        stat_ref[rg, 0:1, :] = jnp.transpose(log_sum)[0:1, :]
        normal = jnp.where(low, 0.0, sums / both)
        sum_ref_row = normal
        outs.append(sum_ref_row)
    for r in range(seqs):
        for p in range((HEADS + 1) // 2):
            g, i = divmod(2 * p, GROUP)
            tile = half_roll(outs[r * KV_HEADS + g][i * rows : (i + 1) * rows])
            if 2 * p + 1 < HEADS:
                g, i = divmod(2 * p + 1, GROUP)
                tile = jnp.where(
                    low_rows, tile, outs[r * KV_HEADS + g][i * rows : (i + 1) * rows]
                )
                att_ref[r * rows : (r + 1) * rows, p * LANES : (p + 1) * LANES] = tile.astype(BF16)
            else:
                att_ref[r * rows : (r + 1) * rows, p * LANES :] = tile[:, :HEAD_DIM].astype(BF16)
    att = att_ref[...]
    cot = cot_ref[...]
    mid = x_ref[...].astype(F32) + dot(att, w_out[...])
    inv = inverse_rms(mid)
    gain = gain_ref[...]
    n2 = (mid * inv * gain).astype(BF16)
    n2_ref[...] = n2
    out_ref[...] = mid
    dn2_ref[...] = jnp.zeros_like(dn2_ref)
    width = ff // 2

    def ff_step(i, carry):
        at = pl.multiple_of(i * width, width)
        cols, cols_up = pl.ds(at, width), pl.ds(pl.multiple_of(at + ff, width), width)
        n2 = n2_ref[...]
        w_g, w_u, w_d = w_gu[:, cols], w_gu[:, cols_up], w_down[cols, :]
        gate = dot(n2, w_g)
        up = dot(n2, w_u)
        sig = 1.0 / (1.0 + jnp.exp(-gate))
        silu = gate * sig
        hidden = (silu * up).astype(BF16)
        out_ref[...] += dot(hidden, w_d)
        d_hidden = dot(cot_ref[...], w_d, NT)
        d_gate = (d_hidden * up * sig * (1.0 + gate * (1.0 - sig))).astype(BF16)
        d_up = (d_hidden * silu).astype(BF16)
        g_down[cols, :] = dot(hidden, cot_ref[...], TN)
        g_gu[:, cols] = dot(n2, d_gate, TN)
        g_gu[:, cols_up] = dot(n2, d_up, TN)
        dn2_ref[...] += dot(d_gate, w_g, NT) + dot(d_up, w_u, NT)
        return carry

    lax.fori_loop(0, 2, ff_step, 0)
    for r in range(seqs):
        turned_ref[r] = jnp.transpose(out_ref[r * rows : (r + 1) * rows, :])
    dn2 = dn2_ref[...]
    scaled = dn2 * gain
    gain_grad = jnp.sum(dn2 * mid * inv, axis=0, keepdims=True)
    d_mid = (
        cot.astype(F32)
        + inv * scaled
        - mid * (inv * inv * inv) * jnp.mean(scaled * mid, axis=-1, keepdims=True)
    )
    d_mid_ref[...] = d_mid
    d_low = d_mid.astype(BF16)
    g_out[...] = dot(att, d_low, TN)
    d_att = dot(d_low, w_out[...], NT)
    for r in range(seqs):
        for p in range((HEADS + 1) // 2):
            stop = min((p + 1) * LANES, dim)
            tile = d_att[r * rows : (r + 1) * rows, p * LANES : stop]
            if stop - p * LANES < LANES:
                tile = jnp.concatenate([tile, jnp.zeros_like(tile)], axis=1)
            for h in (2 * p, 2 * p + 1):
                if h < HEADS:
                    own = half_roll(tile) if h % 2 == 0 else tile
                    own = jnp.where(low_rows, 0.0, own).astype(BF16)
                    g, i = divmod(h, GROUP)
                    d_ref[r * KV_HEADS + g, i * rows : (i + 1) * rows] = own
    for rg in range(tiles):
        prod = d_ref[rg].astype(F32) * outs[rg]
        stat_ref[rg, 1:2, :] = jnp.sum(jnp.transpose(prod), axis=0, keepdims=True)
    cols = 2 * ff // CHUNKS
    part = dim // CHUNKS
    for slot in range(4):
        shard = index ^ SLOTS[slot]
        to = keep_ref if slot < 2 else send_ref
        at = pl.ds(pl.multiple_of(shard * fs, 16), fs)
        slot_ref[0:fd, :] = g_down[pl.ds(pl.multiple_of(shard * fd, 16), fd), :]
        slot_ref[fd : fd + fs, :] = g_out[at, :]
        slot_ref[fd + fs :, :] = jnp.broadcast_to(gain_grad, (dim - fd - fs, dim))
        for c in range(CHUNKS):
            chunk_ref[:fs, :] = g_gu[at, c * cols : (c + 1) * cols]
            chunk_ref[fs : fs + part, :] = slot_ref[c * part : (c + 1) * part, :cols]
            top = slot_ref[c * part : c * part + TOP, cols:]
            rest = slot_ref[c * part + TOP : (c + 1) * part, cols:]
            fill = jnp.zeros((2 * TOP - part, dim - cols), F32)
            chunk_ref[fs + part :, :] = jnp.concatenate(
                [top, jnp.concatenate([rest, fill], axis=0)], axis=1
            )
            to[slot % 2, c] = chunk_ref[...].astype(BF16)


def middle(index, x, cot, gain, top, sums, gu, do):
    n, dim = x.shape
    tiles, total, _ = top.shape
    ff2 = gu[0].shape[1]
    ff = ff2 // 2
    chunk = (dim // 4 + dim // CHUNKS + TOP, ff2 // CHUNKS)
    pair = sds((2, CHUNKS) + chunk, BF16)
    vm = pl.BlockSpec(memory_space=pltpu.VMEM)
    return call(
        middle_kernel,
        (
            sds((tiles // KV_HEADS, dim, total // GROUP), F32),
            sds((n, dim), F32),
            sds((tiles, total, LANES), BF16),
            sds((tiles, 8, total), F32),
            pair,
            pair,
        ),
        [pl.BlockSpec(memory_space=pltpu.SMEM)] + [vm] * 13,
        cost=20.0,
        out_specs=(vm,) * 6,
        scratch_shapes=[
            pltpu.VMEM((n, dim), F32),
            pltpu.VMEM((dim, ff2), BF16),
            pltpu.VMEM((ff, dim), BF16),
            pltpu.VMEM((dim, dim), BF16),
            pltpu.VMEM((n, dim), BF16),
            pltpu.VMEM((n, dim), BF16),
            pltpu.VMEM((n, dim), F32),
            pltpu.VMEM((dim, ff2), F32),
            pltpu.VMEM((ff, dim), F32),
            pltpu.VMEM((dim, dim), F32),
            pltpu.VMEM((dim, dim), F32),
            pltpu.VMEM(chunk, F32),
        ],
    )(index, x, cot, gain, top, sums, *gu, *do)


def end_kernel(
    index_ref,
    x_ref,
    normed_ref,
    w_ref,
    cos_ref,
    sin_ref,
    dq_ref,
    d_mid_ref,
    *refs,
    parts,
):
    dkv_refs = refs[:parts]
    grad_ref, keep, send, lin_ref, g_ref = refs[-5:]
    index = index_ref[0]
    width = w_ref.shape[1]
    tiles, rows, _ = dkv_refs[0].shape
    seqs = tiles // KV_HEADS
    low = lane_of((rows, LANES)) < HEAD_DIM
    for r in range(seqs):
        at = slice(r * rows, (r + 1) * rows)
        cosines, sines = cos_ref[at, :], sin_ref[at, :]
        cos_kv = jnp.where(low, cosines, 1.0)
        sin_kv = jnp.where(low, sines, 0.0)
        for g in range(KV_HEADS):
            tile = dkv_refs[0][r * KV_HEADS + g].astype(F32)
            for ref in dkv_refs[1:]:
                tile = tile + ref[r * KV_HEADS + g].astype(F32)
            back = tile * cos_kv - swap_halves(tile) * sin_kv
            lin_ref[at, g * LANES : (g + 1) * LANES] = back.astype(BF16)
        first = KV_HEADS * LANES
        for p in range((HEADS + 1) // 2):
            backs = []
            for h in (2 * p, 2 * p + 1):
                if h < HEADS:
                    g, i = divmod(h, GROUP)
                    tile = dq_ref[r * KV_HEADS + g, i * rows : (i + 1) * rows]
                    backs.append((tile * cosines - swap_halves(tile) * sines) * SCALE)
                else:
                    backs.append(jnp.zeros((rows, LANES), F32))
            tile = jnp.where(low, backs[0], half_roll(backs[1]))
            lin_ref[at, first + p * LANES : first + (p + 1) * LANES] = tile.astype(BF16)
    lin = lin_ref[...]
    g_ref[...] = dot(normed_ref[...], lin, TN)
    d_normed = dot(lin, w_ref[...], NT)
    gains = jnp.transpose(w_ref[:, width - LANES :].astype(F32))
    gain = gains[HEAD_DIM : HEAD_DIM + 1, :]
    x = x_ref[...].astype(F32)
    inv = inverse_rms(x)
    scaled = d_normed * gain
    grad = (
        d_mid_ref[...]
        + inv * scaled
        - x * (inv * inv * inv) * jnp.mean(scaled * x, axis=-1, keepdims=True)
    )
    for r in range(seqs):
        grad_ref[r] = jnp.transpose(grad[r * rows : (r + 1) * rows, :])
    gain_grad = jnp.sum(d_normed * x * inv, axis=0, keepdims=True)
    dim = x.shape[1]
    fs = dim // 4
    for slot in range(4):
        start = (index ^ SLOTS[slot]) * fs
        to = keep if slot < 2 else send
        for c in range(CHUNKS):
            half, quarter = divmod(c, 4)
            size, cols = fs // 2, width // 4
            at = pl.ds(pl.multiple_of(start + half * size, 8), size)
            tile = g_ref[at, quarter * cols : (quarter + 1) * cols]
            if c == 3:
                pad = jnp.concatenate(
                    [gain_grad[:, k * HEAD_DIM : (k + 1) * HEAD_DIM] for k in range(HEADS)]
                    + [jnp.zeros((size - HEADS, HEAD_DIM), F32)],
                    axis=0,
                )
                pad = jnp.concatenate([tile[:, : cols - HEAD_DIM], pad], axis=1)
                tile = pad
            to[slot % 2, c] = tile.astype(BF16)


def finish(index, x, normed, w, cosines, sines, dq, dkv, d_mid, after):
    n, dim = x.shape
    width = w.shape[1]
    vm = pl.BlockSpec(memory_space=pltpu.VMEM)
    pair = sds((2, CHUNKS, dim // 8, width // 4), BF16)
    tiles = dkv[0].shape[0]
    return call(
        functools.partial(end_kernel, parts=len(dkv)),
        (sds((tiles // KV_HEADS, dim, dkv[0].shape[1]), F32), pair, pair),
        [pl.BlockSpec(memory_space=pltpu.SMEM)] + [vm] * (7 + len(dkv))
        + [pl.BlockSpec(memory_space=pl.ANY)] * len(after),
        cost=7.0,
        out_specs=(vm,) * 3,
        scratch_shapes=[pltpu.VMEM((n, width), BF16), pltpu.VMEM((dim, width), F32)],
    )(index, x, normed, w, cosines, sines, dq, d_mid, *dkv, *after)


def both_halves(place_ref, parts, d):
    near, far = parts[2 * d][...].astype(F32), parts[2 * d + 1][...].astype(F32)
    flag = place_ref[0] == 0
    return place_ref[1] ^ d, jnp.where(flag, near, far), jnp.where(flag, far, near)


def own_gain(place_ref, row, out_ref):
    size = out_ref.shape[1]
    rows = jnp.broadcast_to(row, (8, row.shape[1]))
    fill = -row.shape[1] % LANES
    rows = jnp.concatenate([rows, jnp.zeros((8, fill), F32)], axis=1)
    turned = pltpu.roll(rows, rows.shape[1] - place_ref[2] * size, 1)
    out_ref[...] = turned[0:1, :size]


def own_kernel(place_ref, *refs):
    parts = refs[:CHUNKS]
    gate_ref, up_ref, down_ref, out_ref, gain_ref, all_ref = refs[CHUNKS:]
    own_body(place_ref, parts, gate_ref, up_ref, down_ref, out_ref, gain_ref, all_ref)


def own_body(place_ref, parts, gate_ref, up_ref, down_ref, out_ref, gain_ref, all_ref):
    cols = parts[0].shape[1]
    fs, dim = out_ref.shape
    fd = down_ref.shape[1]
    part = dim // CHUNKS
    width = dim - cols
    for d in range(4):
        quarter, first, second = both_halves(place_ref, parts, d)
        at = pl.ds(pl.multiple_of(quarter * cols, LANES), cols)
        gate_ref[:, at] = first[:fs]
        up_ref[:, at] = second[:fs]
        for c, chunk in ((quarter, first), (4 + quarter, second)):
            start = c * part
            all_ref[pl.ds(pl.multiple_of(start, 8), part), :cols] = chunk[fs : fs + part]
            right = chunk[fs + part :]
            all_ref[pl.ds(pl.multiple_of(start, 8), TOP), cols:] = right[:, :width]
            all_ref[pl.ds(pl.multiple_of(start + TOP, 8), part - TOP), cols:] = right[
                : part - TOP, width:
            ]
    down_ref[...] = jnp.transpose(all_ref[:fd, :])
    out_ref[...] = all_ref[fd : fd + fs, :]
    own_gain(place_ref, all_ref[fd + fs : fd + fs + 1, :], gain_ref)


def own_q_kernel(place_ref, *refs):
    parts = refs[:CHUNKS]
    query_ref, key_ref, value_ref, gain_ref, all_ref = refs[CHUNKS:]
    part, cols = parts[0].shape
    for d in range(4):
        quarter, first, second = both_halves(place_ref, parts, d)
        at = pl.ds(pl.multiple_of(quarter * cols, LANES), cols)
        all_ref[:part, at] = first
        all_ref[part:, at] = second
    first = KV_HEADS * LANES
    for g in range(KV_HEADS):
        to = slice(g * HEAD_DIM, (g + 1) * HEAD_DIM)
        key_ref[:, to] = all_ref[:, g * LANES : g * LANES + HEAD_DIM]
        value_ref[:, to] = all_ref[:, g * LANES + HEAD_DIM : (g + 1) * LANES]
    query_ref[...] = all_ref[:, first : first + HEADS * HEAD_DIM]
    start = all_ref.shape[1] - HEAD_DIM
    row = jnp.concatenate([all_ref[k : k + 1, start:] for k in range(HEADS)], axis=1)
    own_gain(place_ref, row, gain_ref)


def own(kernel, place, outs, parts, scratch):
    vm = pl.BlockSpec(memory_space=pltpu.VMEM)
    return call(
        kernel,
        tuple(sds(shape, F32) for shape in outs),
        [pl.BlockSpec(memory_space=pltpu.SMEM)] + [vm] * CHUNKS,
        cost=3.0,
        out_specs=(vm,) * len(outs),
        scratch_shapes=[pltpu.VMEM(scratch, F32)],
    )(place, *parts)


def pack_kernel(q_ref, k_ref, v_ref, one_ref, two_ref, out_ref):
    for g in range(KV_HEADS):
        at = slice(g * HEAD_DIM, (g + 1) * HEAD_DIM)
        out_ref[:, g * LANES : g * LANES + HEAD_DIM] = k_ref[:, at]
        out_ref[:, g * LANES + HEAD_DIM : (g + 1) * LANES] = v_ref[:, at]
    first = KV_HEADS * LANES
    full = HEADS * HEAD_DIM
    out_ref[:, first : first + full] = q_ref[...]
    fs = q_ref.shape[0]
    row = lax.broadcasted_iota(jnp.int32, (LANES, fs), 0)
    gains = jnp.where(row == HEAD_DIM, one_ref[...].astype(F32)[None, :], 0.0)
    gains = jnp.where(row == HEAD_DIM + 1, two_ref[...].astype(F32)[None, :], gains)
    out_ref[:, first + full :] = jnp.transpose(gains)[:, HEAD_DIM:].astype(BF16)


def gu_pack_kernel(gate_ref, up_ref, unused, out_ref):
    ff = gate_ref.shape[1]
    out_ref[:, :ff] = gate_ref[...]
    out_ref[:, ff:] = up_ref[...]


def flip(x, axis, mask):
    n = lax.axis_size(axis)
    return lax.ppermute(x, axis, [(i, i ^ mask) for i in range(n)])


def gather_shards(own):
    across = flip(own, "fsdp", 2)
    return own, flip(own, "fsdp", 1), across, flip(across, "fsdp", 1)


def add(a, b):
    return (a.astype(F32) + b.astype(F32)).astype(BF16)


def total_of(*parts):
    total = parts[0].astype(F32)
    for part in parts[1:]:
        total = total + part.astype(F32)
    return total.astype(BF16)


def add_kernel(place_ref, *refs):
    refs[-1][...] = total_of(*(ref[...] for ref in refs[:-1]))


def core_kernel(place_ref, keep, got, out):
    out[...] = total_of(keep[0], got[0])


def y_kernel(place_ref, keep, got, far, mine, away):
    x_bit = place_ref[0]
    for c in range(4):
        here, there = 4 * x_bit + c, 4 * (1 - x_bit) + c
        mine[c] = total_of(keep[0, here], got[0, here], far[here])
        away[c] = total_of(keep[0, there], got[0, there], far[there])


def y_direct_kernel(place_ref, keep, got, far, *outs):
    for d in range(CHUNKS):
        c = 4 * (place_ref[0] ^ (d & 1)) + (place_ref[1] ^ (d >> 1))
        outs[d][...] = total_of(keep[0, c], got[0, c], far[c])


def x_kernel(place_ref, keep, got, *outs):
    for d in range(4):
        c = place_ref[1] ^ d
        outs[d][...] = total_of(keep[c], got[c])


def fuse(kernel, place, outs, ins, after=(), specs=None, out_specs=None, grid=None):
    vm = pl.BlockSpec(memory_space=pltpu.VMEM)
    count = 1 + len(ins)

    def body(*refs):
        kernel(*refs[:count], *refs[count + len(after) :])

    return call(
        body,
        tuple(sds(shape, BF16) for shape in outs),
        [pl.BlockSpec(memory_space=pltpu.SMEM)]
        + (specs or [vm] * len(ins))
        + [pl.BlockSpec(memory_space=pl.ANY)] * len(after),
        cost=1.5,
        out_specs=out_specs or (vm,) * len(outs),
        **({"grid": grid} if grid else {}),
    )(place, *ins, *after)


class Sum:
    def __init__(self, place, keep, send):
        self.place, self.shape = place, keep.shape[2:]
        self.parts = (keep, flip(send, "fsdp", 1))

    def core(self, *after):
        keep, got = self.parts
        two = (2,) + self.shape
        source = pl.BlockSpec((1,) + two, lambda i: (1, i, 0, 0))
        target = pl.BlockSpec(two, lambda i: (i, 0, 0))
        (away,) = fuse(
            core_kernel,
            self.place,
            [(CHUNKS,) + self.shape],
            self.parts,
            after,
            [source, source],
            (target,),
            (CHUNKS // 2,),
        )
        self.parts = (keep, got, flip(away, "fsdp", 2))
        return away

    def y_specs(self):
        first = pl.BlockSpec((1, CHUNKS) + self.shape, lambda i: (0, 0, 0, 0))
        return [first, first, pl.BlockSpec(memory_space=pltpu.VMEM)]

    def y(self, *after):
        shape = (4,) + self.shape
        keep, send = fuse(
            y_kernel, self.place, [shape] * 2, self.parts, after, self.y_specs(), None, (1,)
        )
        self.parts = (keep, flip(send, "ctx", 1))
        return keep

    def y_direct(self, *after):
        mine, *away = fuse(
            y_direct_kernel,
            self.place,
            [self.shape] * CHUNKS,
            self.parts,
            after,
            self.y_specs(),
            None,
            (1,),
        )
        self.parts = (mine, *(flip(away[d - 1], "ctx", d) for d in range(1, CHUNKS)))
        return mine

    def x(self, *after):
        mine, *away = fuse(x_kernel, self.place, [self.shape] * 4, self.parts, after)
        self.parts = (mine, *(flip(away[d - 1], "ctx", 2 * d) for d in (1, 2, 3)))
        return mine

    def z(self, *after):
        n = lax.axis_size("ctx")
        (mine,) = fuse(add_kernel, self.place, [self.shape], self.parts, after)
        for b in range(3, n.bit_length() - 1):
            (mine,) = fuse(
                add_kernel, self.place, [self.shape], (mine, flip(mine, "ctx", 1 << b))
            )
        self.parts = (mine, *(flip(mine, "ctx", d) for d in range(1, CHUNKS)))
        return mine


def send_down(x, levels):
    n = lax.axis_size("ctx")
    return lax.ppermute(x, "ctx", [(i, i - 2 * levels) for i in range(2 * levels, n)])


def local(
    tokens,
    cotangent,
    attn_gain,
    w_query,
    w_key,
    w_value,
    w_out,
    mlp_gain,
    w_gate,
    w_up,
    w_down,
    seq_lengths,
    seq_starts,
):
    seqs, rows, dim = tokens.shape
    n = seqs * rows
    n_ctx = lax.axis_size("ctx")
    me = lax.axis_index("ctx")
    index = lax.axis_index("fsdp").reshape(1).astype(jnp.int32)
    fs = w_query.shape[0]
    x = tokens.reshape(n, dim)
    cot = cotangent.reshape(n, dim)

    used = KV_HEADS * LANES + HEADS * HEAD_DIM + 2
    width = used - used % -LANES
    vm = pl.BlockSpec(memory_space=pltpu.VMEM)
    first = call(pack_kernel, sds((fs, width), BF16), [vm] * 5, cost=1.5, out_specs=vm)(
        w_query, w_key, w_value, attn_gain, mlp_gain
    )
    first_shards = gather_shards(first)
    gu_shards = gather_shards(
        call(
            gu_pack_kernel,
            sds((fs, 2 * w_gate.shape[1]), BF16),
            [vm, vm, pl.BlockSpec(memory_space=pl.ANY)],
            cost=1.5,
            out_specs=vm,
        )(w_gate, w_up, first_shards[2])
    )
    do_shards = gather_shards(jnp.concatenate([w_down, w_out], axis=0))

    places = me * rows + jnp.arange(rows, dtype=jnp.int32)
    positions = (places[None, :] - seq_starts[:, None]).astype(F32)
    frequency = THETA ** (-(2.0 * jnp.arange(HEAD_DIM // 2, dtype=F32)) / HEAD_DIM)
    angles = (positions[:, :, None] * frequency).reshape(n, HEAD_DIM // 2)
    cos, sin = jnp.cos(angles), jnp.sin(angles)
    cosines = jnp.concatenate([cos] * 4, axis=1)
    sines = jnp.concatenate([-sin, sin] * 2, axis=1)

    tiles = seqs * KV_HEADS
    weights, normed, queries, kv, gain_two = call(
        qkv_kernel,
        (
            sds((dim, width), BF16),
            sds((n, dim), BF16),
            sds((tiles, GROUP * rows, LANES), BF16),
            sds((tiles, rows, LANES), BF16),
            sds((1, dim), F32),
        ),
        [pl.BlockSpec(memory_space=pltpu.SMEM)] + [vm] * 7,
        cost=4.0,
        out_specs=(vm,) * 5,
    )(index, x, *first_shards, cosines, sines)

    spans = [seq_starts.astype(jnp.int32), (seq_starts + seq_lengths).astype(jnp.int32)]

    def info_of(bases):
        return jnp.concatenate([me.reshape(1).astype(jnp.int32), bases.astype(jnp.int32)] + spans)

    x_bit = me % 2
    if n_ctx <= 8 and n_ctx % 2 == 0:
        levels = n_ctx // 2
        up = [(i, i + 2) for i in range(n_ctx - 2)]
        down = [(i + 2, i) for i in range(n_ctx - 2)]
        pieces = []
        piece = kv
        for k in range(levels):
            other = flip(piece, "ctx", 1)
            pair = (me // 2 - k) * 2
            bases = jnp.stack([pair + x_bit, pair + 1 - x_bit]) * rows
            bases = jnp.where(pair >= 0, bases, FAR)
            pieces.append((bases, piece[None], other[None]))
            if k + 1 < levels:
                piece = lax.ppermute(piece, "ctx", up)
        carry = None
        for k in range(levels):
            bases, a, b = pieces[k]
            carry = attend(info_of(bases), queries, a, b, carry, k == 0)
    else:
        every = lax.all_gather(kv, "ctx", axis=0)
        info = info_of(jnp.arange(n_ctx, dtype=jnp.int32) * rows)
        carry = attend(info, queries, every[0::2], every[1::2], None, True)

    result, d_mid, d_out, stats, keep_mlp, send_mlp = middle(
        index, x, cot, gain_two, carry[0], carry[1], gu_shards, do_shards
    )

    place = jnp.stack([me & 1, (me >> 1) & 3, index[0]]).astype(jnp.int32)
    mlp = Sum(place, keep_mlp, send_mlp)
    if n_ctx <= 8 and n_ctx % 2 == 0:
        dq, last = None, ()
        dkv, partials = [], []
        for k in reversed(range(levels)):
            bases, a, b = pieces[k]
            extra = partials[0][1:] if k < levels - 2 else ()
            dq, da, db, *both = attend_back(
                info_of(bases),
                queries,
                d_out,
                stats,
                a,
                b,
                dq,
                k == 0,
                last,
                k == levels - 1,
                extra,
            )
            if extra:
                dkv.append(send_down(both[0], partials.pop(0)[0]))
            partials.append((k, da[0], flip(db[0], "ctx", 1)))
            last = (mlp.core(dq),) if k == levels - 1 else ()
        while len(partials) > 1:
            far, near, other = partials.pop(0)
            (both,) = fuse(add_kernel, place, [near.shape], (near, other), (dq,))
            dkv.append(send_down(both, far))
            last = (both,)
        dkv = [partials[0][1], partials[0][2]] + dkv
        last = (mlp.y(*last),)
    else:
        dq, da, db = attend_back(
            info, queries, d_out, stats, every[0::2], every[1::2], None, True
        )
        partial = jnp.stack([da, db], axis=1).reshape((n_ctx,) + da.shape[1:])
        dkv = [lax.psum_scatter(partial, "ctx", scatter_dimension=0, tiled=False)]
        mlp.core(dq)
        last = (mlp.y(dq),)

    ff = w_gate.shape[1]
    fd = w_down.shape[0]
    input_grad, keep_q, send_q = finish(
        index, x, normed, weights, cosines, sines, dq, dkv, d_mid, last
    )
    qkv = Sum(place, keep_q, send_q)
    step = mlp.x(keep_q)
    step = qkv.core(step)
    step = mlp.z(step)
    step = qkv.y_direct(step)
    step = qkv.z(step)
    grad_gate, grad_up, grad_down, grad_out, gain_two_grad = own(
        own_kernel,
        place,
        [(fs, ff), (fs, ff), (dim, fd), (fs, dim), (1, fs)],
        mlp.parts,
        (dim, dim),
    )
    grad_down = grad_down.T
    kv_width = KV_HEADS * HEAD_DIM
    grad_query, grad_key, grad_value, gain_one_grad = own(
        own_q_kernel,
        place,
        [(fs, HEADS * HEAD_DIM), (fs, kv_width), (fs, kv_width), (1, fs)],
        qkv.parts,
        (fs, width),
    )
    grad_mlp_gain = gain_two_grad.reshape(fs)
    grad_attn_gain = gain_one_grad.reshape(fs)
    return (
        jnp.transpose(result, (0, 2, 1)),
        jnp.transpose(input_grad, (0, 2, 1)),
        grad_attn_gain,
        grad_query,
        grad_key,
        grad_value,
        grad_out,
        grad_mlp_gain,
        grad_gate,
        grad_up,
        grad_down,
    )


def solution(mesh):
    rows3 = P("fsdp", "ctx", None)
    mat = P("fsdp", None)
    vec = P("fsdp")
    return jax.shard_map(
        local,
        mesh=mesh,
        in_specs=(rows3, rows3, vec, mat, mat, mat, mat, vec, mat, mat, mat, vec, vec),
        out_specs=(rows3, rows3, vec, mat, mat, mat, mat, vec, mat, mat, mat),
        check_vma=False,
    )
```

```python
import functools
import math

import jax
import jax.numpy as jnp
from jax import lax
from jax.experimental import pallas as pl
from jax.experimental.pallas import tpu as pltpu
from jax.sharding import PartitionSpec as P

HEADS = 9
KV_HEADS = 3
HEAD_DIM = 64
GROUP = HEADS // KV_HEADS
LANES = 128
EPSILON = 1e-05
THETA = 100000.0
SCALE = HEAD_DIM ** (-0.5)
MASKED = -2e30
LOWEST = -1e30
FAR = 1 << 29
CHUNKS = 8
SLOTS = (0, 2, 1, 3)
TOP = 40
BF16 = jnp.bfloat16
F32 = jnp.float32
NN = (((1,), (0,)), ((), ()))
NT = (((1,), (1,)), ((), ()))
TN = (((0,), (0,)), ((), ()))
VMEM_LIMIT = 63 * 1024 * 1024
PER_US = 1.0e9


def dot(a, b, dims=NN):
    return lax.dot_general(a, b, dims, preferred_element_type=F32)


def call(kernel, out_shape, in_specs=None, cost=1.0, **kwargs):
    return pl.pallas_call(
        kernel,
        out_shape=out_shape,
        in_specs=in_specs,
        compiler_params=pltpu.CompilerParams(vmem_limit_bytes=VMEM_LIMIT),
        cost_estimate=pl.CostEstimate(
            flops=int(cost * PER_US), bytes_accessed=0, transcendentals=0
        ),
        **kwargs,
    )


def sds(shape, dtype):
    return jax.ShapeDtypeStruct(shape, dtype)


def lane_of(shape):
    return lax.broadcasted_iota(jnp.int32, shape, 1)


def swap_halves(tile):
    lane = lane_of(tile.shape) % HEAD_DIM
    return jnp.where(
        lane < HEAD_DIM // 2, pltpu.roll(tile, LANES - 32, 1), pltpu.roll(tile, 32, 1)
    )


def half_roll(tile):
    return pltpu.roll(tile, HEAD_DIM, 1)


def assemble(target, index, shards, rows):
    for code, ref in zip((0, 1, 2, 3), shards):
        start = pl.multiple_of((index ^ code) * rows, 16)
        target[pl.ds(start, rows), :] = ref[...]


def inverse_rms(rows):
    return lax.rsqrt(jnp.mean(rows * rows, axis=-1, keepdims=True) + EPSILON)


def qkv_kernel(index_ref, x_ref, w0, w1, w2, w3, cos_ref, sin_ref, w_ref, normed_ref, q_ref, kv_ref, two_ref, rows_ref):
    assemble(w_ref, index_ref[0], (w0, w1, w2, w3), w0.shape[0])
    width = w_ref.shape[1]
    gains = jnp.transpose(w_ref[:, width - LANES :].astype(F32))
    count = x_ref.shape[2]
    for r in range(x_ref.shape[0]):
        turned = jnp.transpose(x_ref[r].astype(F32))
        rows_ref[r * count : (r + 1) * count, :] = turned.astype(BF16)
    x = rows_ref[...].astype(F32)
    normed = (x * inverse_rms(x) * gains[HEAD_DIM : HEAD_DIM + 1, :]).astype(BF16)
    normed_ref[...] = normed
    two_ref[...] = gains[HEAD_DIM + 1 : HEAD_DIM + 2, :]
    cosines, sines = cos_ref[...], sin_ref[...]
    lane = lane_of(cosines.shape)
    low = lane < HEAD_DIM
    cos_kv = jnp.where(low, cosines, 1.0)
    sin_kv = jnp.where(low, sines, 0.0)
    rows = kv_ref.shape[1]
    seqs = x.shape[0] // rows
    for g in range(KV_HEADS):
        tile = dot(normed, w_ref[:, g * LANES : (g + 1) * LANES])
        turned = (tile * cos_kv + swap_halves(tile) * sin_kv).astype(BF16)
        for r in range(seqs):
            kv_ref[r * KV_HEADS + g] = turned[r * rows : (r + 1) * rows]
    first = KV_HEADS * LANES
    lin = dot(normed, w_ref[:, first:])
    for p in range((HEADS + 1) // 2):
        tile = lin[:, p * LANES : (p + 1) * LANES]
        turned = (tile * cosines + swap_halves(tile) * sines) * SCALE
        for h in (2 * p, 2 * p + 1):
            if h < HEADS:
                own = turned if h % 2 == 0 else half_roll(turned)
                own = jnp.where(low, own, 0.0).astype(BF16)
                g, i = divmod(h, GROUP)
                for r in range(seqs):
                    q_ref[r * KV_HEADS + g, i * rows : (i + 1) * rows] = own[
                        r * rows : (r + 1) * rows
                    ]


def pair_places(info_ref, step, rows, axis):
    shape = (1, 2 * rows) if axis == 1 else (2 * rows, 1)
    at = lax.broadcasted_iota(jnp.int32, shape, axis)
    first, second = info_ref[1 + 2 * step], info_ref[2 + 2 * step]
    return jnp.where(at < rows, first + at, second + at - rows)


def query_places(info_ref, rows, axis):
    total = GROUP * rows
    shape = (1, total) if axis == 1 else (total, 1)
    at = lax.broadcasted_iota(jnp.int32, shape, axis)
    return info_ref[0] * rows + at % rows


def seen_of(key_places, q_places, start, end, diagonal):
    key_in = (key_places >= start) & (key_places < end)
    query_in = (q_places >= start) & (q_places < end)
    seen = jnp.where(key_in, key_places, FAR) <= jnp.where(query_in, q_places, -1)
    if diagonal:
        seen = seen | (key_places == q_places)
    return seen


def row_active(info_ref, step, rows, start, end):
    own = info_ref[0] * rows
    first, second = info_ref[1 + 2 * step], info_ref[2 + 2 * step]
    keys_in = ((first < end) & (first + rows > start)) | ((second < end) & (second + rows > start))
    return (own < end) & (own + rows > start) & keys_in & (jnp.minimum(first, second) <= own)


def attend_rows(
    info_ref, step, steps, diagonal, q_ref, a_ref, b_ref, max_in, sum_in, max_ref, sum_ref
):
    rows = a_ref.shape[2]
    seqs = q_ref.shape[0] // KV_HEADS
    spans = 1 + 2 * steps

    def one_seq(r, unused):
        start = info_ref[spans + r]
        end = info_ref[spans + seqs + r]

        def one_row():
            seen = seen_of(
                pair_places(info_ref, step, rows, 1),
                query_places(info_ref, rows, 0),
                start,
                end,
                diagonal,
            )
            for g in range(KV_HEADS):
                rg = r * KV_HEADS + g
                kv = jnp.concatenate([a_ref[0, rg], b_ref[0, rg]], axis=0)
                scores = jnp.where(seen, dot(q_ref[rg], kv, NT), MASKED)
                old = max_in[rg]
                new = jnp.maximum(old, jnp.max(scores, axis=-1, keepdims=True))
                weights = jnp.exp(scores - jnp.concatenate([new, new], axis=1)).astype(BF16)
                ones = jnp.where(lane_of(kv.shape) < HEAD_DIM, jnp.ones_like(kv), kv)
                sum_ref[rg] = sum_in[rg] * jnp.exp(old - new) + dot(weights, ones)
                max_ref[rg] = new

        def keep_row():
            for g in range(KV_HEADS):
                max_ref[r * KV_HEADS + g] = max_in[r * KV_HEADS + g]
                sum_ref[r * KV_HEADS + g] = sum_in[r * KV_HEADS + g]

        if diagonal:
            one_row()
        else:
            active = row_active(info_ref, step, rows, start, end)
            pl.when(active)(one_row)
            if max_in is not max_ref:
                pl.when(jnp.logical_not(active))(keep_row)
        return unused

    lax.fori_loop(0, seqs, one_seq, 0)


def attend_kernel(steps, diagonal, fresh, info_ref, q_ref, a_ref, b_ref, *refs):
    if fresh:
        max_ref, sum_ref = refs
    else:
        max_in, sum_in, max_ref, sum_ref = refs
    step = pl.program_id(0)

    @pl.when(step == 0)
    def _():
        if fresh:
            max_ref[...] = jnp.full_like(max_ref, LOWEST)
            sum_ref[...] = jnp.zeros_like(sum_ref)
        else:
            max_ref[...] = max_in[...]
            sum_ref[...] = sum_in[...]

    attend_rows(
        info_ref, step, steps, diagonal, q_ref, a_ref, b_ref, max_ref, sum_ref, max_ref, sum_ref
    )


def attend(info, queries, a, b, carry, diagonal):
    steps = a.shape[0]
    tiles, total, _ = queries.shape
    rows = a.shape[2]
    whole = pl.BlockSpec((tiles, total, LANES), lambda i: (0, 0, 0))
    piece = pl.BlockSpec((1, tiles, rows, LANES), lambda i: (i, 0, 0, 0))
    return call(
        functools.partial(attend_kernel, steps, diagonal, carry is None),
        (sds((tiles, total, LANES), F32),) * 2,
        [pl.BlockSpec(memory_space=pltpu.SMEM), whole, piece, piece]
        + ([] if carry is None else [whole] * 2),
        cost=10.0 * steps,
        out_specs=(whole, whole),
        grid=(steps,),
    )(info, queries, a, b, *(carry or ()))


def attend_back_kernel(
    steps, diagonal, fresh, extra, info_ref, q_ref, d_ref, stat_ref, a_ref, b_ref, *refs
):
    if extra:
        refs[-1][...] = total_of(refs[-6][...], refs[-5][...])
        dq_ref, da_ref, db_ref = refs[-4:-1]
    else:
        dq_ref, da_ref, db_ref = refs[-3:]
    dq_in = refs[0]
    step = pl.program_id(0)
    rows = a_ref.shape[2]
    seqs = q_ref.shape[0] // KV_HEADS
    spans = 1 + 2 * steps

    @pl.when(step == 0)
    def _():
        dq_ref[...] = jnp.zeros_like(dq_ref) if fresh else dq_in[...]

    def one_seq(r, unused):
        start = info_ref[spans + r]
        end = info_ref[spans + seqs + r]

        def one_row():
            seen = seen_of(
                pair_places(info_ref, step, rows, 0),
                query_places(info_ref, rows, 1),
                start,
                end,
                diagonal,
            )
            for g in range(KV_HEADS):
                rg = r * KV_HEADS + g
                kv = jnp.concatenate([a_ref[0, rg], b_ref[0, rg]], axis=0)
                q, d = q_ref[rg], d_ref[rg]
                log_sum = stat_ref[rg, 0:1, :]
                delta = stat_ref[rg, 1:2, :]
                scores = jnp.where(seen, dot(kv, q, NT), MASKED)
                probs = jnp.exp(scores - log_sum)
                d_scores = (probs * (dot(kv, d, NT) - delta)).astype(BF16)
                grad = (dot(d_scores, q) + dot(probs.astype(BF16), d)).astype(BF16)
                da_ref[0, rg] = grad[:rows]
                db_ref[0, rg] = grad[rows:]
                dq_ref[rg] = dq_ref[rg] + dot(d_scores, kv, TN)

        if diagonal:
            one_row()
        else:
            active = row_active(info_ref, step, rows, start, end)
            pl.when(active)(one_row)

            @pl.when(jnp.logical_not(active))
            def _():
                for g in range(KV_HEADS):
                    rg = r * KV_HEADS + g
                    da_ref[0, rg] = jnp.zeros((rows, LANES), BF16)
                    db_ref[0, rg] = jnp.zeros((rows, LANES), BF16)

        return unused

    lax.fori_loop(0, seqs, one_seq, 0)


def attend_back(info, queries, d_out, stats, a, b, carry, diagonal, after=(), extra=()):
    steps = a.shape[0]
    tiles, total, _ = queries.shape
    rows = a.shape[2]
    whole = pl.BlockSpec((tiles, total, LANES), lambda i: (0, 0, 0))
    stat = pl.BlockSpec(stats.shape, lambda i: (0, 0, 0))
    one = pl.BlockSpec(a.shape[1:], lambda i: (0, 0, 0))
    piece = pl.BlockSpec((1, tiles, rows, LANES), lambda i: (i, 0, 0, 0))
    return call(
        functools.partial(attend_back_kernel, steps, diagonal, carry is None, bool(extra)),
        (sds((tiles, total, LANES), F32), sds(a.shape, BF16), sds(b.shape, BF16))
        + ((sds(a.shape[1:], BF16),) if extra else ()),
        [pl.BlockSpec(memory_space=pltpu.SMEM), whole, whole, stat, piece, piece]
        + ([] if carry is None else [whole])
        + [pl.BlockSpec(memory_space=pl.ANY)] * len(after)
        + [one] * len(extra),
        cost=0.05,
        out_specs=(whole, piece, piece) + ((one,) if extra else ()),
        grid=(steps,),
    )(info, queries, d_out, stats, a, b, *(() if carry is None else (carry,)), *after, *extra)


def middle_kernel(
    fused,
    index_ref,
    info_ref,
    x_ref,
    cot_in,
    gain_ref,
    max_ref,
    sum_ref,
    q_ref,
    a_ref,
    b_ref,
    gu0,
    gu1,
    gu2,
    gu3,
    do0,
    do1,
    do2,
    do3,
    turned_ref,
    d_mid_ref,
    d_ref,
    stat_ref,
    keep_ref,
    send_ref,
    out_ref,
    w_gu,
    w_down,
    w_out,
    att_ref,
    n2_ref,
    dn2_ref,
    g_gu,
    g_down,
    g_out,
    slot_ref,
    chunk_ref,
    stage_ref,
    max_out,
    sum_out,
    cot_ref,
    in_sems,
    out_sems,
):
    index = index_ref[0]
    dim = x_ref.shape[1]
    ff = w_down.shape[0]
    fd, fs = ff // 4, dim // 4
    loads = []
    for code, gu, do in zip((0, 1, 2, 3), (gu0, gu1, gu2, gu3), (do0, do1, do2, do3)):
        shard = index ^ code
        down_at = pl.ds(pl.multiple_of(shard * fd, 16), fd)
        at = pl.ds(pl.multiple_of(shard * fs, 16), fs)
        for source, target in (
            (do.at[pl.ds(fd, fs)], w_out.at[at]),
            (gu, w_gu.at[at]),
            (do.at[pl.ds(0, fd)], w_down.at[down_at]),
        ):
            loads.append(pltpu.make_async_copy(source, target, in_sems.at[len(loads)]))
    for copy in loads:
        copy.start()
    if fused:
        attend_rows(
            info_ref, 0, 1, False, q_ref, a_ref, b_ref, max_ref, sum_ref, max_out, sum_out
        )
        max_ref, sum_ref = max_out, sum_out
    tiles, total, _ = max_ref.shape
    seqs = tiles // KV_HEADS
    rows = total // GROUP
    low = lane_of((total, LANES)) < HEAD_DIM
    low_rows = low[:rows]
    outs = []
    for rg in range(tiles):
        sums = sum_ref[rg]
        turned = half_roll(sums)
        both = jnp.where(low, sums, turned)
        log_sum = max_ref[rg] + jnp.log(both)
        stat_ref[rg, 0:1, :] = jnp.transpose(log_sum)[0:1, :]
        normal = jnp.where(low, 0.0, sums / both)
        sum_ref_row = normal
        outs.append(sum_ref_row)
    for r in range(seqs):
        for p in range((HEADS + 1) // 2):
            g, i = divmod(2 * p, GROUP)
            tile = half_roll(outs[r * KV_HEADS + g][i * rows : (i + 1) * rows])
            if 2 * p + 1 < HEADS:
                g, i = divmod(2 * p + 1, GROUP)
                tile = jnp.where(
                    low_rows, tile, outs[r * KV_HEADS + g][i * rows : (i + 1) * rows]
                )
                att_ref[r * rows : (r + 1) * rows, p * LANES : (p + 1) * LANES] = tile.astype(BF16)
            else:
                att_ref[r * rows : (r + 1) * rows, p * LANES :] = tile[:, :HEAD_DIM].astype(BF16)
    for r in range(seqs):
        turned = jnp.transpose(cot_in[r].astype(F32))
        cot_ref[r * rows : (r + 1) * rows, :] = turned.astype(BF16)
    for copy in loads:
        copy.wait()
    att = att_ref[...]
    cot = cot_ref[...]
    mid = x_ref[...].astype(F32) + dot(att, w_out[...])
    inv = inverse_rms(mid)
    gain = gain_ref[...]
    n2 = (mid * inv * gain).astype(BF16)
    n2_ref[...] = n2
    out_ref[...] = mid
    dn2_ref[...] = jnp.zeros_like(dn2_ref)
    width = ff // 2

    def ff_step(i, carry):
        at = pl.multiple_of(i * width, width)
        cols, cols_up = pl.ds(at, width), pl.ds(pl.multiple_of(at + ff, width), width)
        n2 = n2_ref[...]
        w_g, w_u, w_d = w_gu[:, cols], w_gu[:, cols_up], w_down[cols, :]
        gate = dot(n2, w_g)
        up = dot(n2, w_u)
        sig = 1.0 / (1.0 + jnp.exp(-gate))
        silu = gate * sig
        hidden = (silu * up).astype(BF16)
        out_ref[...] += dot(hidden, w_d)
        d_hidden = dot(cot_ref[...], w_d, NT)
        d_gate = (d_hidden * up * sig * (1.0 + gate * (1.0 - sig))).astype(BF16)
        d_up = (d_hidden * silu).astype(BF16)
        g_down[cols, :] = dot(hidden, cot_ref[...], TN)
        g_gu[:, cols] = dot(n2, d_gate, TN).astype(BF16)
        g_gu[:, cols_up] = dot(n2, d_up, TN).astype(BF16)
        dn2_ref[...] += dot(d_gate, w_g, NT) + dot(d_up, w_u, NT)
        return carry

    lax.fori_loop(0, 2, ff_step, 0)
    part = dim // CHUNKS
    quarter = 2 * ff // CHUNKS
    stores = []
    for slot in (2, 3, 0, 1):
        to = keep_ref if slot < 2 else send_ref
        at = pl.ds(pl.multiple_of((index ^ SLOTS[slot]) * fs, 16), fs)
        for c in range(CHUNKS):
            copy = pltpu.make_async_copy(
                g_gu.at[at, pl.ds(c * quarter, quarter)],
                to.at[slot % 2, c, pl.ds(0, fs)],
                out_sems.at[len(stores)],
            )
            copy.start()
            stores.append(copy)
    for r in range(seqs):
        turned_ref[r] = jnp.transpose(out_ref[r * rows : (r + 1) * rows, :])
    dn2 = dn2_ref[...]
    scaled = dn2 * gain
    gain_grad = jnp.sum(dn2 * mid * inv, axis=0, keepdims=True)
    d_mid = (
        cot.astype(F32)
        + inv * scaled
        - mid * (inv * inv * inv) * jnp.mean(scaled * mid, axis=-1, keepdims=True)
    )
    d_mid_ref[...] = d_mid
    d_low = d_mid.astype(BF16)
    g_out[...] = dot(att, d_low, TN)
    d_att = dot(d_low, w_out[...], NT)
    for r in range(seqs):
        for p in range((HEADS + 1) // 2):
            stop = min((p + 1) * LANES, dim)
            tile = d_att[r * rows : (r + 1) * rows, p * LANES : stop]
            if stop - p * LANES < LANES:
                tile = jnp.concatenate([tile, jnp.zeros_like(tile)], axis=1)
            for h in (2 * p, 2 * p + 1):
                if h < HEADS:
                    own = half_roll(tile) if h % 2 == 0 else tile
                    own = jnp.where(low_rows, 0.0, own).astype(BF16)
                    g, i = divmod(h, GROUP)
                    d_ref[r * KV_HEADS + g, i * rows : (i + 1) * rows] = own
    for rg in range(tiles):
        prod = d_ref[rg].astype(F32) * outs[rg]
        stat_ref[rg, 1:2, :] = jnp.sum(jnp.transpose(prod), axis=0, keepdims=True)
    for slot in (2, 3, 0, 1):
        shard = index ^ SLOTS[slot]
        to = keep_ref if slot < 2 else send_ref
        at = pl.ds(pl.multiple_of(shard * fs, 16), fs)
        slot_ref[0:fd, :] = g_down[pl.ds(pl.multiple_of(shard * fd, 16), fd), :]
        slot_ref[fd : fd + fs, :] = g_out[at, :]
        slot_ref[fd + fs :, :] = jnp.broadcast_to(gain_grad, (dim - fd - fs, dim))
        for c in range(CHUNKS):
            chunk_ref[:part, :] = slot_ref[c * part : (c + 1) * part, :quarter]
            top = slot_ref[c * part : c * part + TOP, quarter:]
            rest = slot_ref[c * part + TOP : (c + 1) * part, quarter:]
            fill = jnp.zeros((2 * TOP - part, dim - quarter), F32)
            chunk_ref[part:, :] = jnp.concatenate(
                [top, jnp.concatenate([rest, fill], axis=0)], axis=1
            )
            stage_ref[slot, c] = chunk_ref[...].astype(BF16)
        copy = pltpu.make_async_copy(
            stage_ref.at[slot],
            to.at[slot % 2, pl.ds(0, CHUNKS), pl.ds(fs, part + TOP)],
            out_sems.at[len(stores)],
        )
        copy.start()
        stores.append(copy)
    for copy in stores:
        copy.wait()


def middle(index, x, cot, gain, top, sums, gu, do, info, queries, a, b, fused):
    n, dim = x.shape
    tiles, total, _ = top.shape
    ff2 = gu[0].shape[1]
    ff = ff2 // 2
    chunk = (dim // 4 + dim // CHUNKS + TOP, ff2 // CHUNKS)
    small = (dim // CHUNKS + TOP, ff2 // CHUNKS)
    pair = sds((2, CHUNKS) + chunk, BF16)
    vm = pl.BlockSpec(memory_space=pltpu.VMEM)
    sm = pl.BlockSpec(memory_space=pltpu.SMEM)
    hbm = pl.BlockSpec(memory_space=pl.ANY)
    return call(
        functools.partial(middle_kernel, fused),
        (
            sds((tiles // KV_HEADS, dim, total // GROUP), F32),
            sds((n, dim), F32),
            sds((tiles, total, LANES), BF16),
            sds((tiles, 8, total), F32),
            pair,
            pair,
        ),
        [sm, sm] + [vm] * 8 + [hbm] * 8,
        cost=20.0,
        out_specs=(vm,) * 4 + (hbm,) * 2,
        scratch_shapes=[
            pltpu.VMEM((n, dim), F32),
            pltpu.VMEM((dim, ff2), BF16),
            pltpu.VMEM((ff, dim), BF16),
            pltpu.VMEM((dim, dim), BF16),
            pltpu.VMEM((n, dim), BF16),
            pltpu.VMEM((n, dim), BF16),
            pltpu.VMEM((n, dim), F32),
            pltpu.VMEM((dim, ff2), BF16),
            pltpu.VMEM((ff, dim), F32),
            pltpu.VMEM((dim, dim), F32),
            pltpu.VMEM((dim, dim), F32),
            pltpu.VMEM(small, F32),
            pltpu.VMEM((4, CHUNKS) + small, BF16),
            pltpu.VMEM((tiles, total, LANES), F32),
            pltpu.VMEM((tiles, total, LANES), F32),
            pltpu.VMEM((n, dim), BF16),
            pltpu.SemaphoreType.DMA((12,)),
            pltpu.SemaphoreType.DMA((4 * CHUNKS + 4,)),
        ],
    )(index, info, x, cot, gain, top, sums, queries, a, b, *gu, *do)


def end_kernel(
    index_ref,
    x_ref,
    normed_ref,
    w_ref,
    cos_ref,
    sin_ref,
    dq_ref,
    d_mid_ref,
    *refs,
    parts,
):
    dkv_refs = refs[:parts]
    grad_ref, keep, send, lin_ref, g_ref = refs[-5:]
    index = index_ref[0]
    width = w_ref.shape[1]
    tiles, rows, _ = dkv_refs[0].shape
    seqs = tiles // KV_HEADS
    low = lane_of((rows, LANES)) < HEAD_DIM
    for r in range(seqs):
        at = slice(r * rows, (r + 1) * rows)
        cosines, sines = cos_ref[at, :], sin_ref[at, :]
        cos_kv = jnp.where(low, cosines, 1.0)
        sin_kv = jnp.where(low, sines, 0.0)
        for g in range(KV_HEADS):
            tile = dkv_refs[0][r * KV_HEADS + g].astype(F32)
            for ref in dkv_refs[1:]:
                tile = tile + ref[r * KV_HEADS + g].astype(F32)
            back = tile * cos_kv - swap_halves(tile) * sin_kv
            lin_ref[at, g * LANES : (g + 1) * LANES] = back.astype(BF16)
        first = KV_HEADS * LANES
        for p in range((HEADS + 1) // 2):
            backs = []
            for h in (2 * p, 2 * p + 1):
                if h < HEADS:
                    g, i = divmod(h, GROUP)
                    tile = dq_ref[r * KV_HEADS + g, i * rows : (i + 1) * rows]
                    backs.append((tile * cosines - swap_halves(tile) * sines) * SCALE)
                else:
                    backs.append(jnp.zeros((rows, LANES), F32))
            tile = jnp.where(low, backs[0], half_roll(backs[1]))
            lin_ref[at, first + p * LANES : first + (p + 1) * LANES] = tile.astype(BF16)
    lin = lin_ref[...]
    g_ref[...] = dot(normed_ref[...], lin, TN)
    d_normed = dot(lin, w_ref[...], NT)
    gains = jnp.transpose(w_ref[:, width - LANES :].astype(F32))
    gain = gains[HEAD_DIM : HEAD_DIM + 1, :]
    x = x_ref[...].astype(F32)
    inv = inverse_rms(x)
    scaled = d_normed * gain
    grad = (
        d_mid_ref[...]
        + inv * scaled
        - x * (inv * inv * inv) * jnp.mean(scaled * x, axis=-1, keepdims=True)
    )
    for r in range(seqs):
        grad_ref[r] = jnp.transpose(grad[r * rows : (r + 1) * rows, :])
    gain_grad = jnp.sum(d_normed * x * inv, axis=0, keepdims=True)
    dim = x.shape[1]
    fs = dim // 4
    for slot in range(4):
        start = (index ^ SLOTS[slot]) * fs
        to = keep if slot < 2 else send
        for c in range(CHUNKS):
            half, quarter = divmod(c, 4)
            size, cols = fs // 2, width // 4
            at = pl.ds(pl.multiple_of(start + half * size, 8), size)
            tile = g_ref[at, quarter * cols : (quarter + 1) * cols]
            if c == 3:
                pad = jnp.concatenate(
                    [gain_grad[:, k * HEAD_DIM : (k + 1) * HEAD_DIM] for k in range(HEADS)]
                    + [jnp.zeros((size - HEADS, HEAD_DIM), F32)],
                    axis=0,
                )
                pad = jnp.concatenate([tile[:, : cols - HEAD_DIM], pad], axis=1)
                tile = pad
            to[slot % 2, c] = tile.astype(BF16)


def finish(index, x, normed, w, cosines, sines, dq, dkv, d_mid, after):
    n, dim = x.shape
    width = w.shape[1]
    vm = pl.BlockSpec(memory_space=pltpu.VMEM)
    pair = sds((2, CHUNKS, dim // 8, width // 4), BF16)
    tiles = dkv[0].shape[0]
    return call(
        functools.partial(end_kernel, parts=len(dkv)),
        (sds((tiles // KV_HEADS, dim, dkv[0].shape[1]), F32), pair, pair),
        [pl.BlockSpec(memory_space=pltpu.SMEM)] + [vm] * (7 + len(dkv))
        + [pl.BlockSpec(memory_space=pl.ANY)] * len(after),
        cost=0.05,
        out_specs=(vm,) * 3,
        scratch_shapes=[pltpu.VMEM((n, width), BF16), pltpu.VMEM((dim, width), F32)],
    )(index, x, normed, w, cosines, sines, dq, d_mid, *dkv, *after)


def both_halves(place_ref, parts, d):
    near, far = parts[0][d].astype(F32), parts[1][d].astype(F32)
    flag = place_ref[0] == 0
    return place_ref[1] ^ d, jnp.where(flag, near, far), jnp.where(flag, far, near)


def own_gain(place_ref, row, out_ref):
    size = out_ref.shape[1]
    rows = jnp.broadcast_to(row, (8, row.shape[1]))
    fill = -row.shape[1] % LANES
    rows = jnp.concatenate([rows, jnp.zeros((8, fill), F32)], axis=1)
    turned = pltpu.roll(rows, rows.shape[1] - place_ref[2] * size, 1)
    out_ref[...] = turned[0:1, :size]


def own_kernel(place_ref, *refs):
    parts = refs[:-6]
    gate_ref, up_ref, down_ref, out_ref, gain_ref, all_ref = refs[-6:]
    own_body(place_ref, parts, gate_ref, up_ref, down_ref, out_ref, gain_ref, all_ref)


def own_body(place_ref, parts, gate_ref, up_ref, down_ref, out_ref, gain_ref, all_ref):
    cols = parts[0].shape[-1]
    fs, dim = out_ref.shape
    fd = down_ref.shape[1]
    part = dim // CHUNKS
    width = dim - cols
    for d in range(4):
        quarter, first, second = both_halves(place_ref, parts, d)
        at = pl.ds(pl.multiple_of(quarter * cols, LANES), cols)
        gate_ref[:, at] = first[:fs]
        up_ref[:, at] = second[:fs]
        for c, chunk in ((quarter, first), (4 + quarter, second)):
            start = c * part
            all_ref[pl.ds(pl.multiple_of(start, 8), part), :cols] = chunk[fs : fs + part]
            right = chunk[fs + part :]
            all_ref[pl.ds(pl.multiple_of(start, 8), TOP), cols:] = right[:, :width]
            all_ref[pl.ds(pl.multiple_of(start + TOP, 8), part - TOP), cols:] = right[
                : part - TOP, width:
            ]
    down_ref[...] = jnp.transpose(all_ref[:fd, :])
    out_ref[...] = all_ref[fd : fd + fs, :]
    own_gain(place_ref, all_ref[fd + fs : fd + fs + 1, :], gain_ref)


def own_q_kernel(place_ref, *refs):
    parts = refs[:2]
    query_ref, key_ref, value_ref, gain_ref, all_ref = refs[-5:]
    part, cols = parts[0].shape[1:]
    for d in range(4):
        quarter, first, second = both_halves(place_ref, parts, d)
        at = pl.ds(pl.multiple_of(quarter * cols, LANES), cols)
        all_ref[:part, at] = first
        all_ref[part:, at] = second
    first = KV_HEADS * LANES
    for g in range(KV_HEADS):
        to = slice(g * HEAD_DIM, (g + 1) * HEAD_DIM)
        key_ref[:, to] = all_ref[:, g * LANES : g * LANES + HEAD_DIM]
        value_ref[:, to] = all_ref[:, g * LANES + HEAD_DIM : (g + 1) * LANES]
    query_ref[...] = all_ref[:, first : first + HEADS * HEAD_DIM]
    start = all_ref.shape[1] - HEAD_DIM
    row = jnp.concatenate([all_ref[k : k + 1, start:] for k in range(HEADS)], axis=1)
    own_gain(place_ref, row, gain_ref)


def own(kernel, place, outs, parts, scratch, after=()):
    vm = pl.BlockSpec(memory_space=pltpu.VMEM)
    return call(
        kernel,
        tuple(sds(shape, F32) for shape in outs),
        [pl.BlockSpec(memory_space=pltpu.SMEM)]
        + [vm] * len(parts)
        + [pl.BlockSpec(memory_space=pl.ANY)] * len(after),
        cost=0.05,
        out_specs=(vm,) * len(outs),
        scratch_shapes=[pltpu.VMEM(scratch, F32)],
    )(place, *parts, *after)


def pack_kernel(q_ref, k_ref, v_ref, one_ref, two_ref, out_ref):
    for g in range(KV_HEADS):
        at = slice(g * HEAD_DIM, (g + 1) * HEAD_DIM)
        out_ref[:, g * LANES : g * LANES + HEAD_DIM] = k_ref[:, at]
        out_ref[:, g * LANES + HEAD_DIM : (g + 1) * LANES] = v_ref[:, at]
    first = KV_HEADS * LANES
    full = HEADS * HEAD_DIM
    out_ref[:, first : first + full] = q_ref[...]
    fs = q_ref.shape[0]
    row = lax.broadcasted_iota(jnp.int32, (LANES, fs), 0)
    gains = jnp.where(row == HEAD_DIM, one_ref[...].astype(F32)[None, :], 0.0)
    gains = jnp.where(row == HEAD_DIM + 1, two_ref[...].astype(F32)[None, :], gains)
    out_ref[:, first + full :] = jnp.transpose(gains)[:, HEAD_DIM:].astype(BF16)


def rest_pack_kernel(gate_ref, up_ref, down_ref, w_ref, gu_ref, do_ref):
    ff = gate_ref.shape[1]
    gu_ref[:, :ff] = gate_ref[...]
    gu_ref[:, ff:] = up_ref[...]
    fd = down_ref.shape[1]
    do_ref[:fd, :] = jnp.transpose(down_ref[...].astype(F32)).astype(BF16)
    do_ref[fd:, :] = w_ref[...]


def flip(x, axis, mask):
    n = lax.axis_size(axis)
    return lax.ppermute(x, axis, [(i, i ^ mask) for i in range(n)])


def gather_shards(own):
    across = flip(own, "fsdp", 2)
    return own, flip(own, "fsdp", 1), across, flip(across, "fsdp", 1)


def add(a, b):
    return (a.astype(F32) + b.astype(F32)).astype(BF16)


def total_of(*parts):
    total = parts[0].astype(F32)
    for part in parts[1:]:
        total = total + part.astype(F32)
    return total.astype(BF16)


def add_kernel(place_ref, *refs):
    refs[-1][...] = total_of(*(ref[...] for ref in refs[:-1]))


def core_kernel(place_ref, keep, got, out):
    out[...] = total_of(keep[0], got[0])


def y_kernel(place_ref, keep, got, far, mine, away):
    x_bit = place_ref[0]
    for c in range(4):
        here, there = 4 * x_bit + c, 4 * (1 - x_bit) + c
        mine[c] = total_of(keep[0, here], got[0, here], far[here])
        away[c] = total_of(keep[0, there], got[0, there], far[there])


def x_kernel(place_ref, keep, got, *outs):
    for d in range(4):
        c = place_ref[1] ^ d
        outs[d][...] = total_of(keep[c], got[c])


def stack_kernel(place_ref, *refs):
    for d in range(4):
        refs[4][d] = refs[d][...]


def fuse(kernel, place, outs, ins, after=(), specs=None, out_specs=None, grid=None):
    vm = pl.BlockSpec(memory_space=pltpu.VMEM)
    count = 1 + len(ins)

    def body(*refs):
        kernel(*refs[:count], *refs[count + len(after) :])

    return call(
        body,
        tuple(sds(shape, BF16) for shape in outs),
        [pl.BlockSpec(memory_space=pltpu.SMEM)]
        + (specs or [vm] * len(ins))
        + [pl.BlockSpec(memory_space=pl.ANY)] * len(after),
        cost=0.05,
        out_specs=out_specs or (vm,) * len(outs),
        **({"grid": grid} if grid else {}),
    )(place, *ins, *after)


class Sum:
    def __init__(self, place, keep, send):
        self.place, self.shape = place, keep.shape[2:]
        self.parts = (keep, flip(send, "fsdp", 1))

    def core(self, *after):
        keep, got = self.parts
        two = (2,) + self.shape
        source = pl.BlockSpec((1,) + two, lambda i: (1, i, 0, 0))
        target = pl.BlockSpec(two, lambda i: (i, 0, 0))
        (away,) = fuse(
            core_kernel,
            self.place,
            [(CHUNKS,) + self.shape],
            self.parts,
            after,
            [source, source],
            (target,),
            (CHUNKS // 2,),
        )
        self.parts = (keep, got, flip(away, "fsdp", 2))
        return away

    def y_specs(self):
        first = pl.BlockSpec((1, CHUNKS) + self.shape, lambda i: (0, 0, 0, 0))
        return [first, first, pl.BlockSpec(memory_space=pltpu.VMEM)]

    def y(self, *after):
        shape = (4,) + self.shape
        keep, send = fuse(
            y_kernel, self.place, [shape] * 2, self.parts, after, self.y_specs(), None, (1,)
        )
        self.parts = (keep, flip(send, "ctx", 1))
        return keep

    def x(self, *after):
        mine, *away = fuse(x_kernel, self.place, [self.shape] * 4, self.parts, after)
        self.parts = (mine, *(flip(away[d - 1], "ctx", 2 * d) for d in (1, 2, 3)))
        return mine

    def z(self, *after):
        n = lax.axis_size("ctx")
        (mine,) = fuse(add_kernel, self.place, [self.shape], self.parts, after)
        for b in range(3, n.bit_length() - 1):
            (mine,) = fuse(
                add_kernel, self.place, [self.shape], (mine, flip(mine, "ctx", 1 << b))
            )
        self.parts = (mine, *(flip(mine, "ctx", d) for d in (2, 4, 6)))
        return mine

    def stack(self, *after):
        (every,) = fuse(stack_kernel, self.place, [(4,) + self.shape], self.parts, after)
        self.parts = (every, flip(every, "ctx", 1))
        return every


def send_down(x, levels):
    n = lax.axis_size("ctx")
    return lax.ppermute(x, "ctx", [(i, i - 2 * levels) for i in range(2 * levels, n)])


def local(
    tokens,
    cotangent,
    attn_gain,
    w_query,
    w_key,
    w_value,
    w_out,
    mlp_gain,
    w_gate,
    w_up,
    w_down,
    seq_lengths,
    seq_starts,
):
    seqs, rows, dim = tokens.shape
    n = seqs * rows
    n_ctx = lax.axis_size("ctx")
    me = lax.axis_index("ctx")
    index = lax.axis_index("fsdp").reshape(1).astype(jnp.int32)
    fs = w_query.shape[0]
    cot = jnp.transpose(cotangent, (0, 2, 1))

    used = KV_HEADS * LANES + HEADS * HEAD_DIM + 2
    width = used - used % -LANES
    vm = pl.BlockSpec(memory_space=pltpu.VMEM)
    first = call(pack_kernel, sds((fs, width), BF16), [vm] * 5, cost=1.5, out_specs=vm)(
        w_query, w_key, w_value, attn_gain, mlp_gain
    )
    first_shards = gather_shards(first)
    places = me * rows + jnp.arange(rows, dtype=jnp.int32)
    positions = (places[None, :] - seq_starts[:, None]).astype(F32)
    frequency = THETA ** (-(2.0 * jnp.arange(HEAD_DIM // 2, dtype=F32)) / HEAD_DIM)
    angles = (positions[:, :, None] * frequency).reshape(n, HEAD_DIM // 2)
    cos, sin = jnp.cos(angles), jnp.sin(angles)
    cosines = jnp.concatenate([cos] * 4, axis=1)
    sines = jnp.concatenate([-sin, sin] * 2, axis=1)

    ff, fd = w_gate.shape[1], w_down.shape[0]
    hbm = pl.BlockSpec(memory_space=pl.ANY)
    tiles = seqs * KV_HEADS
    weights, normed, queries, kv, gain_two, x = call(
        qkv_kernel,
        (
            sds((dim, width), BF16),
            sds((n, dim), BF16),
            sds((tiles, GROUP * rows, LANES), BF16),
            sds((tiles, rows, LANES), BF16),
            sds((1, dim), F32),
            sds((n, dim), BF16),
        ),
        [pl.BlockSpec(memory_space=pltpu.SMEM)] + [vm] * 7,
        cost=4.0,
        out_specs=(vm,) * 6,
    )(index, jnp.transpose(tokens, (0, 2, 1)), *first_shards, cosines, sines)

    gu_own, do_own = call(
        rest_pack_kernel,
        (sds((fs, 2 * ff), BF16), sds((fd + fs, dim), BF16)),
        [vm] * 4,
        cost=3.0,
        out_specs=(vm, vm),
    )(w_gate, w_up, w_down.T, w_out)
    gu_shards = gather_shards(gu_own)
    do_shards = gather_shards(do_own)

    spans = [seq_starts.astype(jnp.int32), (seq_starts + seq_lengths).astype(jnp.int32)]

    def info_of(bases):
        return jnp.concatenate([me.reshape(1).astype(jnp.int32), bases.astype(jnp.int32)] + spans)

    x_bit = me % 2
    if n_ctx <= 8 and n_ctx % 2 == 0:
        levels = n_ctx // 2
        up = [(i, i + 2) for i in range(n_ctx - 2)]
        down = [(i + 2, i) for i in range(n_ctx - 2)]
        pieces = []
        piece = kv
        for k in range(levels):
            other = flip(piece, "ctx", 1)
            pair = (me // 2 - k) * 2
            bases = jnp.stack([pair + x_bit, pair + 1 - x_bit]) * rows
            bases = jnp.where(pair >= 0, bases, FAR)
            pieces.append((bases, piece[None], other[None]))
            if k + 1 < levels:
                piece = lax.ppermute(piece, "ctx", up)
        carry = None
        for k in range(levels - 1):
            bases, a, b = pieces[k]
            carry = attend(info_of(bases), queries, a, b, carry, k == 0)
        bases, a, b = pieces[-1]
        last_piece = (info_of(bases), queries, a, b, True)
    else:
        every = lax.all_gather(kv, "ctx", axis=0)
        info = info_of(jnp.arange(n_ctx, dtype=jnp.int32) * rows)
        carry = attend(info, queries, every[0::2], every[1::2], None, True)
        last_piece = (info, queries, every[:1], every[:1], False)

    result, d_mid, d_out, stats, keep_mlp, send_mlp = middle(
        index, x, cot, gain_two, carry[0], carry[1], gu_shards, do_shards, *last_piece
    )

    place = jnp.stack([me & 1, (me >> 1) & 3, index[0]]).astype(jnp.int32)
    mlp = Sum(place, keep_mlp, send_mlp)
    if n_ctx <= 8 and n_ctx % 2 == 0:
        dq, last = None, ()
        dkv, partials = [], []
        for k in reversed(range(levels)):
            bases, a, b = pieces[k]
            extra = partials[0][1:] if k < levels - 2 else ()
            dq, da, db, *both = attend_back(
                info_of(bases),
                queries,
                d_out,
                stats,
                a,
                b,
                dq,
                k == 0,
                last,
                extra,
            )
            if extra:
                dkv.append(send_down(both[0], partials.pop(0)[0]))
            partials.append((k, da[0], flip(db[0], "ctx", 1)))
            last = (mlp.core(dq),) if k == levels - 1 else ()
        while len(partials) > 1:
            far, near, other = partials.pop(0)
            (both,) = fuse(add_kernel, place, [near.shape], (near, other), (dq,))
            dkv.append(send_down(both, far))
            last = (both,)
        dkv = [partials[0][1], partials[0][2]] + dkv
        last = (mlp.y(*last),)
    else:
        dq, da, db = attend_back(
            info, queries, d_out, stats, every[0::2], every[1::2], None, True
        )
        partial = jnp.stack([da, db], axis=1).reshape((n_ctx,) + da.shape[1:])
        dkv = [lax.psum_scatter(partial, "ctx", scatter_dimension=0, tiled=False)]
        mlp.core(dq)
        last = (mlp.y(dq),)

    input_grad, keep_q, send_q = finish(
        index, x, normed, weights, cosines, sines, dq, dkv, d_mid, last
    )
    qkv = Sum(place, keep_q, send_q)
    step = mlp.x(keep_q)
    step = qkv.core(step)
    step = mlp.z(step)
    step = qkv.y(step)
    step = qkv.x(step)
    step = mlp.stack(step)
    step = qkv.z(step)
    step = qkv.stack(step)
    grad_gate, grad_up, grad_down, grad_out, gain_two_grad = own(
        own_kernel,
        place,
        [(fs, ff), (fs, ff), (dim, fd), (fs, dim), (1, fs)],
        mlp.parts,
        (dim, dim),
    )
    grad_down = grad_down.T
    kv_width = KV_HEADS * HEAD_DIM
    grad_query, grad_key, grad_value, gain_one_grad = own(
        own_q_kernel,
        place,
        [(fs, HEADS * HEAD_DIM), (fs, kv_width), (fs, kv_width), (1, fs)],
        qkv.parts,
        (fs, width),
        (grad_gate,),
    )
    grad_mlp_gain = gain_two_grad.reshape(fs)
    grad_attn_gain = gain_one_grad.reshape(fs)
    return (
        jnp.transpose(result, (0, 2, 1)),
        jnp.transpose(input_grad, (0, 2, 1)),
        grad_attn_gain,
        grad_query,
        grad_key,
        grad_value,
        grad_out,
        grad_mlp_gain,
        grad_gate,
        grad_up,
        grad_down,
    )


def solution(mesh):
    rows3 = P("fsdp", "ctx", None)
    mat = P("fsdp", None)
    vec = P("fsdp")
    return jax.shard_map(
        local,
        mesh=mesh,
        in_specs=(rows3, rows3, vec, mat, mat, mat, mat, vec, mat, mat, mat, vec, vec),
        out_specs=(rows3, rows3, vec, mat, mat, mat, mat, vec, mat, mat, mat),
        check_vma=False,
    )
```

```python
import functools
import math

import jax
import jax.numpy as jnp
from jax import lax
from jax.experimental import pallas as pl
from jax.experimental.pallas import tpu as pltpu
from jax.sharding import PartitionSpec as P

HEADS = 9
KV_HEADS = 3
HEAD_DIM = 64
GROUP = HEADS // KV_HEADS
LANES = 128
EPSILON = 1e-05
THETA = 100000.0
SCALE = HEAD_DIM ** (-0.5)
MASKED = -2e30
LOWEST = -1e30
FAR = 1 << 29
CHUNKS = 8
SLOTS = (0, 2, 1, 3)
TOP = 40
BF16 = jnp.bfloat16
F32 = jnp.float32
NN = (((1,), (0,)), ((), ()))
NT = (((1,), (1,)), ((), ()))
TN = (((0,), (0,)), ((), ()))
VMEM_LIMIT = 64 * 1024 * 1024 - 65536
PER_US = 1.0e9


def dot(a, b, dims=NN):
    return lax.dot_general(a, b, dims, preferred_element_type=F32)


def call(kernel, out_shape, in_specs=None, cost=1.0, **kwargs):
    return pl.pallas_call(
        kernel,
        out_shape=out_shape,
        in_specs=in_specs,
        compiler_params=pltpu.CompilerParams(vmem_limit_bytes=VMEM_LIMIT),
        cost_estimate=pl.CostEstimate(
            flops=int(cost * PER_US), bytes_accessed=0, transcendentals=0
        ),
        **kwargs,
    )


def sds(shape, dtype):
    return jax.ShapeDtypeStruct(shape, dtype)


def lane_of(shape):
    return lax.broadcasted_iota(jnp.int32, shape, 1)


def swap_halves(tile):
    lane = lane_of(tile.shape) % HEAD_DIM
    return jnp.where(
        lane < HEAD_DIM // 2, pltpu.roll(tile, LANES - 32, 1), pltpu.roll(tile, 32, 1)
    )


def half_roll(tile):
    return pltpu.roll(tile, HEAD_DIM, 1)


def assemble(target, index, shards, rows):
    for code, ref in zip((0, 1, 2, 3), shards):
        start = pl.multiple_of((index ^ code) * rows, 16)
        target[pl.ds(start, rows), :] = ref[...]


def inverse_rms(rows):
    return lax.rsqrt(jnp.mean(rows * rows, axis=-1, keepdims=True) + EPSILON)


def qkv_kernel(index_ref, x_ref, w0, w1, w2, w3, cos_ref, sin_ref, w_ref, normed_ref, q_ref, kv_ref, two_ref, rows_ref):
    assemble(w_ref, index_ref[0], (w0, w1, w2, w3), w0.shape[0])
    width = w_ref.shape[1]
    gains = jnp.transpose(w_ref[:, width - LANES :].astype(F32))
    count = x_ref.shape[2]
    for r in range(x_ref.shape[0]):
        turned = jnp.transpose(x_ref[r].astype(F32))
        rows_ref[r * count : (r + 1) * count, :] = turned.astype(BF16)
    x = rows_ref[...].astype(F32)
    normed = (x * inverse_rms(x) * gains[HEAD_DIM : HEAD_DIM + 1, :]).astype(BF16)
    normed_ref[...] = normed
    two_ref[...] = gains[HEAD_DIM + 1 : HEAD_DIM + 2, :]
    cosines, sines = cos_ref[...], sin_ref[...]
    lane = lane_of(cosines.shape)
    low = lane < HEAD_DIM
    cos_kv = jnp.where(low, cosines, 1.0)
    sin_kv = jnp.where(low, sines, 0.0)
    rows = kv_ref.shape[1]
    seqs = x.shape[0] // rows
    for g in range(KV_HEADS):
        tile = dot(normed, w_ref[:, g * LANES : (g + 1) * LANES])
        turned = (tile * cos_kv + swap_halves(tile) * sin_kv).astype(BF16)
        for r in range(seqs):
            kv_ref[r * KV_HEADS + g] = turned[r * rows : (r + 1) * rows]
    first = KV_HEADS * LANES
    lin = dot(normed, w_ref[:, first:])
    for p in range((HEADS + 1) // 2):
        tile = lin[:, p * LANES : (p + 1) * LANES]
        turned = (tile * cosines + swap_halves(tile) * sines) * SCALE
        for h in (2 * p, 2 * p + 1):
            if h < HEADS:
                own = turned if h % 2 == 0 else half_roll(turned)
                own = jnp.where(low, own, 0.0).astype(BF16)
                g, i = divmod(h, GROUP)
                for r in range(seqs):
                    q_ref[r * KV_HEADS + g, i * rows : (i + 1) * rows] = own[
                        r * rows : (r + 1) * rows
                    ]


def pair_places(info_ref, step, rows, axis):
    shape = (1, 2 * rows) if axis == 1 else (2 * rows, 1)
    at = lax.broadcasted_iota(jnp.int32, shape, axis)
    first, second = info_ref[1 + 2 * step], info_ref[2 + 2 * step]
    return jnp.where(at < rows, first + at, second + at - rows)


def query_places(info_ref, rows, axis):
    total = GROUP * rows
    shape = (1, total) if axis == 1 else (total, 1)
    at = lax.broadcasted_iota(jnp.int32, shape, axis)
    return info_ref[0] * rows + at % rows


def seen_of(key_places, q_places, start, end, diagonal):
    key_in = (key_places >= start) & (key_places < end)
    query_in = (q_places >= start) & (q_places < end)
    seen = jnp.where(key_in, key_places, FAR) <= jnp.where(query_in, q_places, -1)
    if diagonal:
        seen = seen | (key_places == q_places)
    return seen


def row_active(info_ref, step, rows, start, end):
    own = info_ref[0] * rows
    first, second = info_ref[1 + 2 * step], info_ref[2 + 2 * step]
    keys_in = ((first < end) & (first + rows > start)) | ((second < end) & (second + rows > start))
    return (own < end) & (own + rows > start) & keys_in & (jnp.minimum(first, second) <= own)


def attend_rows(
    info_ref, step, steps, diagonal, q_ref, a_ref, b_ref, max_in, sum_in, max_ref, sum_ref
):
    rows = a_ref.shape[2]
    seqs = q_ref.shape[0] // KV_HEADS
    spans = 1 + 2 * steps

    def one_seq(r, unused):
        start = info_ref[spans + r]
        end = info_ref[spans + seqs + r]

        def one_row():
            seen = seen_of(
                pair_places(info_ref, step, rows, 1),
                query_places(info_ref, rows, 0),
                start,
                end,
                diagonal,
            )
            for g in range(KV_HEADS):
                rg = r * KV_HEADS + g
                kv = jnp.concatenate([a_ref[0, rg], b_ref[0, rg]], axis=0)
                scores = jnp.where(seen, dot(q_ref[rg], kv, NT), MASKED)
                old = max_in[rg]
                new = jnp.maximum(old, jnp.max(scores, axis=-1, keepdims=True))
                weights = jnp.exp(scores - jnp.concatenate([new, new], axis=1)).astype(BF16)
                ones = jnp.where(lane_of(kv.shape) < HEAD_DIM, jnp.ones_like(kv), kv)
                sum_ref[rg] = sum_in[rg] * jnp.exp(old - new) + dot(weights, ones)
                max_ref[rg] = new

        def keep_row():
            for g in range(KV_HEADS):
                max_ref[r * KV_HEADS + g] = max_in[r * KV_HEADS + g]
                sum_ref[r * KV_HEADS + g] = sum_in[r * KV_HEADS + g]

        if diagonal:
            one_row()
        else:
            active = row_active(info_ref, step, rows, start, end)
            pl.when(active)(one_row)
            if max_in is not max_ref:
                pl.when(jnp.logical_not(active))(keep_row)
        return unused

    lax.fori_loop(0, seqs, one_seq, 0)


def attend_kernel(steps, diagonal, fresh, info_ref, q_ref, a_ref, b_ref, *refs):
    if fresh:
        max_ref, sum_ref = refs
    else:
        max_in, sum_in, max_ref, sum_ref = refs
    step = pl.program_id(0)

    @pl.when(step == 0)
    def _():
        if fresh:
            max_ref[...] = jnp.full_like(max_ref, LOWEST)
            sum_ref[...] = jnp.zeros_like(sum_ref)
        else:
            max_ref[...] = max_in[...]
            sum_ref[...] = sum_in[...]

    attend_rows(
        info_ref, step, steps, diagonal, q_ref, a_ref, b_ref, max_ref, sum_ref, max_ref, sum_ref
    )


def attend(info, queries, a, b, carry, diagonal):
    steps = a.shape[0]
    tiles, total, _ = queries.shape
    rows = a.shape[2]
    whole = pl.BlockSpec((tiles, total, LANES), lambda i: (0, 0, 0))
    piece = pl.BlockSpec((1, tiles, rows, LANES), lambda i: (i, 0, 0, 0))
    return call(
        functools.partial(attend_kernel, steps, diagonal, carry is None),
        (sds((tiles, total, LANES), F32),) * 2,
        [pl.BlockSpec(memory_space=pltpu.SMEM), whole, piece, piece]
        + ([] if carry is None else [whole] * 2),
        cost=10.0 * steps,
        out_specs=(whole, whole),
        grid=(steps,),
    )(info, queries, a, b, *(carry or ()))


def attend_back_kernel(
    steps, diagonal, fresh, extra, info_ref, q_ref, d_ref, stat_ref, a_ref, b_ref, *refs
):
    if extra:
        refs[-1][...] = total_of(refs[-6][...], refs[-5][...])
        dq_ref, da_ref, db_ref = refs[-4:-1]
    else:
        dq_ref, da_ref, db_ref = refs[-3:]
    dq_in = refs[0]
    step = pl.program_id(0)
    rows = a_ref.shape[2]
    seqs = q_ref.shape[0] // KV_HEADS
    spans = 1 + 2 * steps

    @pl.when(step == 0)
    def _():
        dq_ref[...] = jnp.zeros_like(dq_ref) if fresh else dq_in[...]

    def one_seq(r, unused):
        start = info_ref[spans + r]
        end = info_ref[spans + seqs + r]

        def one_row():
            seen = seen_of(
                pair_places(info_ref, step, rows, 0),
                query_places(info_ref, rows, 1),
                start,
                end,
                diagonal,
            )
            for g in range(KV_HEADS):
                rg = r * KV_HEADS + g
                kv = jnp.concatenate([a_ref[0, rg], b_ref[0, rg]], axis=0)
                q, d = q_ref[rg], d_ref[rg]
                log_sum = stat_ref[rg, 0:1, :]
                delta = stat_ref[rg, 1:2, :]
                scores = jnp.where(seen, dot(kv, q, NT), MASKED)
                probs = jnp.exp(scores - log_sum)
                d_scores = (probs * (dot(kv, d, NT) - delta)).astype(BF16)
                grad = (dot(d_scores, q) + dot(probs.astype(BF16), d)).astype(BF16)
                da_ref[0, rg] = grad[:rows]
                db_ref[0, rg] = grad[rows:]
                dq_ref[rg] = dq_ref[rg] + dot(d_scores, kv, TN)

        if diagonal:
            one_row()
        else:
            active = row_active(info_ref, step, rows, start, end)
            pl.when(active)(one_row)

            @pl.when(jnp.logical_not(active))
            def _():
                for g in range(KV_HEADS):
                    rg = r * KV_HEADS + g
                    da_ref[0, rg] = jnp.zeros((rows, LANES), BF16)
                    db_ref[0, rg] = jnp.zeros((rows, LANES), BF16)

        return unused

    lax.fori_loop(0, seqs, one_seq, 0)


def attend_back(info, queries, d_out, stats, a, b, carry, diagonal, after=(), extra=()):
    steps = a.shape[0]
    tiles, total, _ = queries.shape
    rows = a.shape[2]
    whole = pl.BlockSpec((tiles, total, LANES), lambda i: (0, 0, 0))
    stat = pl.BlockSpec(stats.shape, lambda i: (0, 0, 0))
    one = pl.BlockSpec(a.shape[1:], lambda i: (0, 0, 0))
    piece = pl.BlockSpec((1, tiles, rows, LANES), lambda i: (i, 0, 0, 0))
    return call(
        functools.partial(attend_back_kernel, steps, diagonal, carry is None, bool(extra)),
        (sds((tiles, total, LANES), F32), sds(a.shape, BF16), sds(b.shape, BF16))
        + ((sds(a.shape[1:], BF16),) if extra else ()),
        [pl.BlockSpec(memory_space=pltpu.SMEM), whole, whole, stat, piece, piece]
        + ([] if carry is None else [whole])
        + [pl.BlockSpec(memory_space=pl.ANY)] * len(after)
        + [one] * len(extra),
        cost=0.05,
        out_specs=(whole, piece, piece) + ((one,) if extra else ()),
        grid=(steps,),
    )(info, queries, d_out, stats, a, b, *(() if carry is None else (carry,)), *after, *extra)


def middle_kernel(
    fused,
    index_ref,
    info_ref,
    x_ref,
    cot_in,
    gain_ref,
    max_ref,
    sum_ref,
    q_ref,
    a_ref,
    b_ref,
    gu0,
    gu1,
    gu2,
    gu3,
    do0,
    do1,
    do2,
    do3,
    turned_ref,
    d_mid_ref,
    d_ref,
    stat_ref,
    keep_ref,
    send_ref,
    out_ref,
    w_gu,
    w_down,
    w_out,
    att_ref,
    n2_ref,
    dn2_ref,
    g_gu,
    g_down,
    g_out,
    slot_ref,
    chunk_ref,
    stage_ref,
    max_out,
    sum_out,
    cot_ref,
    in_sems,
    out_sems,
):
    index = index_ref[0]
    dim = x_ref.shape[1]
    ff = w_down.shape[0]
    fd, fs = ff // 4, dim // 4
    loads = []
    for code, gu, do in zip((0, 1, 2, 3), (gu0, gu1, gu2, gu3), (do0, do1, do2, do3)):
        shard = index ^ code
        down_at = pl.ds(pl.multiple_of(shard * fd, 16), fd)
        at = pl.ds(pl.multiple_of(shard * fs, 16), fs)
        for source, target in (
            (do.at[pl.ds(fd, fs)], w_out.at[at]),
            (gu, w_gu.at[at]),
            (do.at[pl.ds(0, fd)], w_down.at[down_at]),
        ):
            loads.append(pltpu.make_async_copy(source, target, in_sems.at[len(loads)]))
    for copy in loads:
        copy.start()
    if fused:
        attend_rows(
            info_ref, 0, 1, False, q_ref, a_ref, b_ref, max_ref, sum_ref, max_out, sum_out
        )
        max_ref, sum_ref = max_out, sum_out
    tiles, total, _ = max_ref.shape
    seqs = tiles // KV_HEADS
    rows = total // GROUP
    low = lane_of((total, LANES)) < HEAD_DIM
    low_rows = low[:rows]
    outs = []
    for rg in range(tiles):
        sums = sum_ref[rg]
        turned = half_roll(sums)
        both = jnp.where(low, sums, turned)
        log_sum = max_ref[rg] + jnp.log(both)
        stat_ref[rg, 0:1, :] = jnp.transpose(log_sum)[0:1, :]
        normal = jnp.where(low, 0.0, sums / both)
        sum_ref_row = normal
        outs.append(sum_ref_row)
    for r in range(seqs):
        for p in range((HEADS + 1) // 2):
            g, i = divmod(2 * p, GROUP)
            tile = half_roll(outs[r * KV_HEADS + g][i * rows : (i + 1) * rows])
            if 2 * p + 1 < HEADS:
                g, i = divmod(2 * p + 1, GROUP)
                tile = jnp.where(
                    low_rows, tile, outs[r * KV_HEADS + g][i * rows : (i + 1) * rows]
                )
                att_ref[r * rows : (r + 1) * rows, p * LANES : (p + 1) * LANES] = tile.astype(BF16)
            else:
                att_ref[r * rows : (r + 1) * rows, p * LANES :] = tile[:, :HEAD_DIM].astype(BF16)
    for r in range(seqs):
        turned = jnp.transpose(cot_in[r].astype(F32))
        cot_ref[r * rows : (r + 1) * rows, :] = turned.astype(BF16)
    for copy in loads:
        copy.wait()
    att = att_ref[...]
    cot = cot_ref[...]
    mid = x_ref[...].astype(F32) + dot(att, w_out[...])
    inv = inverse_rms(mid)
    gain = gain_ref[...]
    n2 = (mid * inv * gain).astype(BF16)
    n2_ref[...] = n2
    out_ref[...] = mid
    dn2_ref[...] = jnp.zeros_like(dn2_ref)
    width = ff // 2

    def ff_step(i, carry):
        at = pl.multiple_of(i * width, width)
        cols, cols_up = pl.ds(at, width), pl.ds(pl.multiple_of(at + ff, width), width)
        n2 = n2_ref[...]
        w_g, w_u, w_d = w_gu[:, cols], w_gu[:, cols_up], w_down[cols, :]
        gate = dot(n2, w_g)
        up = dot(n2, w_u)
        sig = 1.0 / (1.0 + jnp.exp(-gate))
        silu = gate * sig
        hidden = (silu * up).astype(BF16)
        out_ref[...] += dot(hidden, w_d)
        d_hidden = dot(cot_ref[...], w_d, NT)
        d_gate = (d_hidden * up * sig * (1.0 + gate * (1.0 - sig))).astype(BF16)
        d_up = (d_hidden * silu).astype(BF16)
        g_down[cols, :] = dot(hidden, cot_ref[...], TN)
        g_gu[:, cols] = dot(n2, d_gate, TN).astype(BF16)
        g_gu[:, cols_up] = dot(n2, d_up, TN).astype(BF16)
        dn2_ref[...] += dot(d_gate, w_g, NT) + dot(d_up, w_u, NT)
        return carry

    lax.fori_loop(0, 2, ff_step, 0)
    part = dim // CHUNKS
    quarter = 2 * ff // CHUNKS
    stores = []
    for slot in (2, 3, 0, 1):
        to = keep_ref if slot < 2 else send_ref
        at = pl.ds(pl.multiple_of((index ^ SLOTS[slot]) * fs, 16), fs)
        for c in range(CHUNKS):
            copy = pltpu.make_async_copy(
                g_gu.at[at, pl.ds(c * quarter, quarter)],
                to.at[slot % 2, c, pl.ds(0, fs)],
                out_sems.at[len(stores)],
            )
            copy.start()
            stores.append(copy)
    for r in range(seqs):
        turned_ref[r] = jnp.transpose(out_ref[r * rows : (r + 1) * rows, :])
    dn2 = dn2_ref[...]
    scaled = dn2 * gain
    gain_grad = jnp.sum(dn2 * mid * inv, axis=0, keepdims=True)
    d_mid = (
        cot.astype(F32)
        + inv * scaled
        - mid * (inv * inv * inv) * jnp.mean(scaled * mid, axis=-1, keepdims=True)
    )
    d_mid_ref[...] = d_mid
    d_low = d_mid.astype(BF16)
    g_out[...] = dot(att, d_low, TN)
    d_att = dot(d_low, w_out[...], NT)
    for r in range(seqs):
        for p in range((HEADS + 1) // 2):
            stop = min((p + 1) * LANES, dim)
            tile = d_att[r * rows : (r + 1) * rows, p * LANES : stop]
            if stop - p * LANES < LANES:
                tile = jnp.concatenate([tile, jnp.zeros_like(tile)], axis=1)
            for h in (2 * p, 2 * p + 1):
                if h < HEADS:
                    own = half_roll(tile) if h % 2 == 0 else tile
                    own = jnp.where(low_rows, 0.0, own).astype(BF16)
                    g, i = divmod(h, GROUP)
                    d_ref[r * KV_HEADS + g, i * rows : (i + 1) * rows] = own
    for rg in range(tiles):
        prod = d_ref[rg].astype(F32) * outs[rg]
        stat_ref[rg, 1:2, :] = jnp.sum(jnp.transpose(prod), axis=0, keepdims=True)
    for slot in (2, 3, 0, 1):
        shard = index ^ SLOTS[slot]
        to = keep_ref if slot < 2 else send_ref
        at = pl.ds(pl.multiple_of(shard * fs, 16), fs)
        slot_ref[0:fd, :] = g_down[pl.ds(pl.multiple_of(shard * fd, 16), fd), :]
        slot_ref[fd : fd + fs, :] = g_out[at, :]
        slot_ref[fd + fs :, :] = jnp.broadcast_to(gain_grad, (dim - fd - fs, dim))
        for c in range(CHUNKS):
            chunk_ref[:part, :] = slot_ref[c * part : (c + 1) * part, :quarter]
            top = slot_ref[c * part : c * part + TOP, quarter:]
            rest = slot_ref[c * part + TOP : (c + 1) * part, quarter:]
            fill = jnp.zeros((2 * TOP - part, dim - quarter), F32)
            chunk_ref[part:, :] = jnp.concatenate(
                [top, jnp.concatenate([rest, fill], axis=0)], axis=1
            )
            stage_ref[slot, c] = chunk_ref[...].astype(BF16)
        copy = pltpu.make_async_copy(
            stage_ref.at[slot],
            to.at[slot % 2, pl.ds(0, CHUNKS), pl.ds(fs, part + TOP)],
            out_sems.at[len(stores)],
        )
        copy.start()
        stores.append(copy)
    for copy in stores:
        copy.wait()


def middle(index, x, cot, gain, top, sums, gu, do, info, queries, a, b, fused):
    n, dim = x.shape
    tiles, total, _ = top.shape
    ff2 = gu[0].shape[1]
    ff = ff2 // 2
    chunk = (dim // 4 + dim // CHUNKS + TOP, ff2 // CHUNKS)
    small = (dim // CHUNKS + TOP, ff2 // CHUNKS)
    pair = sds((2, CHUNKS) + chunk, BF16)
    vm = pl.BlockSpec(memory_space=pltpu.VMEM)
    sm = pl.BlockSpec(memory_space=pltpu.SMEM)
    hbm = pl.BlockSpec(memory_space=pl.ANY)
    return call(
        functools.partial(middle_kernel, fused),
        (
            sds((tiles // KV_HEADS, dim, total // GROUP), F32),
            sds((n, dim), F32),
            sds((tiles, total, LANES), BF16),
            sds((tiles, 8, total), F32),
            pair,
            pair,
        ),
        [sm, sm] + [vm] * 8 + [hbm] * 8,
        cost=20.0,
        out_specs=(vm,) * 4 + (hbm,) * 2,
        scratch_shapes=[
            pltpu.VMEM((n, dim), F32),
            pltpu.VMEM((dim, ff2), BF16),
            pltpu.VMEM((ff, dim), BF16),
            pltpu.VMEM((dim, dim), BF16),
            pltpu.VMEM((n, dim), BF16),
            pltpu.VMEM((n, dim), BF16),
            pltpu.VMEM((n, dim), F32),
            pltpu.VMEM((dim, ff2), BF16),
            pltpu.VMEM((ff, dim), F32),
            pltpu.VMEM((dim, dim), F32),
            pltpu.VMEM((dim, dim), F32),
            pltpu.VMEM(small, F32),
            pltpu.VMEM((4, CHUNKS) + small, BF16),
            pltpu.VMEM((tiles, total, LANES), F32),
            pltpu.VMEM((tiles, total, LANES), F32),
            pltpu.VMEM((n, dim), BF16),
            pltpu.SemaphoreType.DMA((12,)),
            pltpu.SemaphoreType.DMA((4 * CHUNKS + 4,)),
        ],
    )(index, info, x, cot, gain, top, sums, queries, a, b, *gu, *do)


def end_kernel(
    index_ref,
    x_ref,
    normed_ref,
    w_ref,
    cos_ref,
    sin_ref,
    dq_ref,
    d_mid_ref,
    *refs,
    parts,
):
    dkv_refs = refs[:parts]
    grad_ref, keep, send, lin_ref, g_ref = refs[-5:]
    index = index_ref[0]
    width = w_ref.shape[1]
    tiles, rows, _ = dkv_refs[0].shape
    seqs = tiles // KV_HEADS
    low = lane_of((rows, LANES)) < HEAD_DIM
    for r in range(seqs):
        at = slice(r * rows, (r + 1) * rows)
        cosines, sines = cos_ref[at, :], sin_ref[at, :]
        cos_kv = jnp.where(low, cosines, 1.0)
        sin_kv = jnp.where(low, sines, 0.0)
        for g in range(KV_HEADS):
            tile = dkv_refs[0][r * KV_HEADS + g].astype(F32)
            for ref in dkv_refs[1:]:
                tile = tile + ref[r * KV_HEADS + g].astype(F32)
            back = tile * cos_kv - swap_halves(tile) * sin_kv
            lin_ref[at, g * LANES : (g + 1) * LANES] = back.astype(BF16)
        first = KV_HEADS * LANES
        for p in range((HEADS + 1) // 2):
            backs = []
            for h in (2 * p, 2 * p + 1):
                if h < HEADS:
                    g, i = divmod(h, GROUP)
                    tile = dq_ref[r * KV_HEADS + g, i * rows : (i + 1) * rows]
                    backs.append((tile * cosines - swap_halves(tile) * sines) * SCALE)
                else:
                    backs.append(jnp.zeros((rows, LANES), F32))
            tile = jnp.where(low, backs[0], half_roll(backs[1]))
            lin_ref[at, first + p * LANES : first + (p + 1) * LANES] = tile.astype(BF16)
    lin = lin_ref[...]
    g_ref[...] = dot(normed_ref[...], lin, TN)
    d_normed = dot(lin, w_ref[...], NT)
    gains = jnp.transpose(w_ref[:, width - LANES :].astype(F32))
    gain = gains[HEAD_DIM : HEAD_DIM + 1, :]
    x = x_ref[...].astype(F32)
    inv = inverse_rms(x)
    scaled = d_normed * gain
    grad = (
        d_mid_ref[...]
        + inv * scaled
        - x * (inv * inv * inv) * jnp.mean(scaled * x, axis=-1, keepdims=True)
    )
    for r in range(seqs):
        grad_ref[r] = jnp.transpose(grad[r * rows : (r + 1) * rows, :])
    gain_grad = jnp.sum(d_normed * x * inv, axis=0, keepdims=True)
    dim = x.shape[1]
    fs = dim // 4
    for slot in range(4):
        start = (index ^ SLOTS[slot]) * fs
        to = keep if slot < 2 else send
        for c in range(CHUNKS):
            half, quarter = divmod(c, 4)
            size, cols = fs // 2, width // 4
            at = pl.ds(pl.multiple_of(start + half * size, 8), size)
            tile = g_ref[at, quarter * cols : (quarter + 1) * cols]
            if c == 3:
                pad = jnp.concatenate(
                    [gain_grad[:, k * HEAD_DIM : (k + 1) * HEAD_DIM] for k in range(HEADS)]
                    + [jnp.zeros((size - HEADS, HEAD_DIM), F32)],
                    axis=0,
                )
                pad = jnp.concatenate([tile[:, : cols - HEAD_DIM], pad], axis=1)
                tile = pad
            to[slot % 2, c] = tile.astype(BF16)


def finish(index, x, normed, w, cosines, sines, dq, dkv, d_mid, after):
    n, dim = x.shape
    width = w.shape[1]
    vm = pl.BlockSpec(memory_space=pltpu.VMEM)
    pair = sds((2, CHUNKS, dim // 8, width // 4), BF16)
    tiles = dkv[0].shape[0]
    return call(
        functools.partial(end_kernel, parts=len(dkv)),
        (sds((tiles // KV_HEADS, dim, dkv[0].shape[1]), F32), pair, pair),
        [pl.BlockSpec(memory_space=pltpu.SMEM)] + [vm] * (7 + len(dkv))
        + [pl.BlockSpec(memory_space=pl.ANY)] * len(after),
        cost=0.05,
        out_specs=(vm,) * 3,
        scratch_shapes=[pltpu.VMEM((n, width), BF16), pltpu.VMEM((dim, width), F32)],
    )(index, x, normed, w, cosines, sines, dq, d_mid, *dkv, *after)


def both_halves(place_ref, parts, d):
    near, far = parts[0][d].astype(F32), parts[1][d].astype(F32)
    flag = place_ref[0] == 0
    return place_ref[1] ^ d, jnp.where(flag, near, far), jnp.where(flag, far, near)


def own_gain(place_ref, row, out_ref):
    size = out_ref.shape[1]
    rows = jnp.broadcast_to(row, (8, row.shape[1]))
    fill = -row.shape[1] % LANES
    rows = jnp.concatenate([rows, jnp.zeros((8, fill), F32)], axis=1)
    turned = pltpu.roll(rows, rows.shape[1] - place_ref[2] * size, 1)
    out_ref[...] = turned[0:1, :size]


def own_kernel(place_ref, *refs):
    parts = refs[:-6]
    gate_ref, up_ref, down_ref, out_ref, gain_ref, all_ref = refs[-6:]
    own_body(place_ref, parts, gate_ref, up_ref, down_ref, out_ref, gain_ref, all_ref)


def own_body(place_ref, parts, gate_ref, up_ref, down_ref, out_ref, gain_ref, all_ref):
    cols = parts[0].shape[-1]
    fs, dim = out_ref.shape
    fd = down_ref.shape[1]
    part = dim // CHUNKS
    width = dim - cols
    for d in range(4):
        quarter, first, second = both_halves(place_ref, parts, d)
        at = pl.ds(pl.multiple_of(quarter * cols, LANES), cols)
        gate_ref[:, at] = first[:fs]
        up_ref[:, at] = second[:fs]
        for c, chunk in ((quarter, first), (4 + quarter, second)):
            start = c * part
            all_ref[pl.ds(pl.multiple_of(start, 8), part), :cols] = chunk[fs : fs + part]
            right = chunk[fs + part :]
            all_ref[pl.ds(pl.multiple_of(start, 8), TOP), cols:] = right[:, :width]
            all_ref[pl.ds(pl.multiple_of(start + TOP, 8), part - TOP), cols:] = right[
                : part - TOP, width:
            ]
    down_ref[...] = jnp.transpose(all_ref[:fd, :])
    out_ref[...] = all_ref[fd : fd + fs, :]
    own_gain(place_ref, all_ref[fd + fs : fd + fs + 1, :], gain_ref)


def own_q_kernel(place_ref, *refs):
    parts = refs[:2]
    query_ref, key_ref, value_ref, gain_ref, all_ref = refs[-5:]
    part, cols = parts[0].shape[1:]
    for d in range(4):
        quarter, first, second = both_halves(place_ref, parts, d)
        at = pl.ds(pl.multiple_of(quarter * cols, LANES), cols)
        all_ref[:part, at] = first
        all_ref[part:, at] = second
    first = KV_HEADS * LANES
    for g in range(KV_HEADS):
        to = slice(g * HEAD_DIM, (g + 1) * HEAD_DIM)
        key_ref[:, to] = all_ref[:, g * LANES : g * LANES + HEAD_DIM]
        value_ref[:, to] = all_ref[:, g * LANES + HEAD_DIM : (g + 1) * LANES]
    query_ref[...] = all_ref[:, first : first + HEADS * HEAD_DIM]
    start = all_ref.shape[1] - HEAD_DIM
    row = jnp.concatenate([all_ref[k : k + 1, start:] for k in range(HEADS)], axis=1)
    own_gain(place_ref, row, gain_ref)


def own(kernel, place, outs, parts, scratch, after=()):
    vm = pl.BlockSpec(memory_space=pltpu.VMEM)
    return call(
        kernel,
        tuple(sds(shape, F32) for shape in outs),
        [pl.BlockSpec(memory_space=pltpu.SMEM)]
        + [vm] * len(parts)
        + [pl.BlockSpec(memory_space=pl.ANY)] * len(after),
        cost=0.05,
        out_specs=(vm,) * len(outs),
        scratch_shapes=[pltpu.VMEM(scratch, F32)],
    )(place, *parts, *after)


def pack_kernel(q_ref, k_ref, v_ref, one_ref, two_ref, out_ref):
    for g in range(KV_HEADS):
        at = slice(g * HEAD_DIM, (g + 1) * HEAD_DIM)
        out_ref[:, g * LANES : g * LANES + HEAD_DIM] = k_ref[:, at]
        out_ref[:, g * LANES + HEAD_DIM : (g + 1) * LANES] = v_ref[:, at]
    first = KV_HEADS * LANES
    full = HEADS * HEAD_DIM
    out_ref[:, first : first + full] = q_ref[...]
    fs = q_ref.shape[0]
    row = lax.broadcasted_iota(jnp.int32, (LANES, fs), 0)
    gains = jnp.where(row == HEAD_DIM, one_ref[...].astype(F32)[None, :], 0.0)
    gains = jnp.where(row == HEAD_DIM + 1, two_ref[...].astype(F32)[None, :], gains)
    out_ref[:, first + full :] = jnp.transpose(gains)[:, HEAD_DIM:].astype(BF16)


def rest_pack_kernel(gate_ref, up_ref, down_ref, w_ref, gu_ref, do_ref):
    ff = gate_ref.shape[1]
    gu_ref[:, :ff] = gate_ref[...]
    gu_ref[:, ff:] = up_ref[...]
    fd = down_ref.shape[1]
    do_ref[:fd, :] = jnp.transpose(down_ref[...].astype(F32)).astype(BF16)
    do_ref[fd:, :] = w_ref[...]


def flip(x, axis, mask):
    n = lax.axis_size(axis)
    return lax.ppermute(x, axis, [(i, i ^ mask) for i in range(n)])


def gather_shards(own):
    across = flip(own, "fsdp", 2)
    return own, flip(own, "fsdp", 1), across, flip(across, "fsdp", 1)


def add(a, b):
    return (a.astype(F32) + b.astype(F32)).astype(BF16)


def total_of(*parts):
    total = parts[0].astype(F32)
    for part in parts[1:]:
        total = total + part.astype(F32)
    return total.astype(BF16)


def add_kernel(place_ref, *refs):
    refs[-1][...] = total_of(*(ref[...] for ref in refs[:-1]))


def core_kernel(place_ref, keep, got, *refs):
    out, keep_all, got_all, out_all, sems = refs[-5:]
    loads = []
    for c in range(CHUNKS):
        for i, (source, target) in enumerate(((keep, keep_all), (got, got_all))):
            copy = pltpu.make_async_copy(source.at[1, c], target.at[c], sems.at[i, c])
            copy.start()
            loads.append(copy)
    stores = []
    for c in range(CHUNKS):
        loads[2 * c].wait()
        loads[2 * c + 1].wait()
        out_all[c] = total_of(keep_all[c], got_all[c])
        copy = pltpu.make_async_copy(out_all.at[c], out.at[c], sems.at[2, c])
        copy.start()
        stores.append(copy)
    for copy in stores:
        copy.wait()


def core_sum(place, keep, got, after):
    hbm = pl.BlockSpec(memory_space=pl.ANY)
    shape = keep.shape[1:]
    return call(
        core_kernel,
        sds(shape, BF16),
        [pl.BlockSpec(memory_space=pltpu.SMEM)] + [hbm] * (2 + len(after)),
        cost=0.05,
        out_specs=hbm,
        scratch_shapes=[pltpu.VMEM(shape, BF16)] * 3 + [pltpu.SemaphoreType.DMA((3, CHUNKS))],
    )(place, keep, got, *after)


def y_kernel(place_ref, keep, got, far, mine, away):
    x_bit = place_ref[0]
    for c in range(4):
        here, there = 4 * x_bit + c, 4 * (1 - x_bit) + c
        mine[c] = total_of(keep[0, here], got[0, here], far[here])
        away[c] = total_of(keep[0, there], got[0, there], far[there])


def x_kernel(place_ref, keep, got, *outs):
    for d in range(4):
        c = place_ref[1] ^ d
        outs[d][...] = total_of(keep[c], got[c])


def stack_kernel(place_ref, *refs):
    for d in range(4):
        refs[4][d] = refs[d][...]


def fuse(kernel, place, outs, ins, after=(), specs=None, out_specs=None, grid=None):
    vm = pl.BlockSpec(memory_space=pltpu.VMEM)
    count = 1 + len(ins)

    def body(*refs):
        kernel(*refs[:count], *refs[count + len(after) :])

    return call(
        body,
        tuple(sds(shape, BF16) for shape in outs),
        [pl.BlockSpec(memory_space=pltpu.SMEM)]
        + (specs or [vm] * len(ins))
        + [pl.BlockSpec(memory_space=pl.ANY)] * len(after),
        cost=0.05,
        out_specs=out_specs or (vm,) * len(outs),
        **({"grid": grid} if grid else {}),
    )(place, *ins, *after)


class Sum:
    def __init__(self, place, keep, send):
        self.place, self.shape = place, keep.shape[2:]
        self.parts = (keep, flip(send, "fsdp", 1))

    def core(self, *after):
        keep, got = self.parts
        away = core_sum(self.place, keep, got, after)
        self.parts = (keep, got, flip(away, "fsdp", 2))
        return away

    def y_specs(self):
        first = pl.BlockSpec((1, CHUNKS) + self.shape, lambda i: (0, 0, 0, 0))
        return [first, first, pl.BlockSpec(memory_space=pltpu.VMEM)]

    def y(self, *after):
        shape = (4,) + self.shape
        keep, send = fuse(
            y_kernel, self.place, [shape] * 2, self.parts, after, self.y_specs(), None, (1,)
        )
        self.parts = (keep, flip(send, "ctx", 1))
        return keep

    def x(self, *after):
        mine, *away = fuse(x_kernel, self.place, [self.shape] * 4, self.parts, after)
        self.parts = (mine, *(flip(away[d - 1], "ctx", 2 * d) for d in (1, 2, 3)))
        return mine

    def z(self, *after):
        n = lax.axis_size("ctx")
        (mine,) = fuse(add_kernel, self.place, [self.shape], self.parts, after)
        for b in range(3, n.bit_length() - 1):
            (mine,) = fuse(
                add_kernel, self.place, [self.shape], (mine, flip(mine, "ctx", 1 << b))
            )
        self.parts = (mine, *(flip(mine, "ctx", d) for d in (2, 4, 6)))
        return mine

    def stack(self, *after):
        (every,) = fuse(stack_kernel, self.place, [(4,) + self.shape], self.parts, after)
        self.parts = (every, flip(every, "ctx", 1))
        return every


def send_down(x, levels):
    n = lax.axis_size("ctx")
    return lax.ppermute(x, "ctx", [(i, i - 2 * levels) for i in range(2 * levels, n)])


def local(
    tokens,
    cotangent,
    attn_gain,
    w_query,
    w_key,
    w_value,
    w_out,
    mlp_gain,
    w_gate,
    w_up,
    w_down,
    seq_lengths,
    seq_starts,
):
    seqs, rows, dim = tokens.shape
    n = seqs * rows
    n_ctx = lax.axis_size("ctx")
    me = lax.axis_index("ctx")
    index = lax.axis_index("fsdp").reshape(1).astype(jnp.int32)
    fs = w_query.shape[0]
    cot = jnp.transpose(cotangent, (0, 2, 1))

    used = KV_HEADS * LANES + HEADS * HEAD_DIM + 2
    width = used - used % -LANES
    vm = pl.BlockSpec(memory_space=pltpu.VMEM)
    first = call(pack_kernel, sds((fs, width), BF16), [vm] * 5, cost=1.5, out_specs=vm)(
        w_query, w_key, w_value, attn_gain, mlp_gain
    )
    first_shards = gather_shards(first)
    places = me * rows + jnp.arange(rows, dtype=jnp.int32)
    positions = (places[None, :] - seq_starts[:, None]).astype(F32)
    frequency = THETA ** (-(2.0 * jnp.arange(HEAD_DIM // 2, dtype=F32)) / HEAD_DIM)
    angles = (positions[:, :, None] * frequency).reshape(n, HEAD_DIM // 2)
    cos, sin = jnp.cos(angles), jnp.sin(angles)
    cosines = jnp.concatenate([cos] * 4, axis=1)
    sines = jnp.concatenate([-sin, sin] * 2, axis=1)

    ff, fd = w_gate.shape[1], w_down.shape[0]
    hbm = pl.BlockSpec(memory_space=pl.ANY)
    tiles = seqs * KV_HEADS
    weights, normed, queries, kv, gain_two, x = call(
        qkv_kernel,
        (
            sds((dim, width), BF16),
            sds((n, dim), BF16),
            sds((tiles, GROUP * rows, LANES), BF16),
            sds((tiles, rows, LANES), BF16),
            sds((1, dim), F32),
            sds((n, dim), BF16),
        ),
        [pl.BlockSpec(memory_space=pltpu.SMEM)] + [vm] * 7,
        cost=4.0,
        out_specs=(vm,) * 6,
    )(index, jnp.transpose(tokens, (0, 2, 1)), *first_shards, cosines, sines)

    gu_own, do_own = call(
        rest_pack_kernel,
        (sds((fs, 2 * ff), BF16), sds((fd + fs, dim), BF16)),
        [vm] * 4,
        cost=3.0,
        out_specs=(vm, vm),
    )(w_gate, w_up, w_down.T, w_out)
    gu_shards = gather_shards(gu_own)
    do_shards = gather_shards(do_own)

    spans = [seq_starts.astype(jnp.int32), (seq_starts + seq_lengths).astype(jnp.int32)]

    def info_of(bases):
        return jnp.concatenate([me.reshape(1).astype(jnp.int32), bases.astype(jnp.int32)] + spans)

    x_bit = me % 2
    if n_ctx <= 8 and n_ctx % 2 == 0:
        levels = n_ctx // 2
        up = [(i, i + 2) for i in range(n_ctx - 2)]
        down = [(i + 2, i) for i in range(n_ctx - 2)]
        pieces = []
        piece = kv
        for k in range(levels):
            other = flip(piece, "ctx", 1)
            pair = (me // 2 - k) * 2
            bases = jnp.stack([pair + x_bit, pair + 1 - x_bit]) * rows
            bases = jnp.where(pair >= 0, bases, FAR)
            pieces.append((bases, piece[None], other[None]))
            if k + 1 < levels:
                piece = lax.ppermute(piece, "ctx", up)
        carry = None
        for k in range(levels - 1):
            bases, a, b = pieces[k]
            carry = attend(info_of(bases), queries, a, b, carry, k == 0)
        bases, a, b = pieces[-1]
        last_piece = (info_of(bases), queries, a, b, True)
    else:
        every = lax.all_gather(kv, "ctx", axis=0)
        info = info_of(jnp.arange(n_ctx, dtype=jnp.int32) * rows)
        carry = attend(info, queries, every[0::2], every[1::2], None, True)
        last_piece = (info, queries, every[:1], every[:1], False)

    result, d_mid, d_out, stats, keep_mlp, send_mlp = middle(
        index, x, cot, gain_two, carry[0], carry[1], gu_shards, do_shards, *last_piece
    )

    place = jnp.stack([me & 1, (me >> 1) & 3, index[0]]).astype(jnp.int32)
    mlp = Sum(place, keep_mlp, send_mlp)
    if n_ctx <= 8 and n_ctx % 2 == 0:
        dq, last = None, ()
        dkv, partials = [], []
        for k in reversed(range(levels)):
            bases, a, b = pieces[k]
            extra = partials[0][1:] if k < levels - 2 else ()
            dq, da, db, *both = attend_back(
                info_of(bases),
                queries,
                d_out,
                stats,
                a,
                b,
                dq,
                k == 0,
                last,
                extra,
            )
            if extra:
                dkv.append(send_down(both[0], partials.pop(0)[0]))
            partials.append((k, da[0], flip(db[0], "ctx", 1)))
            last = (mlp.core(dq),) if k == levels - 1 else ()
        while len(partials) > 1:
            far, near, other = partials.pop(0)
            (both,) = fuse(add_kernel, place, [near.shape], (near, other), (dq,))
            dkv.append(send_down(both, far))
            last = (both,)
        dkv = [partials[0][1], partials[0][2]] + dkv
        last = (mlp.y(*last),)
    else:
        dq, da, db = attend_back(
            info, queries, d_out, stats, every[0::2], every[1::2], None, True
        )
        partial = jnp.stack([da, db], axis=1).reshape((n_ctx,) + da.shape[1:])
        dkv = [lax.psum_scatter(partial, "ctx", scatter_dimension=0, tiled=False)]
        mlp.core(dq)
        last = (mlp.y(dq),)

    input_grad, keep_q, send_q = finish(
        index, x, normed, weights, cosines, sines, dq, dkv, d_mid, last
    )
    qkv = Sum(place, keep_q, send_q)
    step = mlp.x(keep_q)
    step = qkv.core(step)
    step = mlp.z(step)
    step = qkv.y(step)
    step = qkv.x(step)
    step = mlp.stack(step)
    step = qkv.z(step)
    step = qkv.stack(step)
    grad_gate, grad_up, grad_down, grad_out, gain_two_grad = own(
        own_kernel,
        place,
        [(fs, ff), (fs, ff), (dim, fd), (fs, dim), (1, fs)],
        mlp.parts,
        (dim, dim),
    )
    grad_down = grad_down.T
    kv_width = KV_HEADS * HEAD_DIM
    grad_query, grad_key, grad_value, gain_one_grad = own(
        own_q_kernel,
        place,
        [(fs, HEADS * HEAD_DIM), (fs, kv_width), (fs, kv_width), (1, fs)],
        qkv.parts,
        (fs, width),
        (grad_gate,),
    )
    grad_mlp_gain = gain_two_grad.reshape(fs)
    grad_attn_gain = gain_one_grad.reshape(fs)
    return (
        jnp.transpose(result, (0, 2, 1)),
        jnp.transpose(input_grad, (0, 2, 1)),
        grad_attn_gain,
        grad_query,
        grad_key,
        grad_value,
        grad_out,
        grad_mlp_gain,
        grad_gate,
        grad_up,
        grad_down,
    )


def solution(mesh):
    rows3 = P("fsdp", "ctx", None)
    mat = P("fsdp", None)
    vec = P("fsdp")
    return jax.shard_map(
        local,
        mesh=mesh,
        in_specs=(rows3, rows3, vec, mat, mat, mat, mat, vec, mat, mat, mat, vec, vec),
        out_specs=(rows3, rows3, vec, mat, mat, mat, mat, vec, mat, mat, mat),
        check_vma=False,
    )
```

```python
import functools
import math

import jax
import jax.numpy as jnp
from jax import lax
from jax.experimental import pallas as pl
from jax.experimental.pallas import tpu as pltpu
from jax.sharding import PartitionSpec as P

HEADS = 9
KV_HEADS = 3
HEAD_DIM = 64
GROUP = HEADS // KV_HEADS
LANES = 128
EPSILON = 1e-05
THETA = 100000.0
SCALE = HEAD_DIM ** (-0.5)
MASKED = -2e30
LOWEST = -1e30
FAR = 1 << 29
CHUNKS = 8
SLOTS = (0, 2, 1, 3)
TOP = 40
BF16 = jnp.bfloat16
F32 = jnp.float32
NN = (((1,), (0,)), ((), ()))
NT = (((1,), (1,)), ((), ()))
TN = (((0,), (0,)), ((), ()))
VMEM_LIMIT = 64 * 1024 * 1024 - 65536
PER_US = 1.0e9


def dot(a, b, dims=NN):
    return lax.dot_general(a, b, dims, preferred_element_type=F32)


def call(kernel, out_shape, in_specs=None, cost=1.0, **kwargs):
    return pl.pallas_call(
        kernel,
        out_shape=out_shape,
        in_specs=in_specs,
        compiler_params=pltpu.CompilerParams(vmem_limit_bytes=VMEM_LIMIT),
        cost_estimate=pl.CostEstimate(
            flops=int(cost * PER_US), bytes_accessed=0, transcendentals=0
        ),
        **kwargs,
    )


def sds(shape, dtype):
    return jax.ShapeDtypeStruct(shape, dtype)


def lane_of(shape):
    return lax.broadcasted_iota(jnp.int32, shape, 1)


def swap_halves(tile):
    lane = lane_of(tile.shape) % HEAD_DIM
    return jnp.where(
        lane < HEAD_DIM // 2, pltpu.roll(tile, LANES - 32, 1), pltpu.roll(tile, 32, 1)
    )


def half_roll(tile):
    return pltpu.roll(tile, HEAD_DIM, 1)


def assemble(target, index, shards, rows):
    for code, ref in zip((0, 1, 2, 3), shards):
        start = pl.multiple_of((index ^ code) * rows, 16)
        target[pl.ds(start, rows), :] = ref[...]


def inverse_rms(rows):
    return lax.rsqrt(jnp.mean(rows * rows, axis=-1, keepdims=True) + EPSILON)


def qkv_kernel(index_ref, x_ref, w0, w1, w2, w3, cos_ref, sin_ref, w_ref, normed_ref, q_ref, kv_ref, two_ref, rows_ref):
    assemble(w_ref, index_ref[0], (w0, w1, w2, w3), w0.shape[0])
    width = w_ref.shape[1]
    gains = jnp.transpose(w_ref[:, width - LANES :].astype(F32))
    count = x_ref.shape[2]
    for r in range(x_ref.shape[0]):
        turned = jnp.transpose(x_ref[r].astype(F32))
        rows_ref[r * count : (r + 1) * count, :] = turned.astype(BF16)
    x = rows_ref[...].astype(F32)
    normed = (x * inverse_rms(x) * gains[HEAD_DIM : HEAD_DIM + 1, :]).astype(BF16)
    normed_ref[...] = normed
    two_ref[...] = gains[HEAD_DIM + 1 : HEAD_DIM + 2, :]
    cosines, sines = cos_ref[...], sin_ref[...]
    lane = lane_of(cosines.shape)
    low = lane < HEAD_DIM
    cos_kv = jnp.where(low, cosines, 1.0)
    sin_kv = jnp.where(low, sines, 0.0)
    rows = kv_ref.shape[1]
    seqs = x.shape[0] // rows
    for g in range(KV_HEADS):
        tile = dot(normed, w_ref[:, g * LANES : (g + 1) * LANES])
        turned = (tile * cos_kv + swap_halves(tile) * sin_kv).astype(BF16)
        for r in range(seqs):
            kv_ref[r * KV_HEADS + g] = turned[r * rows : (r + 1) * rows]
    first = KV_HEADS * LANES
    lin = dot(normed, w_ref[:, first:])
    for p in range((HEADS + 1) // 2):
        tile = lin[:, p * LANES : (p + 1) * LANES]
        turned = (tile * cosines + swap_halves(tile) * sines) * SCALE
        for h in (2 * p, 2 * p + 1):
            if h < HEADS:
                own = turned if h % 2 == 0 else half_roll(turned)
                own = jnp.where(low, own, 0.0).astype(BF16)
                g, i = divmod(h, GROUP)
                for r in range(seqs):
                    q_ref[r * KV_HEADS + g, i * rows : (i + 1) * rows] = own[
                        r * rows : (r + 1) * rows
                    ]


def pair_places(info_ref, step, rows, axis):
    shape = (1, 2 * rows) if axis == 1 else (2 * rows, 1)
    at = lax.broadcasted_iota(jnp.int32, shape, axis)
    first, second = info_ref[1 + 2 * step], info_ref[2 + 2 * step]
    return jnp.where(at < rows, first + at, second + at - rows)


def query_places(info_ref, rows, axis):
    total = GROUP * rows
    shape = (1, total) if axis == 1 else (total, 1)
    at = lax.broadcasted_iota(jnp.int32, shape, axis)
    return info_ref[0] * rows + at % rows


def seen_of(key_places, q_places, start, end, diagonal):
    key_in = (key_places >= start) & (key_places < end)
    query_in = (q_places >= start) & (q_places < end)
    seen = jnp.where(key_in, key_places, FAR) <= jnp.where(query_in, q_places, -1)
    if diagonal:
        seen = seen | (key_places == q_places)
    return seen


def row_active(info_ref, step, rows, start, end):
    own = info_ref[0] * rows
    first, second = info_ref[1 + 2 * step], info_ref[2 + 2 * step]
    keys_in = ((first < end) & (first + rows > start)) | ((second < end) & (second + rows > start))
    return (own < end) & (own + rows > start) & keys_in & (jnp.minimum(first, second) <= own)


def attend_rows(
    info_ref, step, steps, diagonal, q_ref, a_ref, b_ref, max_in, sum_in, max_ref, sum_ref
):
    rows = a_ref.shape[2]
    seqs = q_ref.shape[0] // KV_HEADS
    spans = 1 + 2 * steps

    def one_seq(r, unused):
        start = info_ref[spans + r]
        end = info_ref[spans + seqs + r]

        def one_row():
            seen = seen_of(
                pair_places(info_ref, step, rows, 1),
                query_places(info_ref, rows, 0),
                start,
                end,
                diagonal,
            )
            for g in range(KV_HEADS):
                rg = r * KV_HEADS + g
                kv = jnp.concatenate([a_ref[0, rg], b_ref[0, rg]], axis=0)
                scores = jnp.where(seen, dot(q_ref[rg], kv, NT), MASKED)
                old = max_in[rg]
                new = jnp.maximum(old, jnp.max(scores, axis=-1, keepdims=True))
                weights = jnp.exp(scores - jnp.concatenate([new, new], axis=1)).astype(BF16)
                ones = jnp.where(lane_of(kv.shape) < HEAD_DIM, jnp.ones_like(kv), kv)
                sum_ref[rg] = sum_in[rg] * jnp.exp(old - new) + dot(weights, ones)
                max_ref[rg] = new

        def keep_row():
            for g in range(KV_HEADS):
                max_ref[r * KV_HEADS + g] = max_in[r * KV_HEADS + g]
                sum_ref[r * KV_HEADS + g] = sum_in[r * KV_HEADS + g]

        if diagonal:
            one_row()
        else:
            active = row_active(info_ref, step, rows, start, end)
            pl.when(active)(one_row)
            if max_in is not max_ref:
                pl.when(jnp.logical_not(active))(keep_row)
        return unused

    lax.fori_loop(0, seqs, one_seq, 0)


def attend_kernel(steps, diagonal, fresh, info_ref, q_ref, a_ref, b_ref, *refs):
    if fresh:
        max_ref, sum_ref = refs
    else:
        max_in, sum_in, max_ref, sum_ref = refs
    step = pl.program_id(0)

    @pl.when(step == 0)
    def _():
        if fresh:
            max_ref[...] = jnp.full_like(max_ref, LOWEST)
            sum_ref[...] = jnp.zeros_like(sum_ref)
        else:
            max_ref[...] = max_in[...]
            sum_ref[...] = sum_in[...]

    attend_rows(
        info_ref, step, steps, diagonal, q_ref, a_ref, b_ref, max_ref, sum_ref, max_ref, sum_ref
    )


def attend(info, queries, a, b, carry, diagonal):
    steps = a.shape[0]
    tiles, total, _ = queries.shape
    rows = a.shape[2]
    whole = pl.BlockSpec((tiles, total, LANES), lambda i: (0, 0, 0))
    piece = pl.BlockSpec((1, tiles, rows, LANES), lambda i: (i, 0, 0, 0))
    return call(
        functools.partial(attend_kernel, steps, diagonal, carry is None),
        (sds((tiles, total, LANES), F32),) * 2,
        [pl.BlockSpec(memory_space=pltpu.SMEM), whole, piece, piece]
        + ([] if carry is None else [whole] * 2),
        cost=10.0 * steps,
        out_specs=(whole, whole),
        grid=(steps,),
    )(info, queries, a, b, *(carry or ()))


def attend_back_kernel(
    steps, diagonal, fresh, extra, info_ref, q_ref, d_ref, stat_ref, a_ref, b_ref, *refs
):
    if extra:
        refs[-1][...] = total_of(refs[-6][...], refs[-5][...])
        dq_ref, da_ref, db_ref = refs[-4:-1]
    else:
        dq_ref, da_ref, db_ref = refs[-3:]
    dq_in = refs[0]
    step = pl.program_id(0)
    rows = a_ref.shape[2]
    seqs = q_ref.shape[0] // KV_HEADS
    spans = 1 + 2 * steps

    @pl.when(step == 0)
    def _():
        dq_ref[...] = jnp.zeros_like(dq_ref) if fresh else dq_in[...]

    def one_seq(r, unused):
        start = info_ref[spans + r]
        end = info_ref[spans + seqs + r]

        def one_row():
            seen = seen_of(
                pair_places(info_ref, step, rows, 0),
                query_places(info_ref, rows, 1),
                start,
                end,
                diagonal,
            )
            for g in range(KV_HEADS):
                rg = r * KV_HEADS + g
                kv = jnp.concatenate([a_ref[0, rg], b_ref[0, rg]], axis=0)
                q, d = q_ref[rg], d_ref[rg]
                log_sum = stat_ref[rg, 0:1, :]
                delta = stat_ref[rg, 1:2, :]
                scores = jnp.where(seen, dot(kv, q, NT), MASKED)
                probs = jnp.exp(scores - log_sum)
                d_scores = (probs * (dot(kv, d, NT) - delta)).astype(BF16)
                grad = (dot(d_scores, q) + dot(probs.astype(BF16), d)).astype(BF16)
                da_ref[0, rg] = grad[:rows]
                db_ref[0, rg] = grad[rows:]
                dq_ref[rg] = dq_ref[rg] + dot(d_scores, kv, TN)

        if diagonal:
            one_row()
        else:
            active = row_active(info_ref, step, rows, start, end)
            pl.when(active)(one_row)

            @pl.when(jnp.logical_not(active))
            def _():
                for g in range(KV_HEADS):
                    rg = r * KV_HEADS + g
                    da_ref[0, rg] = jnp.zeros((rows, LANES), BF16)
                    db_ref[0, rg] = jnp.zeros((rows, LANES), BF16)

        return unused

    lax.fori_loop(0, seqs, one_seq, 0)


def attend_back(info, queries, d_out, stats, a, b, carry, diagonal, after=(), extra=()):
    steps = a.shape[0]
    tiles, total, _ = queries.shape
    rows = a.shape[2]
    whole = pl.BlockSpec((tiles, total, LANES), lambda i: (0, 0, 0))
    stat = pl.BlockSpec(stats.shape, lambda i: (0, 0, 0))
    one = pl.BlockSpec(a.shape[1:], lambda i: (0, 0, 0))
    piece = pl.BlockSpec((1, tiles, rows, LANES), lambda i: (i, 0, 0, 0))
    return call(
        functools.partial(attend_back_kernel, steps, diagonal, carry is None, bool(extra)),
        (sds((tiles, total, LANES), F32), sds(a.shape, BF16), sds(b.shape, BF16))
        + ((sds(a.shape[1:], BF16),) if extra else ()),
        [pl.BlockSpec(memory_space=pltpu.SMEM), whole, whole, stat, piece, piece]
        + ([] if carry is None else [whole])
        + [pl.BlockSpec(memory_space=pl.ANY)] * len(after)
        + [one] * len(extra),
        cost=0.05,
        out_specs=(whole, piece, piece) + ((one,) if extra else ()),
        grid=(steps,),
    )(info, queries, d_out, stats, a, b, *(() if carry is None else (carry,)), *after, *extra)


def middle_kernel(
    fused,
    index_ref,
    info_ref,
    x_ref,
    cot_in,
    gain_ref,
    max_ref,
    sum_ref,
    q_ref,
    a_ref,
    b_ref,
    gu0,
    gu1,
    gu2,
    gu3,
    do0,
    do1,
    do2,
    do3,
    turned_ref,
    d_mid_ref,
    d_ref,
    stat_ref,
    keep_ref,
    send_ref,
    out_ref,
    w_gu,
    w_down,
    w_out,
    att_ref,
    n2_ref,
    dn2_ref,
    g_gu,
    g_down,
    g_out,
    slot_ref,
    chunk_ref,
    stage_ref,
    max_out,
    sum_out,
    cot_ref,
    in_sems,
    out_sems,
):
    index = index_ref[0]
    dim = x_ref.shape[1]
    ff = w_down.shape[0]
    fd, fs = ff // 4, dim // 4
    loads = []
    for code, gu, do in zip((0, 1, 2, 3), (gu0, gu1, gu2, gu3), (do0, do1, do2, do3)):
        shard = index ^ code
        down_at = pl.ds(pl.multiple_of(shard * fd, 16), fd)
        at = pl.ds(pl.multiple_of(shard * fs, 16), fs)
        for source, target in (
            (do.at[pl.ds(fd, fs)], w_out.at[at]),
            (gu, w_gu.at[at]),
            (do.at[pl.ds(0, fd)], w_down.at[down_at]),
        ):
            loads.append(pltpu.make_async_copy(source, target, in_sems.at[len(loads)]))
    for copy in loads:
        copy.start()
    if fused:
        attend_rows(
            info_ref, 0, 1, False, q_ref, a_ref, b_ref, max_ref, sum_ref, max_out, sum_out
        )
        max_ref, sum_ref = max_out, sum_out
    tiles, total, _ = max_ref.shape
    seqs = tiles // KV_HEADS
    rows = total // GROUP
    low = lane_of((total, LANES)) < HEAD_DIM
    low_rows = low[:rows]
    outs = []
    for rg in range(tiles):
        sums = sum_ref[rg]
        turned = half_roll(sums)
        both = jnp.where(low, sums, turned)
        log_sum = max_ref[rg] + jnp.log(both)
        stat_ref[rg, 0:1, :] = jnp.transpose(log_sum)[0:1, :]
        normal = jnp.where(low, 0.0, sums / both)
        sum_ref_row = normal
        outs.append(sum_ref_row)
    for r in range(seqs):
        for p in range((HEADS + 1) // 2):
            g, i = divmod(2 * p, GROUP)
            tile = half_roll(outs[r * KV_HEADS + g][i * rows : (i + 1) * rows])
            if 2 * p + 1 < HEADS:
                g, i = divmod(2 * p + 1, GROUP)
                tile = jnp.where(
                    low_rows, tile, outs[r * KV_HEADS + g][i * rows : (i + 1) * rows]
                )
                att_ref[r * rows : (r + 1) * rows, p * LANES : (p + 1) * LANES] = tile.astype(BF16)
            else:
                att_ref[r * rows : (r + 1) * rows, p * LANES :] = tile[:, :HEAD_DIM].astype(BF16)
    for r in range(seqs):
        turned = jnp.transpose(cot_in[r].astype(F32))
        cot_ref[r * rows : (r + 1) * rows, :] = turned.astype(BF16)
    for copy in loads:
        copy.wait()
    att = att_ref[...]
    cot = cot_ref[...]
    mid = x_ref[...].astype(F32) + dot(att, w_out[...])
    inv = inverse_rms(mid)
    gain = gain_ref[...]
    n2 = (mid * inv * gain).astype(BF16)
    n2_ref[...] = n2
    out_ref[...] = mid
    dn2_ref[...] = jnp.zeros_like(dn2_ref)
    width = ff // 2

    def ff_step(i, carry):
        at = i * width
        cols, cols_up = pl.ds(at, width), pl.ds(at + ff, width)
        n2 = n2_ref[...]
        w_g, w_u, w_d = w_gu[:, cols], w_gu[:, cols_up], w_down[cols, :]
        gate = dot(n2, w_g)
        up = dot(n2, w_u)
        sig = 1.0 / (1.0 + jnp.exp(-gate))
        silu = gate * sig
        hidden = (silu * up).astype(BF16)
        out_ref[...] += dot(hidden, w_d)
        d_hidden = dot(cot_ref[...], w_d, NT)
        d_gate = (d_hidden * up * sig * (1.0 + gate * (1.0 - sig))).astype(BF16)
        d_up = (d_hidden * silu).astype(BF16)
        g_down[cols, :] = dot(hidden, cot_ref[...], TN)
        g_gu[:, cols] = dot(n2, d_gate, TN).astype(BF16)
        g_gu[:, cols_up] = dot(n2, d_up, TN).astype(BF16)
        dn2_ref[...] += dot(d_gate, w_g, NT) + dot(d_up, w_u, NT)
        return carry

    ff_step(0, 0)
    ff_step(1, 0)
    part = dim // CHUNKS
    quarter = 2 * ff // CHUNKS
    stores = []
    for slot in (2, 3, 0, 1):
        to = keep_ref if slot < 2 else send_ref
        at = pl.ds(pl.multiple_of((index ^ SLOTS[slot]) * fs, 16), fs)
        for c in range(CHUNKS):
            copy = pltpu.make_async_copy(
                g_gu.at[at, pl.ds(c * quarter, quarter)],
                to.at[slot % 2, c, pl.ds(0, fs)],
                out_sems.at[len(stores)],
            )
            copy.start()
            stores.append(copy)
    for r in range(seqs):
        turned_ref[r] = jnp.transpose(out_ref[r * rows : (r + 1) * rows, :])
    dn2 = dn2_ref[...]
    scaled = dn2 * gain
    gain_grad = jnp.sum(dn2 * mid * inv, axis=0, keepdims=True)
    d_mid = (
        cot.astype(F32)
        + inv * scaled
        - mid * (inv * inv * inv) * jnp.mean(scaled * mid, axis=-1, keepdims=True)
    )
    d_mid_ref[...] = d_mid
    d_low = d_mid.astype(BF16)
    g_out[...] = dot(att, d_low, TN)
    d_att = dot(d_low, w_out[...], NT)
    for r in range(seqs):
        for p in range((HEADS + 1) // 2):
            stop = min((p + 1) * LANES, dim)
            tile = d_att[r * rows : (r + 1) * rows, p * LANES : stop]
            if stop - p * LANES < LANES:
                tile = jnp.concatenate([tile, jnp.zeros_like(tile)], axis=1)
            for h in (2 * p, 2 * p + 1):
                if h < HEADS:
                    own = half_roll(tile) if h % 2 == 0 else tile
                    own = jnp.where(low_rows, 0.0, own).astype(BF16)
                    g, i = divmod(h, GROUP)
                    d_ref[r * KV_HEADS + g, i * rows : (i + 1) * rows] = own
    for rg in range(tiles):
        prod = d_ref[rg].astype(F32) * outs[rg]
        stat_ref[rg, 1:2, :] = jnp.sum(jnp.transpose(prod), axis=0, keepdims=True)
    for slot in (2, 3, 0, 1):
        shard = index ^ SLOTS[slot]
        to = keep_ref if slot < 2 else send_ref
        at = pl.ds(pl.multiple_of(shard * fs, 16), fs)
        slot_ref[0:fd, :] = g_down[pl.ds(pl.multiple_of(shard * fd, 16), fd), :]
        slot_ref[fd : fd + fs, :] = g_out[at, :]
        slot_ref[fd + fs :, :] = jnp.broadcast_to(gain_grad, (dim - fd - fs, dim))
        for c in range(CHUNKS):
            chunk_ref[:part, :] = slot_ref[c * part : (c + 1) * part, :quarter]
            top = slot_ref[c * part : c * part + TOP, quarter:]
            rest = slot_ref[c * part + TOP : (c + 1) * part, quarter:]
            fill = jnp.zeros((2 * TOP - part, dim - quarter), F32)
            chunk_ref[part:, :] = jnp.concatenate(
                [top, jnp.concatenate([rest, fill], axis=0)], axis=1
            )
            stage_ref[slot, c] = chunk_ref[...].astype(BF16)
        copy = pltpu.make_async_copy(
            stage_ref.at[slot],
            to.at[slot % 2, pl.ds(0, CHUNKS), pl.ds(fs, part + TOP)],
            out_sems.at[len(stores)],
        )
        copy.start()
        stores.append(copy)
    for copy in stores:
        copy.wait()


def middle(index, x, cot, gain, top, sums, gu, do, info, queries, a, b, fused):
    n, dim = x.shape
    tiles, total, _ = top.shape
    ff2 = gu[0].shape[1]
    ff = ff2 // 2
    chunk = (dim // 4 + dim // CHUNKS + TOP, ff2 // CHUNKS)
    small = (dim // CHUNKS + TOP, ff2 // CHUNKS)
    pair = sds((2, CHUNKS) + chunk, BF16)
    vm = pl.BlockSpec(memory_space=pltpu.VMEM)
    sm = pl.BlockSpec(memory_space=pltpu.SMEM)
    hbm = pl.BlockSpec(memory_space=pl.ANY)
    return call(
        functools.partial(middle_kernel, fused),
        (
            sds((tiles // KV_HEADS, dim, total // GROUP), F32),
            sds((n, dim), F32),
            sds((tiles, total, LANES), BF16),
            sds((tiles, 8, total), F32),
            pair,
            pair,
        ),
        [sm, sm] + [vm] * 8 + [hbm] * 8,
        cost=20.0,
        out_specs=(vm,) * 4 + (hbm,) * 2,
        scratch_shapes=[
            pltpu.VMEM((n, dim), F32),
            pltpu.VMEM((dim, ff2), BF16),
            pltpu.VMEM((ff, dim), BF16),
            pltpu.VMEM((dim, dim), BF16),
            pltpu.VMEM((n, dim), BF16),
            pltpu.VMEM((n, dim), BF16),
            pltpu.VMEM((n, dim), F32),
            pltpu.VMEM((dim, ff2), BF16),
            pltpu.VMEM((ff, dim), F32),
            pltpu.VMEM((dim, dim), F32),
            pltpu.VMEM((dim, dim), F32),
            pltpu.VMEM(small, F32),
            pltpu.VMEM((4, CHUNKS) + small, BF16),
            pltpu.VMEM((tiles, total, LANES), F32),
            pltpu.VMEM((tiles, total, LANES), F32),
            pltpu.VMEM((n, dim), BF16),
            pltpu.SemaphoreType.DMA((12,)),
            pltpu.SemaphoreType.DMA((4 * CHUNKS + 4,)),
        ],
    )(index, info, x, cot, gain, top, sums, queries, a, b, *gu, *do)


def end_kernel(
    index_ref,
    x_ref,
    normed_ref,
    w_ref,
    cos_ref,
    sin_ref,
    dq_ref,
    d_mid_ref,
    *refs,
    parts,
):
    dkv_refs = refs[:parts]
    grad_ref, keep, send, lin_ref, g_ref = refs[-5:]
    index = index_ref[0]
    width = w_ref.shape[1]
    tiles, rows, _ = dkv_refs[0].shape
    seqs = tiles // KV_HEADS
    low = lane_of((rows, LANES)) < HEAD_DIM
    for r in range(seqs):
        at = slice(r * rows, (r + 1) * rows)
        cosines, sines = cos_ref[at, :], sin_ref[at, :]
        cos_kv = jnp.where(low, cosines, 1.0)
        sin_kv = jnp.where(low, sines, 0.0)
        for g in range(KV_HEADS):
            tile = dkv_refs[0][r * KV_HEADS + g].astype(F32)
            for ref in dkv_refs[1:]:
                tile = tile + ref[r * KV_HEADS + g].astype(F32)
            back = tile * cos_kv - swap_halves(tile) * sin_kv
            lin_ref[at, g * LANES : (g + 1) * LANES] = back.astype(BF16)
        first = KV_HEADS * LANES
        for p in range((HEADS + 1) // 2):
            backs = []
            for h in (2 * p, 2 * p + 1):
                if h < HEADS:
                    g, i = divmod(h, GROUP)
                    tile = dq_ref[r * KV_HEADS + g, i * rows : (i + 1) * rows]
                    backs.append((tile * cosines - swap_halves(tile) * sines) * SCALE)
                else:
                    backs.append(jnp.zeros((rows, LANES), F32))
            tile = jnp.where(low, backs[0], half_roll(backs[1]))
            lin_ref[at, first + p * LANES : first + (p + 1) * LANES] = tile.astype(BF16)
    lin = lin_ref[...]
    g_ref[...] = dot(normed_ref[...], lin, TN)
    d_normed = dot(lin, w_ref[...], NT)
    gains = jnp.transpose(w_ref[:, width - LANES :].astype(F32))
    gain = gains[HEAD_DIM : HEAD_DIM + 1, :]
    x = x_ref[...].astype(F32)
    inv = inverse_rms(x)
    scaled = d_normed * gain
    grad = (
        d_mid_ref[...]
        + inv * scaled
        - x * (inv * inv * inv) * jnp.mean(scaled * x, axis=-1, keepdims=True)
    )
    for r in range(seqs):
        grad_ref[r] = jnp.transpose(grad[r * rows : (r + 1) * rows, :])
    gain_grad = jnp.sum(d_normed * x * inv, axis=0, keepdims=True)
    dim = x.shape[1]
    fs = dim // 4
    for slot in range(4):
        at = pl.ds(pl.multiple_of((index ^ SLOTS[slot]) * fs, 16), fs)
        to = keep if slot < 2 else send
        for c in range(CHUNKS):
            tile = g_ref[at, c * LANES : (c + 1) * LANES]
            if c == CHUNKS - 1:
                pad = jnp.concatenate(
                    [gain_grad[:, k * HEAD_DIM : (k + 1) * HEAD_DIM] for k in range(HEADS)]
                    + [jnp.zeros((fs - HEADS, HEAD_DIM), F32)],
                    axis=0,
                )
                tile = jnp.concatenate([tile[:, :HEAD_DIM], pad], axis=1)
            to[slot % 2, c] = tile.astype(BF16)


def finish(index, x, normed, w, cosines, sines, dq, dkv, d_mid, after):
    n, dim = x.shape
    width = w.shape[1]
    vm = pl.BlockSpec(memory_space=pltpu.VMEM)
    pair = sds((2, CHUNKS, dim // 4, width // CHUNKS), BF16)
    tiles = dkv[0].shape[0]
    return call(
        functools.partial(end_kernel, parts=len(dkv)),
        (sds((tiles // KV_HEADS, dim, dkv[0].shape[1]), F32), pair, pair),
        [pl.BlockSpec(memory_space=pltpu.SMEM)] + [vm] * (7 + len(dkv))
        + [pl.BlockSpec(memory_space=pl.ANY)] * len(after),
        cost=0.05,
        out_specs=(vm,) * 3,
        scratch_shapes=[pltpu.VMEM((n, width), BF16), pltpu.VMEM((dim, width), F32)],
    )(index, x, normed, w, cosines, sines, dq, d_mid, *dkv, *after)


def both_halves(place_ref, parts, d):
    near, far = parts[0][d].astype(F32), parts[1][d].astype(F32)
    flag = place_ref[0] == 0
    return place_ref[1] ^ d, jnp.where(flag, near, far), jnp.where(flag, far, near)


def own_gain(place_ref, row, out_ref):
    size = out_ref.shape[1]
    rows = jnp.broadcast_to(row, (8, row.shape[1]))
    fill = -row.shape[1] % LANES
    rows = jnp.concatenate([rows, jnp.zeros((8, fill), F32)], axis=1)
    turned = pltpu.roll(rows, rows.shape[1] - place_ref[2] * size, 1)
    out_ref[...] = turned[0:1, :size]


def own_kernel(place_ref, *refs):
    parts = refs[:-6]
    gate_ref, up_ref, down_ref, out_ref, gain_ref, all_ref = refs[-6:]
    own_body(place_ref, parts, gate_ref, up_ref, down_ref, out_ref, gain_ref, all_ref)


def own_body(place_ref, parts, gate_ref, up_ref, down_ref, out_ref, gain_ref, all_ref):
    cols = parts[0].shape[-1]
    fs, dim = out_ref.shape
    fd = down_ref.shape[1]
    part = dim // CHUNKS
    width = dim - cols
    for d in range(4):
        quarter, first, second = both_halves(place_ref, parts, d)
        at = pl.ds(pl.multiple_of(quarter * cols, LANES), cols)
        gate_ref[:, at] = first[:fs]
        up_ref[:, at] = second[:fs]
        for c, chunk in ((quarter, first), (4 + quarter, second)):
            start = c * part
            all_ref[pl.ds(pl.multiple_of(start, 8), part), :cols] = chunk[fs : fs + part]
            right = chunk[fs + part :]
            all_ref[pl.ds(pl.multiple_of(start, 8), TOP), cols:] = right[:, :width]
            all_ref[pl.ds(pl.multiple_of(start + TOP, 8), part - TOP), cols:] = right[
                : part - TOP, width:
            ]
    down_ref[...] = jnp.transpose(all_ref[:fd, :])
    out_ref[...] = all_ref[fd : fd + fs, :]
    own_gain(place_ref, all_ref[fd + fs : fd + fs + 1, :], gain_ref)


def own_q_kernel(place_ref, *refs):
    parts = refs[:2]
    query_ref, key_ref, value_ref, gain_ref, all_ref = refs[-5:]
    for d in range(4):
        quarter, first, second = both_halves(place_ref, parts, d)
        all_ref[:, pl.ds(pl.multiple_of(quarter * LANES, LANES), LANES)] = first
        all_ref[:, pl.ds(pl.multiple_of((4 + quarter) * LANES, LANES), LANES)] = second
    first = KV_HEADS * LANES
    for g in range(KV_HEADS):
        to = slice(g * HEAD_DIM, (g + 1) * HEAD_DIM)
        key_ref[:, to] = all_ref[:, g * LANES : g * LANES + HEAD_DIM]
        value_ref[:, to] = all_ref[:, g * LANES + HEAD_DIM : (g + 1) * LANES]
    query_ref[...] = all_ref[:, first : first + HEADS * HEAD_DIM]
    start = all_ref.shape[1] - HEAD_DIM
    row = jnp.concatenate([all_ref[k : k + 1, start:] for k in range(HEADS)], axis=1)
    own_gain(place_ref, row, gain_ref)


def own(kernel, place, outs, parts, scratch, after=()):
    vm = pl.BlockSpec(memory_space=pltpu.VMEM)
    return call(
        kernel,
        tuple(sds(shape, F32) for shape in outs),
        [pl.BlockSpec(memory_space=pltpu.SMEM)]
        + [vm] * len(parts)
        + [pl.BlockSpec(memory_space=pl.ANY)] * len(after),
        cost=0.05,
        out_specs=(vm,) * len(outs),
        scratch_shapes=[pltpu.VMEM(scratch, F32)],
    )(place, *parts, *after)


def pack_kernel(q_ref, k_ref, v_ref, one_ref, two_ref, out_ref):
    for g in range(KV_HEADS):
        at = slice(g * HEAD_DIM, (g + 1) * HEAD_DIM)
        out_ref[:, g * LANES : g * LANES + HEAD_DIM] = k_ref[:, at]
        out_ref[:, g * LANES + HEAD_DIM : (g + 1) * LANES] = v_ref[:, at]
    first = KV_HEADS * LANES
    full = HEADS * HEAD_DIM
    out_ref[:, first : first + full] = q_ref[...]
    fs = q_ref.shape[0]
    row = lax.broadcasted_iota(jnp.int32, (LANES, fs), 0)
    gains = jnp.where(row == HEAD_DIM, one_ref[...].astype(F32)[None, :], 0.0)
    gains = jnp.where(row == HEAD_DIM + 1, two_ref[...].astype(F32)[None, :], gains)
    out_ref[:, first + full :] = jnp.transpose(gains)[:, HEAD_DIM:].astype(BF16)


def rest_pack_kernel(gate_ref, up_ref, down_ref, w_ref, gu_ref, do_ref):
    ff = gate_ref.shape[1]
    gu_ref[:, :ff] = gate_ref[...]
    gu_ref[:, ff:] = up_ref[...]
    fd = down_ref.shape[1]
    do_ref[:fd, :] = jnp.transpose(down_ref[...].astype(F32)).astype(BF16)
    do_ref[fd:, :] = w_ref[...]


def flip(x, axis, mask):
    n = lax.axis_size(axis)
    return lax.ppermute(x, axis, [(i, i ^ mask) for i in range(n)])


def gather_shards(own):
    across = flip(own, "fsdp", 2)
    return own, flip(own, "fsdp", 1), across, flip(across, "fsdp", 1)


def add(a, b):
    return (a.astype(F32) + b.astype(F32)).astype(BF16)


def total_of(*parts):
    total = parts[0].astype(F32)
    for part in parts[1:]:
        total = total + part.astype(F32)
    return total.astype(BF16)


def add_kernel(place_ref, *refs):
    refs[-1][...] = total_of(*(ref[...] for ref in refs[:-1]))


def core_kernel(place_ref, keep, got, *refs):
    out, keep_all, got_all, out_all, sems = refs[-5:]
    loads = []
    for c in range(CHUNKS):
        for i, (source, target) in enumerate(((keep, keep_all), (got, got_all))):
            copy = pltpu.make_async_copy(source.at[1, c], target.at[c], sems.at[i, c])
            copy.start()
            loads.append(copy)
    stores = []
    for c in range(CHUNKS):
        loads[2 * c].wait()
        loads[2 * c + 1].wait()
        out_all[c] = total_of(keep_all[c], got_all[c])
        copy = pltpu.make_async_copy(out_all.at[c], out.at[c], sems.at[2, c])
        copy.start()
        stores.append(copy)
    for copy in stores:
        copy.wait()


def core_sum(place, keep, got, after):
    hbm = pl.BlockSpec(memory_space=pl.ANY)
    shape = keep.shape[1:]
    return call(
        core_kernel,
        sds(shape, BF16),
        [pl.BlockSpec(memory_space=pltpu.SMEM)] + [hbm] * (2 + len(after)),
        cost=0.05,
        out_specs=hbm,
        scratch_shapes=[pltpu.VMEM(shape, BF16)] * 3 + [pltpu.SemaphoreType.DMA((3, CHUNKS))],
    )(place, keep, got, *after)


def y_kernel(place_ref, keep, got, far, mine, away):
    x_bit = place_ref[0]
    for c in range(4):
        here, there = 4 * x_bit + c, 4 * (1 - x_bit) + c
        mine[c] = total_of(keep[0, here], got[0, here], far[here])
        away[c] = total_of(keep[0, there], got[0, there], far[there])


def x_kernel(place_ref, keep, got, *outs):
    for d in range(4):
        c = place_ref[1] ^ d
        outs[d][...] = total_of(keep[c], got[c])


def stack_kernel(place_ref, *refs):
    for d in range(4):
        refs[4][d] = refs[d][...]


def fuse(kernel, place, outs, ins, after=(), specs=None, out_specs=None, grid=None):
    vm = pl.BlockSpec(memory_space=pltpu.VMEM)
    count = 1 + len(ins)

    def body(*refs):
        kernel(*refs[:count], *refs[count + len(after) :])

    return call(
        body,
        tuple(sds(shape, BF16) for shape in outs),
        [pl.BlockSpec(memory_space=pltpu.SMEM)]
        + (specs or [vm] * len(ins))
        + [pl.BlockSpec(memory_space=pl.ANY)] * len(after),
        cost=0.05,
        out_specs=out_specs or (vm,) * len(outs),
        **({"grid": grid} if grid else {}),
    )(place, *ins, *after)


class Sum:
    def __init__(self, place, keep, send):
        self.place, self.shape = place, keep.shape[2:]
        self.parts = (keep, flip(send, "fsdp", 1))

    def core(self, *after):
        keep, got = self.parts
        away = core_sum(self.place, keep, got, after)
        self.parts = (keep, got, flip(away, "fsdp", 2))
        return away

    def y_specs(self):
        first = pl.BlockSpec((1, CHUNKS) + self.shape, lambda i: (0, 0, 0, 0))
        return [first, first, pl.BlockSpec(memory_space=pltpu.VMEM)]

    def y(self, *after):
        shape = (4,) + self.shape
        keep, send = fuse(
            y_kernel, self.place, [shape] * 2, self.parts, after, self.y_specs(), None, (1,)
        )
        self.parts = (keep, flip(send, "ctx", 1))
        return keep

    def x(self, *after):
        mine, *away = fuse(x_kernel, self.place, [self.shape] * 4, self.parts, after)
        self.parts = (mine, *(flip(away[d - 1], "ctx", 2 * d) for d in (1, 2, 3)))
        return mine

    def z(self, *after):
        n = lax.axis_size("ctx")
        (mine,) = fuse(add_kernel, self.place, [self.shape], self.parts, after)
        for b in range(3, n.bit_length() - 1):
            (mine,) = fuse(
                add_kernel, self.place, [self.shape], (mine, flip(mine, "ctx", 1 << b))
            )
        self.parts = (mine, *(flip(mine, "ctx", d) for d in (2, 4, 6)))
        return mine

    def stack(self, *after):
        (every,) = fuse(stack_kernel, self.place, [(4,) + self.shape], self.parts, after)
        self.parts = (every, flip(every, "ctx", 1))
        return every


def send_down(x, levels):
    n = lax.axis_size("ctx")
    return lax.ppermute(x, "ctx", [(i, i - 2 * levels) for i in range(2 * levels, n)])


def local(
    tokens,
    cotangent,
    attn_gain,
    w_query,
    w_key,
    w_value,
    w_out,
    mlp_gain,
    w_gate,
    w_up,
    w_down,
    seq_lengths,
    seq_starts,
):
    seqs, rows, dim = tokens.shape
    n = seqs * rows
    n_ctx = lax.axis_size("ctx")
    me = lax.axis_index("ctx")
    index = lax.axis_index("fsdp").reshape(1).astype(jnp.int32)
    fs = w_query.shape[0]
    cot = jnp.transpose(cotangent, (0, 2, 1))

    used = KV_HEADS * LANES + HEADS * HEAD_DIM + 2
    width = used - used % -LANES
    vm = pl.BlockSpec(memory_space=pltpu.VMEM)
    first = call(pack_kernel, sds((fs, width), BF16), [vm] * 5, cost=1.5, out_specs=vm)(
        w_query, w_key, w_value, attn_gain, mlp_gain
    )
    first_shards = gather_shards(first)
    places = me * rows + jnp.arange(rows, dtype=jnp.int32)
    positions = (places[None, :] - seq_starts[:, None]).astype(F32)
    frequency = THETA ** (-(2.0 * jnp.arange(HEAD_DIM // 2, dtype=F32)) / HEAD_DIM)
    angles = (positions[:, :, None] * frequency).reshape(n, HEAD_DIM // 2)
    cos, sin = jnp.cos(angles), jnp.sin(angles)
    cosines = jnp.concatenate([cos] * 4, axis=1)
    sines = jnp.concatenate([-sin, sin] * 2, axis=1)

    ff, fd = w_gate.shape[1], w_down.shape[0]
    hbm = pl.BlockSpec(memory_space=pl.ANY)
    tiles = seqs * KV_HEADS
    weights, normed, queries, kv, gain_two, x = call(
        qkv_kernel,
        (
            sds((dim, width), BF16),
            sds((n, dim), BF16),
            sds((tiles, GROUP * rows, LANES), BF16),
            sds((tiles, rows, LANES), BF16),
            sds((1, dim), F32),
            sds((n, dim), BF16),
        ),
        [pl.BlockSpec(memory_space=pltpu.SMEM)] + [vm] * 7,
        cost=4.0,
        out_specs=(vm,) * 6,
    )(index, jnp.transpose(tokens, (0, 2, 1)), *first_shards, cosines, sines)

    gu_own, do_own = call(
        rest_pack_kernel,
        (sds((fs, 2 * ff), BF16), sds((fd + fs, dim), BF16)),
        [vm] * 4,
        cost=3.0,
        out_specs=(vm, vm),
    )(w_gate, w_up, w_down.T, w_out)
    gu_shards = gather_shards(gu_own)
    do_shards = gather_shards(do_own)

    spans = [seq_starts.astype(jnp.int32), (seq_starts + seq_lengths).astype(jnp.int32)]

    def info_of(bases):
        return jnp.concatenate([me.reshape(1).astype(jnp.int32), bases.astype(jnp.int32)] + spans)

    x_bit = me % 2
    if n_ctx <= 8 and n_ctx % 2 == 0:
        levels = n_ctx // 2
        up = [(i, i + 2) for i in range(n_ctx - 2)]
        down = [(i + 2, i) for i in range(n_ctx - 2)]
        pieces = []
        piece = kv
        for k in range(levels):
            other = flip(piece, "ctx", 1)
            pair = (me // 2 - k) * 2
            bases = jnp.stack([pair + x_bit, pair + 1 - x_bit]) * rows
            bases = jnp.where(pair >= 0, bases, FAR)
            pieces.append((bases, piece[None], other[None]))
            if k + 1 < levels:
                piece = lax.ppermute(piece, "ctx", up)
        carry = None
        for k in range(levels - 1):
            bases, a, b = pieces[k]
            carry = attend(info_of(bases), queries, a, b, carry, k == 0)
        bases, a, b = pieces[-1]
        last_piece = (info_of(bases), queries, a, b, True)
    else:
        every = lax.all_gather(kv, "ctx", axis=0)
        info = info_of(jnp.arange(n_ctx, dtype=jnp.int32) * rows)
        carry = attend(info, queries, every[0::2], every[1::2], None, True)
        last_piece = (info, queries, every[:1], every[:1], False)

    result, d_mid, d_out, stats, keep_mlp, send_mlp = middle(
        index, x, cot, gain_two, carry[0], carry[1], gu_shards, do_shards, *last_piece
    )

    place = jnp.stack([me & 1, (me >> 1) & 3, index[0]]).astype(jnp.int32)
    mlp = Sum(place, keep_mlp, send_mlp)
    if n_ctx <= 8 and n_ctx % 2 == 0:
        dq, last = None, ()
        dkv, partials = [], []
        for k in reversed(range(levels)):
            bases, a, b = pieces[k]
            extra = partials[0][1:] if k < levels - 2 else ()
            dq, da, db, *both = attend_back(
                info_of(bases),
                queries,
                d_out,
                stats,
                a,
                b,
                dq,
                k == 0,
                last,
                extra,
            )
            if extra:
                dkv.append(send_down(both[0], partials.pop(0)[0]))
            partials.append((k, da[0], flip(db[0], "ctx", 1)))
            last = (mlp.core(dq),) if k == levels - 1 else ()
        while len(partials) > 1:
            far, near, other = partials.pop(0)
            (both,) = fuse(add_kernel, place, [near.shape], (near, other), (dq,))
            dkv.append(send_down(both, far))
            last = (both,)
        dkv = [partials[0][1], partials[0][2]] + dkv
        last = (mlp.y(*last),)
    else:
        dq, da, db = attend_back(
            info, queries, d_out, stats, every[0::2], every[1::2], None, True
        )
        partial = jnp.stack([da, db], axis=1).reshape((n_ctx,) + da.shape[1:])
        dkv = [lax.psum_scatter(partial, "ctx", scatter_dimension=0, tiled=False)]
        mlp.core(dq)
        last = (mlp.y(dq),)

    input_grad, keep_q, send_q = finish(
        index, x, normed, weights, cosines, sines, dq, dkv, d_mid, last
    )
    qkv = Sum(place, keep_q, send_q)
    step = mlp.x(keep_q)
    step = qkv.core(step)
    step = mlp.z(step)
    step = qkv.y(step)
    step = qkv.x(step)
    step = mlp.stack(step)
    step = qkv.z(step)
    step = qkv.stack(step)
    grad_gate, grad_up, grad_down, grad_out, gain_two_grad = own(
        own_kernel,
        place,
        [(fs, ff), (fs, ff), (dim, fd), (fs, dim), (1, fs)],
        mlp.parts,
        (dim, dim),
    )
    grad_down = grad_down.T
    kv_width = KV_HEADS * HEAD_DIM
    grad_query, grad_key, grad_value, gain_one_grad = own(
        own_q_kernel,
        place,
        [(fs, HEADS * HEAD_DIM), (fs, kv_width), (fs, kv_width), (1, fs)],
        qkv.parts,
        (fs, width),
        (grad_gate,),
    )
    grad_mlp_gain = gain_two_grad.reshape(fs)
    grad_attn_gain = gain_one_grad.reshape(fs)
    return (
        jnp.transpose(result, (0, 2, 1)),
        jnp.transpose(input_grad, (0, 2, 1)),
        grad_attn_gain,
        grad_query,
        grad_key,
        grad_value,
        grad_out,
        grad_mlp_gain,
        grad_gate,
        grad_up,
        grad_down,
    )


def solution(mesh):
    rows3 = P("fsdp", "ctx", None)
    mat = P("fsdp", None)
    vec = P("fsdp")
    return jax.shard_map(
        local,
        mesh=mesh,
        in_specs=(rows3, rows3, vec, mat, mat, mat, mat, vec, mat, mat, mat, vec, vec),
        out_specs=(rows3, rows3, vec, mat, mat, mat, mat, vec, mat, mat, mat),
        check_vma=False,
    )
```

```python
import functools
import math

import jax
import jax.numpy as jnp
from jax import lax
from jax.experimental import pallas as pl
from jax.experimental.pallas import tpu as pltpu
from jax.sharding import PartitionSpec as P

HEADS = 9
KV_HEADS = 3
HEAD_DIM = 64
GROUP = HEADS // KV_HEADS
LANES = 128
EPSILON = 1e-05
THETA = 100000.0
SCALE = HEAD_DIM ** (-0.5)
MASKED = -2e30
LOWEST = -1e30
FAR = 1 << 29
CHUNKS = 8
SLOTS = (0, 2, 1, 3)
TOP = 40
BF16 = jnp.bfloat16
F32 = jnp.float32
NN = (((1,), (0,)), ((), ()))
NT = (((1,), (1,)), ((), ()))
TN = (((0,), (0,)), ((), ()))
VMEM_LIMIT = 64 * 1024 * 1024 - 65536
PER_US = 1.0e9


def dot(a, b, dims=NN):
    return lax.dot_general(a, b, dims, preferred_element_type=F32)


def call(kernel, out_shape, in_specs=None, cost=1.0, **kwargs):
    return pl.pallas_call(
        kernel,
        out_shape=out_shape,
        in_specs=in_specs,
        compiler_params=pltpu.CompilerParams(vmem_limit_bytes=VMEM_LIMIT),
        cost_estimate=pl.CostEstimate(
            flops=int(cost * PER_US), bytes_accessed=0, transcendentals=0
        ),
        **kwargs,
    )


def sds(shape, dtype):
    return jax.ShapeDtypeStruct(shape, dtype)


def lane_of(shape):
    return lax.broadcasted_iota(jnp.int32, shape, 1)


def swap_halves(tile):
    lane = lane_of(tile.shape) % HEAD_DIM
    return jnp.where(
        lane < HEAD_DIM // 2, pltpu.roll(tile, LANES - 32, 1), pltpu.roll(tile, 32, 1)
    )


def half_roll(tile):
    return pltpu.roll(tile, HEAD_DIM, 1)


def assemble(target, index, shards, rows):
    for code, ref in zip((0, 1, 2, 3), shards):
        start = pl.multiple_of((index ^ code) * rows, 16)
        target[pl.ds(start, rows), :] = ref[...]


def inverse_rms(rows):
    return lax.rsqrt(jnp.mean(rows * rows, axis=-1, keepdims=True) + EPSILON)


def qkv_kernel(index_ref, x_ref, w0, w1, w2, w3, cos_ref, sin_ref, w_ref, normed_ref, q_ref, kv_ref, two_ref, rows_ref):
    assemble(w_ref, index_ref[0], (w0, w1, w2, w3), w0.shape[0])
    width = w_ref.shape[1]
    gains = jnp.transpose(w_ref[:, width - LANES :].astype(F32))
    count = x_ref.shape[2]
    for r in range(x_ref.shape[0]):
        turned = jnp.transpose(x_ref[r].astype(F32))
        rows_ref[r * count : (r + 1) * count, :] = turned.astype(BF16)
    x = rows_ref[...].astype(F32)
    normed = (x * inverse_rms(x) * gains[HEAD_DIM : HEAD_DIM + 1, :]).astype(BF16)
    normed_ref[...] = normed
    two_ref[...] = gains[HEAD_DIM + 1 : HEAD_DIM + 2, :]
    cosines, sines = cos_ref[...], sin_ref[...]
    lane = lane_of(cosines.shape)
    low = lane < HEAD_DIM
    cos_kv = jnp.where(low, cosines, 1.0)
    sin_kv = jnp.where(low, sines, 0.0)
    rows = kv_ref.shape[1]
    seqs = x.shape[0] // rows
    for g in range(KV_HEADS):
        tile = dot(normed, w_ref[:, g * LANES : (g + 1) * LANES])
        turned = (tile * cos_kv + swap_halves(tile) * sin_kv).astype(BF16)
        for r in range(seqs):
            kv_ref[r * KV_HEADS + g] = turned[r * rows : (r + 1) * rows]
    first = KV_HEADS * LANES
    lin = dot(normed, w_ref[:, first:])
    for p in range((HEADS + 1) // 2):
        tile = lin[:, p * LANES : (p + 1) * LANES]
        turned = (tile * cosines + swap_halves(tile) * sines) * SCALE
        for h in (2 * p, 2 * p + 1):
            if h < HEADS:
                own = turned if h % 2 == 0 else half_roll(turned)
                own = jnp.where(low, own, 0.0).astype(BF16)
                g, i = divmod(h, GROUP)
                for r in range(seqs):
                    q_ref[r * KV_HEADS + g, i * rows : (i + 1) * rows] = own[
                        r * rows : (r + 1) * rows
                    ]


def pair_places(info_ref, step, rows, axis):
    shape = (1, 2 * rows) if axis == 1 else (2 * rows, 1)
    at = lax.broadcasted_iota(jnp.int32, shape, axis)
    first, second = info_ref[1 + 2 * step], info_ref[2 + 2 * step]
    return jnp.where(at < rows, first + at, second + at - rows)


def query_places(info_ref, rows, axis):
    total = GROUP * rows
    shape = (1, total) if axis == 1 else (total, 1)
    at = lax.broadcasted_iota(jnp.int32, shape, axis)
    return info_ref[0] * rows + at % rows


def seen_of(key_places, q_places, start, end, diagonal):
    key_in = (key_places >= start) & (key_places < end)
    query_in = (q_places >= start) & (q_places < end)
    seen = jnp.where(key_in, key_places, FAR) <= jnp.where(query_in, q_places, -1)
    if diagonal:
        seen = seen | (key_places == q_places)
    return seen


def row_active(info_ref, step, rows, start, end):
    own = info_ref[0] * rows
    first, second = info_ref[1 + 2 * step], info_ref[2 + 2 * step]
    keys_in = ((first < end) & (first + rows > start)) | ((second < end) & (second + rows > start))
    return (own < end) & (own + rows > start) & keys_in & (jnp.minimum(first, second) <= own)


def attend_rows(
    info_ref, step, steps, diagonal, q_ref, a_ref, b_ref, max_in, sum_in, max_ref, sum_ref
):
    rows = a_ref.shape[2]
    seqs = q_ref.shape[0] // KV_HEADS
    spans = 1 + 2 * steps

    def one_seq(r, unused):
        start = info_ref[spans + r]
        end = info_ref[spans + seqs + r]

        def one_row():
            seen = seen_of(
                pair_places(info_ref, step, rows, 1),
                query_places(info_ref, rows, 0),
                start,
                end,
                diagonal,
            )
            for g in range(KV_HEADS):
                rg = r * KV_HEADS + g
                kv = jnp.concatenate([a_ref[0, rg], b_ref[0, rg]], axis=0)
                scores = jnp.where(seen, dot(q_ref[rg], kv, NT), MASKED)
                old = max_in[rg]
                new = jnp.maximum(old, jnp.max(scores, axis=-1, keepdims=True))
                weights = jnp.exp(scores - jnp.concatenate([new, new], axis=1)).astype(BF16)
                ones = jnp.where(lane_of(kv.shape) < HEAD_DIM, jnp.ones_like(kv), kv)
                sum_ref[rg] = sum_in[rg] * jnp.exp(old - new) + dot(weights, ones)
                max_ref[rg] = new

        def keep_row():
            for g in range(KV_HEADS):
                max_ref[r * KV_HEADS + g] = max_in[r * KV_HEADS + g]
                sum_ref[r * KV_HEADS + g] = sum_in[r * KV_HEADS + g]

        if diagonal:
            one_row()
        else:
            active = row_active(info_ref, step, rows, start, end)
            pl.when(active)(one_row)
            if max_in is not max_ref:
                pl.when(jnp.logical_not(active))(keep_row)
        return unused

    lax.fori_loop(0, seqs, one_seq, 0)


def attend_kernel(steps, diagonal, fresh, info_ref, q_ref, a_ref, b_ref, *refs):
    if fresh:
        max_ref, sum_ref = refs
    else:
        max_in, sum_in, max_ref, sum_ref = refs
    step = pl.program_id(0)

    @pl.when(step == 0)
    def _():
        if fresh:
            max_ref[...] = jnp.full_like(max_ref, LOWEST)
            sum_ref[...] = jnp.zeros_like(sum_ref)
        else:
            max_ref[...] = max_in[...]
            sum_ref[...] = sum_in[...]

    attend_rows(
        info_ref, step, steps, diagonal, q_ref, a_ref, b_ref, max_ref, sum_ref, max_ref, sum_ref
    )


def attend(info, queries, a, b, carry, diagonal):
    steps = a.shape[0]
    tiles, total, _ = queries.shape
    rows = a.shape[2]
    whole = pl.BlockSpec((tiles, total, LANES), lambda i: (0, 0, 0))
    piece = pl.BlockSpec((1, tiles, rows, LANES), lambda i: (i, 0, 0, 0))
    return call(
        functools.partial(attend_kernel, steps, diagonal, carry is None),
        (sds((tiles, total, LANES), F32),) * 2,
        [pl.BlockSpec(memory_space=pltpu.SMEM), whole, piece, piece]
        + ([] if carry is None else [whole] * 2),
        cost=10.0 * steps,
        out_specs=(whole, whole),
        grid=(steps,),
    )(info, queries, a, b, *(carry or ()))


def attend_back_kernel(
    steps, diagonal, fresh, extra, info_ref, q_ref, d_ref, stat_ref, a_ref, b_ref, *refs
):
    if extra:
        refs[-1][...] = total_of(refs[-6][...], refs[-5][...])
        dq_ref, da_ref, db_ref = refs[-4:-1]
    else:
        dq_ref, da_ref, db_ref = refs[-3:]
    dq_in = refs[0]
    step = pl.program_id(0)
    rows = a_ref.shape[2]
    seqs = q_ref.shape[0] // KV_HEADS
    spans = 1 + 2 * steps

    @pl.when(step == 0)
    def _():
        dq_ref[...] = jnp.zeros_like(dq_ref) if fresh else dq_in[...]

    def one_seq(r, unused):
        start = info_ref[spans + r]
        end = info_ref[spans + seqs + r]

        def one_row():
            seen = seen_of(
                pair_places(info_ref, step, rows, 0),
                query_places(info_ref, rows, 1),
                start,
                end,
                diagonal,
            )
            for g in range(KV_HEADS):
                rg = r * KV_HEADS + g
                kv = jnp.concatenate([a_ref[0, rg], b_ref[0, rg]], axis=0)
                q, d = q_ref[rg], d_ref[rg]
                log_sum = stat_ref[rg, 0:1, :]
                delta = stat_ref[rg, 1:2, :]
                scores = jnp.where(seen, dot(kv, q, NT), MASKED)
                probs = jnp.exp(scores - log_sum)
                d_scores = (probs * (dot(kv, d, NT) - delta)).astype(BF16)
                grad = (dot(d_scores, q) + dot(probs.astype(BF16), d)).astype(BF16)
                da_ref[0, rg] = grad[:rows]
                db_ref[0, rg] = grad[rows:]
                dq_ref[rg] = dq_ref[rg] + dot(d_scores, kv, TN)

        if diagonal:
            one_row()
        else:
            active = row_active(info_ref, step, rows, start, end)
            pl.when(active)(one_row)

            @pl.when(jnp.logical_not(active))
            def _():
                for g in range(KV_HEADS):
                    rg = r * KV_HEADS + g
                    da_ref[0, rg] = jnp.zeros((rows, LANES), BF16)
                    db_ref[0, rg] = jnp.zeros((rows, LANES), BF16)

        return unused

    lax.fori_loop(0, seqs, one_seq, 0)


def attend_back(info, queries, d_out, stats, a, b, carry, diagonal, after=(), extra=()):
    steps = a.shape[0]
    tiles, total, _ = queries.shape
    rows = a.shape[2]
    whole = pl.BlockSpec((tiles, total, LANES), lambda i: (0, 0, 0))
    stat = pl.BlockSpec(stats.shape, lambda i: (0, 0, 0))
    one = pl.BlockSpec(a.shape[1:], lambda i: (0, 0, 0))
    piece = pl.BlockSpec((1, tiles, rows, LANES), lambda i: (i, 0, 0, 0))
    return call(
        functools.partial(attend_back_kernel, steps, diagonal, carry is None, bool(extra)),
        (sds((tiles, total, LANES), F32), sds(a.shape, BF16), sds(b.shape, BF16))
        + ((sds(a.shape[1:], BF16),) if extra else ()),
        [pl.BlockSpec(memory_space=pltpu.SMEM), whole, whole, stat, piece, piece]
        + ([] if carry is None else [whole])
        + [pl.BlockSpec(memory_space=pl.ANY)] * len(after)
        + [one] * len(extra),
        cost=0.05,
        out_specs=(whole, piece, piece) + ((one,) if extra else ()),
        grid=(steps,),
    )(info, queries, d_out, stats, a, b, *(() if carry is None else (carry,)), *after, *extra)


def middle_kernel(
    fused,
    index_ref,
    info_ref,
    x_ref,
    cot_in,
    gain_ref,
    max_ref,
    sum_ref,
    q_ref,
    a_ref,
    b_ref,
    gu0,
    gu1,
    gu2,
    gu3,
    do0,
    do1,
    do2,
    do3,
    turned_ref,
    d_mid_ref,
    d_ref,
    stat_ref,
    keep_ref,
    send_ref,
    out_ref,
    w_gu,
    w_down,
    w_out,
    att_ref,
    n2_ref,
    dn2_ref,
    g_gu,
    g_down,
    g_out,
    slot_ref,
    chunk_ref,
    stage_ref,
    max_out,
    sum_out,
    cot_ref,
    in_sems,
    out_sems,
):
    index = index_ref[0]
    dim = x_ref.shape[1]
    ff = w_down.shape[0]
    fd, fs = ff // 4, dim // 4
    loads = []
    for code, gu, do in zip((0, 1, 2, 3), (gu0, gu1, gu2, gu3), (do0, do1, do2, do3)):
        shard = index ^ code
        down_at = pl.ds(pl.multiple_of(shard * fd, 16), fd)
        at = pl.ds(pl.multiple_of(shard * fs, 16), fs)
        for source, target in (
            (do.at[pl.ds(fd, fs)], w_out.at[at]),
            (gu, w_gu.at[at]),
            (do.at[pl.ds(0, fd)], w_down.at[down_at]),
        ):
            loads.append(pltpu.make_async_copy(source, target, in_sems.at[len(loads)]))
    for copy in loads:
        copy.start()
    if fused:
        attend_rows(
            info_ref, 0, 1, False, q_ref, a_ref, b_ref, max_ref, sum_ref, max_out, sum_out
        )
        max_ref, sum_ref = max_out, sum_out
    tiles, total, _ = max_ref.shape
    seqs = tiles // KV_HEADS
    rows = total // GROUP
    low = lane_of((total, LANES)) < HEAD_DIM
    low_rows = low[:rows]
    outs = []
    for rg in range(tiles):
        sums = sum_ref[rg]
        turned = half_roll(sums)
        both = jnp.where(low, sums, turned)
        log_sum = max_ref[rg] + jnp.log(both)
        stat_ref[rg, 0:1, :] = jnp.transpose(log_sum)[0:1, :]
        normal = jnp.where(low, 0.0, sums / both)
        sum_ref_row = normal
        outs.append(sum_ref_row)
    for r in range(seqs):
        for p in range((HEADS + 1) // 2):
            g, i = divmod(2 * p, GROUP)
            tile = half_roll(outs[r * KV_HEADS + g][i * rows : (i + 1) * rows])
            if 2 * p + 1 < HEADS:
                g, i = divmod(2 * p + 1, GROUP)
                tile = jnp.where(
                    low_rows, tile, outs[r * KV_HEADS + g][i * rows : (i + 1) * rows]
                )
                att_ref[r * rows : (r + 1) * rows, p * LANES : (p + 1) * LANES] = tile.astype(BF16)
            else:
                att_ref[r * rows : (r + 1) * rows, p * LANES :] = tile[:, :HEAD_DIM].astype(BF16)
    for r in range(seqs):
        turned = jnp.transpose(cot_in[r].astype(F32))
        cot_ref[r * rows : (r + 1) * rows, :] = turned.astype(BF16)
    for copy in loads:
        copy.wait()
    att = att_ref[...]
    cot = cot_ref[...]
    mid = x_ref[...].astype(F32) + dot(att, w_out[...])
    inv = inverse_rms(mid)
    gain = gain_ref[...]
    n2 = (mid * inv * gain).astype(BF16)
    n2_ref[...] = n2
    out_ref[...] = mid
    dn2_ref[...] = jnp.zeros_like(dn2_ref)
    width = ff // 2

    def ff_step(i, carry):
        at = i * width
        cols, cols_up = pl.ds(at, width), pl.ds(at + ff, width)
        n2 = n2_ref[...]
        w_g, w_u, w_d = w_gu[:, cols], w_gu[:, cols_up], w_down[cols, :]
        gate = dot(n2, w_g)
        up = dot(n2, w_u)
        sig = 1.0 / (1.0 + jnp.exp(-gate))
        silu = gate * sig
        hidden = (silu * up).astype(BF16)
        out_ref[...] += dot(hidden, w_d)
        d_hidden = dot(cot_ref[...], w_d, NT)
        d_gate = (d_hidden * up * sig * (1.0 + gate * (1.0 - sig))).astype(BF16)
        d_up = (d_hidden * silu).astype(BF16)
        g_down[cols, :] = dot(hidden, cot_ref[...], TN)
        g_gu[:, cols] = dot(n2, d_gate, TN).astype(BF16)
        g_gu[:, cols_up] = dot(n2, d_up, TN).astype(BF16)
        dn2_ref[...] += dot(d_gate, w_g, NT) + dot(d_up, w_u, NT)
        return carry

    ff_step(0, 0)
    ff_step(1, 0)
    part = dim // CHUNKS
    quarter = 2 * ff // CHUNKS
    stores = []
    for slot in (2, 3, 0, 1):
        to = keep_ref if slot < 2 else send_ref
        at = pl.ds(pl.multiple_of((index ^ SLOTS[slot]) * fs, 16), fs)
        for c in range(CHUNKS):
            copy = pltpu.make_async_copy(
                g_gu.at[at, pl.ds(c * quarter, quarter)],
                to.at[slot % 2, c, pl.ds(0, fs)],
                out_sems.at[len(stores)],
            )
            copy.start()
            stores.append(copy)
    for r in range(seqs):
        turned_ref[r] = jnp.transpose(out_ref[r * rows : (r + 1) * rows, :])
    dn2 = dn2_ref[...]
    scaled = dn2 * gain
    gain_grad = jnp.sum(dn2 * mid * inv, axis=0, keepdims=True)
    d_mid = (
        cot.astype(F32)
        + inv * scaled
        - mid * (inv * inv * inv) * jnp.mean(scaled * mid, axis=-1, keepdims=True)
    )
    d_mid_ref[...] = d_mid
    d_low = d_mid.astype(BF16)
    g_out[...] = dot(att, d_low, TN)
    d_att = dot(d_low, w_out[...], NT)
    for r in range(seqs):
        for p in range((HEADS + 1) // 2):
            stop = min((p + 1) * LANES, dim)
            tile = d_att[r * rows : (r + 1) * rows, p * LANES : stop]
            if stop - p * LANES < LANES:
                tile = jnp.concatenate([tile, jnp.zeros_like(tile)], axis=1)
            for h in (2 * p, 2 * p + 1):
                if h < HEADS:
                    own = half_roll(tile) if h % 2 == 0 else tile
                    own = jnp.where(low_rows, 0.0, own).astype(BF16)
                    g, i = divmod(h, GROUP)
                    d_ref[r * KV_HEADS + g, i * rows : (i + 1) * rows] = own
    for rg in range(tiles):
        prod = d_ref[rg].astype(F32) * outs[rg]
        stat_ref[rg, 1:2, :] = jnp.sum(jnp.transpose(prod), axis=0, keepdims=True)
    for slot in (2, 3, 0, 1):
        shard = index ^ SLOTS[slot]
        to = keep_ref if slot < 2 else send_ref
        at = pl.ds(pl.multiple_of(shard * fs, 16), fs)
        slot_ref[0:fd, :] = g_down[pl.ds(pl.multiple_of(shard * fd, 16), fd), :]
        slot_ref[fd : fd + fs, :] = g_out[at, :]
        slot_ref[fd + fs :, :] = jnp.broadcast_to(gain_grad, (dim - fd - fs, dim))
        for c in range(CHUNKS):
            chunk_ref[:part, :] = slot_ref[c * part : (c + 1) * part, :quarter]
            top = slot_ref[c * part : c * part + TOP, quarter:]
            rest = slot_ref[c * part + TOP : (c + 1) * part, quarter:]
            fill = jnp.zeros((2 * TOP - part, dim - quarter), F32)
            chunk_ref[part:, :] = jnp.concatenate(
                [top, jnp.concatenate([rest, fill], axis=0)], axis=1
            )
            stage_ref[slot, c] = chunk_ref[...].astype(BF16)
        copy = pltpu.make_async_copy(
            stage_ref.at[slot],
            to.at[slot % 2, pl.ds(0, CHUNKS), pl.ds(fs, part + TOP)],
            out_sems.at[len(stores)],
        )
        copy.start()
        stores.append(copy)
    for copy in stores:
        copy.wait()


def middle(index, x, cot, gain, top, sums, gu, do, info, queries, a, b, fused):
    n, dim = x.shape
    tiles, total, _ = top.shape
    ff2 = gu[0].shape[1]
    ff = ff2 // 2
    chunk = (dim // 4 + dim // CHUNKS + TOP, ff2 // CHUNKS)
    small = (dim // CHUNKS + TOP, ff2 // CHUNKS)
    pair = sds((2, CHUNKS) + chunk, BF16)
    vm = pl.BlockSpec(memory_space=pltpu.VMEM)
    sm = pl.BlockSpec(memory_space=pltpu.SMEM)
    hbm = pl.BlockSpec(memory_space=pl.ANY)
    return call(
        functools.partial(middle_kernel, fused),
        (
            sds((tiles // KV_HEADS, dim, total // GROUP), F32),
            sds((n, dim), F32),
            sds((tiles, total, LANES), BF16),
            sds((tiles, 8, total), F32),
            pair,
            pair,
        ),
        [sm, sm] + [vm] * 8 + [hbm] * 8,
        cost=20.0,
        out_specs=(vm,) * 4 + (hbm,) * 2,
        scratch_shapes=[
            pltpu.VMEM((n, dim), F32),
            pltpu.VMEM((dim, ff2), BF16),
            pltpu.VMEM((ff, dim), BF16),
            pltpu.VMEM((dim, dim), BF16),
            pltpu.VMEM((n, dim), BF16),
            pltpu.VMEM((n, dim), BF16),
            pltpu.VMEM((n, dim), F32),
            pltpu.VMEM((dim, ff2), BF16),
            pltpu.VMEM((ff, dim), F32),
            pltpu.VMEM((dim, dim), F32),
            pltpu.VMEM((dim, dim), F32),
            pltpu.VMEM(small, F32),
            pltpu.VMEM((4, CHUNKS) + small, BF16),
            pltpu.VMEM((tiles, total, LANES), F32),
            pltpu.VMEM((tiles, total, LANES), F32),
            pltpu.VMEM((n, dim), BF16),
            pltpu.SemaphoreType.DMA((12,)),
            pltpu.SemaphoreType.DMA((4 * CHUNKS + 4,)),
        ],
    )(index, info, x, cot, gain, top, sums, queries, a, b, *gu, *do)


def end_kernel(
    index_ref,
    x_ref,
    normed_ref,
    w_ref,
    cos_ref,
    sin_ref,
    dq_ref,
    d_mid_ref,
    *refs,
    parts,
):
    dkv_refs = refs[:parts]
    grad_ref, keep, send, lin_ref, g_ref = refs[-5:]
    index = index_ref[0]
    width = w_ref.shape[1]
    tiles, rows, _ = dkv_refs[0].shape
    seqs = tiles // KV_HEADS
    low = lane_of((rows, LANES)) < HEAD_DIM
    for r in range(seqs):
        at = slice(r * rows, (r + 1) * rows)
        cosines, sines = cos_ref[at, :], sin_ref[at, :]
        cos_kv = jnp.where(low, cosines, 1.0)
        sin_kv = jnp.where(low, sines, 0.0)
        for g in range(KV_HEADS):
            tile = dkv_refs[0][r * KV_HEADS + g].astype(F32)
            for ref in dkv_refs[1:]:
                tile = tile + ref[r * KV_HEADS + g].astype(F32)
            back = tile * cos_kv - swap_halves(tile) * sin_kv
            lin_ref[at, g * LANES : (g + 1) * LANES] = back.astype(BF16)
        first = KV_HEADS * LANES
        for p in range((HEADS + 1) // 2):
            backs = []
            for h in (2 * p, 2 * p + 1):
                if h < HEADS:
                    g, i = divmod(h, GROUP)
                    tile = dq_ref[r * KV_HEADS + g, i * rows : (i + 1) * rows]
                    backs.append((tile * cosines - swap_halves(tile) * sines) * SCALE)
                else:
                    backs.append(jnp.zeros((rows, LANES), F32))
            tile = jnp.where(low, backs[0], half_roll(backs[1]))
            lin_ref[at, first + p * LANES : first + (p + 1) * LANES] = tile.astype(BF16)
    lin = lin_ref[...]
    g_ref[...] = dot(normed_ref[...], lin, TN)
    d_normed = dot(lin, w_ref[...], NT)
    gains = jnp.transpose(w_ref[:, width - LANES :].astype(F32))
    gain = gains[HEAD_DIM : HEAD_DIM + 1, :]
    x = x_ref[...].astype(F32)
    inv = inverse_rms(x)
    scaled = d_normed * gain
    grad = (
        d_mid_ref[...]
        + inv * scaled
        - x * (inv * inv * inv) * jnp.mean(scaled * x, axis=-1, keepdims=True)
    )
    for r in range(seqs):
        grad_ref[r] = jnp.transpose(grad[r * rows : (r + 1) * rows, :])
    gain_grad = jnp.sum(d_normed * x * inv, axis=0, keepdims=True)
    dim = x.shape[1]
    fs = dim // 4
    for slot in range(4):
        at = pl.ds(pl.multiple_of((index ^ SLOTS[slot]) * fs, 16), fs)
        to = keep if slot < 2 else send
        for c in range(CHUNKS):
            tile = g_ref[at, c * LANES : (c + 1) * LANES]
            if c == CHUNKS - 1:
                pad = jnp.concatenate(
                    [gain_grad[:, k * HEAD_DIM : (k + 1) * HEAD_DIM] for k in range(HEADS)]
                    + [jnp.zeros((fs - HEADS, HEAD_DIM), F32)],
                    axis=0,
                )
                tile = jnp.concatenate([tile[:, :HEAD_DIM], pad], axis=1)
            to[slot % 2, c] = tile.astype(BF16)


def finish(index, x, normed, w, cosines, sines, dq, dkv, d_mid, after):
    n, dim = x.shape
    width = w.shape[1]
    vm = pl.BlockSpec(memory_space=pltpu.VMEM)
    pair = sds((2, CHUNKS, dim // 4, width // CHUNKS), BF16)
    tiles = dkv[0].shape[0]
    return call(
        functools.partial(end_kernel, parts=len(dkv)),
        (sds((tiles // KV_HEADS, dim, dkv[0].shape[1]), F32), pair, pair),
        [pl.BlockSpec(memory_space=pltpu.SMEM)] + [vm] * (7 + len(dkv))
        + [pl.BlockSpec(memory_space=pl.ANY)] * len(after),
        cost=0.05,
        out_specs=(vm,) * 3,
        scratch_shapes=[pltpu.VMEM((n, width), BF16), pltpu.VMEM((dim, width), F32)],
    )(index, x, normed, w, cosines, sines, dq, d_mid, *dkv, *after)


def both_halves(place_ref, parts, d):
    near, far = parts[0][d].astype(F32), parts[1][d].astype(F32)
    flag = place_ref[0] == 0
    return place_ref[1] ^ d, jnp.where(flag, near, far), jnp.where(flag, far, near)


def own_gain(place_ref, row, out_ref):
    size = out_ref.shape[1]
    rows = jnp.broadcast_to(row, (8, row.shape[1]))
    fill = -row.shape[1] % LANES
    rows = jnp.concatenate([rows, jnp.zeros((8, fill), F32)], axis=1)
    turned = pltpu.roll(rows, rows.shape[1] - place_ref[2] * size, 1)
    out_ref[...] = turned[0:1, :size]


def own_kernel(place_ref, *refs):
    parts = refs[:-6]
    gate_ref, up_ref, down_ref, out_ref, gain_ref, all_ref = refs[-6:]
    own_body(place_ref, parts, gate_ref, up_ref, down_ref, out_ref, gain_ref, all_ref)


def own_body(place_ref, parts, gate_ref, up_ref, down_ref, out_ref, gain_ref, all_ref):
    cols = parts[0].shape[-1]
    fs, dim = out_ref.shape
    fd = down_ref.shape[1]
    part = dim // CHUNKS
    width = dim - cols
    for d in range(4):
        quarter, first, second = both_halves(place_ref, parts, d)
        at = pl.ds(pl.multiple_of(quarter * cols, LANES), cols)
        gate_ref[:, at] = first[:fs]
        up_ref[:, at] = second[:fs]
        for c, chunk in ((quarter, first), (4 + quarter, second)):
            start = c * part
            all_ref[pl.ds(pl.multiple_of(start, 8), part), :cols] = chunk[fs : fs + part]
            right = chunk[fs + part :]
            all_ref[pl.ds(pl.multiple_of(start, 8), TOP), cols:] = right[:, :width]
            all_ref[pl.ds(pl.multiple_of(start + TOP, 8), part - TOP), cols:] = right[
                : part - TOP, width:
            ]
    down_ref[...] = jnp.transpose(all_ref[:fd, :])
    out_ref[...] = all_ref[fd : fd + fs, :]
    own_gain(place_ref, all_ref[fd + fs : fd + fs + 1, :], gain_ref)


def own_q_kernel(place_ref, *refs):
    parts = refs[:2]
    query_ref, key_ref, value_ref, gain_ref, all_ref = refs[-5:]
    for d in range(4):
        quarter, first, second = both_halves(place_ref, parts, d)
        all_ref[:, pl.ds(pl.multiple_of(quarter * LANES, LANES), LANES)] = first
        all_ref[:, pl.ds(pl.multiple_of((4 + quarter) * LANES, LANES), LANES)] = second
    first = KV_HEADS * LANES
    for g in range(KV_HEADS):
        to = slice(g * HEAD_DIM, (g + 1) * HEAD_DIM)
        key_ref[:, to] = all_ref[:, g * LANES : g * LANES + HEAD_DIM]
        value_ref[:, to] = all_ref[:, g * LANES + HEAD_DIM : (g + 1) * LANES]
    query_ref[...] = all_ref[:, first : first + HEADS * HEAD_DIM]
    start = all_ref.shape[1] - HEAD_DIM
    row = jnp.concatenate([all_ref[k : k + 1, start:] for k in range(HEADS)], axis=1)
    own_gain(place_ref, row, gain_ref)


def own(kernel, place, outs, parts, scratch, after=()):
    vm = pl.BlockSpec(memory_space=pltpu.VMEM)
    return call(
        kernel,
        tuple(sds(shape, F32) for shape in outs),
        [pl.BlockSpec(memory_space=pltpu.SMEM)]
        + [vm] * len(parts)
        + [pl.BlockSpec(memory_space=pl.ANY)] * len(after),
        cost=0.05,
        out_specs=(vm,) * len(outs),
        scratch_shapes=[pltpu.VMEM(scratch, F32)],
    )(place, *parts, *after)


def pack_kernel(q_ref, k_ref, v_ref, one_ref, two_ref, out_ref):
    for g in range(KV_HEADS):
        at = slice(g * HEAD_DIM, (g + 1) * HEAD_DIM)
        out_ref[:, g * LANES : g * LANES + HEAD_DIM] = k_ref[:, at]
        out_ref[:, g * LANES + HEAD_DIM : (g + 1) * LANES] = v_ref[:, at]
    first = KV_HEADS * LANES
    full = HEADS * HEAD_DIM
    out_ref[:, first : first + full] = q_ref[...]
    fs = q_ref.shape[0]
    row = lax.broadcasted_iota(jnp.int32, (LANES, fs), 0)
    gains = jnp.where(row == HEAD_DIM, one_ref[...].astype(F32)[None, :], 0.0)
    gains = jnp.where(row == HEAD_DIM + 1, two_ref[...].astype(F32)[None, :], gains)
    out_ref[:, first + full :] = jnp.transpose(gains)[:, HEAD_DIM:].astype(BF16)


def rest_pack_kernel(gate_ref, up_ref, down_ref, w_ref, gu_ref, do_ref):
    ff = gate_ref.shape[1]
    gu_ref[:, :ff] = gate_ref[...]
    gu_ref[:, ff:] = up_ref[...]
    fd = down_ref.shape[1]
    do_ref[:fd, :] = jnp.transpose(down_ref[...].astype(F32)).astype(BF16)
    do_ref[fd:, :] = w_ref[...]


def flip(x, axis, mask):
    n = lax.axis_size(axis)
    return lax.ppermute(x, axis, [(i, i ^ mask) for i in range(n)])


def gather_shards(own):
    across = flip(own, "fsdp", 2)
    return own, flip(own, "fsdp", 1), across, flip(across, "fsdp", 1)


def add(a, b):
    return (a.astype(F32) + b.astype(F32)).astype(BF16)


def total_of(*parts):
    total = parts[0].astype(F32)
    for part in parts[1:]:
        total = total + part.astype(F32)
    return total.astype(BF16)


def add_kernel(place_ref, *refs):
    refs[-1][...] = total_of(*(ref[...] for ref in refs[:-1]))


def core_kernel(place_ref, keep, got, *refs):
    out, keep_all, got_all, out_all, sems = refs[-5:]
    loads = []
    for c in range(CHUNKS):
        for i, (source, target) in enumerate(((keep, keep_all), (got, got_all))):
            copy = pltpu.make_async_copy(source.at[1, c], target.at[c], sems.at[i, c])
            copy.start()
            loads.append(copy)
    stores = []
    for c in range(CHUNKS):
        loads[2 * c].wait()
        loads[2 * c + 1].wait()
        out_all[c] = total_of(keep_all[c], got_all[c])
        copy = pltpu.make_async_copy(out_all.at[c], out.at[c], sems.at[2, c])
        copy.start()
        stores.append(copy)
    for copy in stores:
        copy.wait()


def core_sum(place, keep, got, after):
    hbm = pl.BlockSpec(memory_space=pl.ANY)
    shape = keep.shape[1:]
    return call(
        core_kernel,
        sds(shape, BF16),
        [pl.BlockSpec(memory_space=pltpu.SMEM)] + [hbm] * (2 + len(after)),
        cost=0.05,
        out_specs=hbm,
        scratch_shapes=[pltpu.VMEM(shape, BF16)] * 3 + [pltpu.SemaphoreType.DMA((3, CHUNKS))],
    )(place, keep, got, *after)


def y_kernel(place_ref, keep, got, far, *refs):
    mine, away, keep_all, got_all, far_all, mine_all, away_all, sems = refs[-8:]
    x_bit = place_ref[0]
    plan = [(4 * (1 - x_bit) + c, away_all, away, c) for c in range(4)]
    plan += [(4 * x_bit + c, mine_all, mine, c) for c in range(4)]
    loads = []
    for at, (chunk, *_) in enumerate(plan):
        sources = ((keep.at[0], keep_all), (got.at[0], got_all), (far, far_all))
        for i, (source, target) in enumerate(sources):
            copy = pltpu.make_async_copy(source.at[chunk], target.at[at], sems.at[i, at])
            copy.start()
            loads.append(copy)
    stores = []
    for at, (chunk, held, target, c) in enumerate(plan):
        for copy in loads[3 * at : 3 * at + 3]:
            copy.wait()
        held[c] = total_of(keep_all[at], got_all[at], far_all[at])
        copy = pltpu.make_async_copy(held.at[c], target.at[c], sems.at[3, at])
        copy.start()
        stores.append(copy)
    for copy in stores:
        copy.wait()


def y_sum(place, keep, got, far, after):
    hbm = pl.BlockSpec(memory_space=pl.ANY)
    whole, half = far.shape, (4,) + far.shape[1:]
    return call(
        y_kernel,
        (sds(half, BF16), sds(half, BF16)),
        [pl.BlockSpec(memory_space=pltpu.SMEM)] + [hbm] * (3 + len(after)),
        cost=0.05,
        out_specs=(hbm, hbm),
        scratch_shapes=[pltpu.VMEM(whole, BF16)] * 3
        + [pltpu.VMEM(half, BF16)] * 2
        + [pltpu.SemaphoreType.DMA((4, CHUNKS))],
    )(place, keep, got, far, *after)


def x_kernel(place_ref, keep, got, *outs):
    for d in range(4):
        c = place_ref[1] ^ d
        outs[d][...] = total_of(keep[c], got[c])


def stack_kernel(place_ref, *refs):
    for d in range(4):
        refs[4][d] = refs[d][...]


def fuse(kernel, place, outs, ins, after=(), specs=None, out_specs=None, grid=None):
    vm = pl.BlockSpec(memory_space=pltpu.VMEM)
    count = 1 + len(ins)

    def body(*refs):
        kernel(*refs[:count], *refs[count + len(after) :])

    return call(
        body,
        tuple(sds(shape, BF16) for shape in outs),
        [pl.BlockSpec(memory_space=pltpu.SMEM)]
        + (specs or [vm] * len(ins))
        + [pl.BlockSpec(memory_space=pl.ANY)] * len(after),
        cost=0.05,
        out_specs=out_specs or (vm,) * len(outs),
        **({"grid": grid} if grid else {}),
    )(place, *ins, *after)


class Sum:
    def __init__(self, place, keep, send):
        self.place, self.shape = place, keep.shape[2:]
        self.parts = (keep, flip(send, "fsdp", 1))

    def core(self, *after):
        keep, got = self.parts
        away = core_sum(self.place, keep, got, after)
        self.parts = (keep, got, flip(away, "fsdp", 2))
        return away

    def y(self, *after):
        keep, send = y_sum(self.place, *self.parts, after)
        self.parts = (keep, flip(send, "ctx", 1))
        return keep

    def x(self, *after):
        mine, *away = fuse(x_kernel, self.place, [self.shape] * 4, self.parts, after)
        self.parts = (mine, *(flip(away[d - 1], "ctx", 2 * d) for d in (1, 2, 3)))
        return mine

    def z(self, *after):
        n = lax.axis_size("ctx")
        (mine,) = fuse(add_kernel, self.place, [self.shape], self.parts, after)
        for b in range(3, n.bit_length() - 1):
            (mine,) = fuse(
                add_kernel, self.place, [self.shape], (mine, flip(mine, "ctx", 1 << b))
            )
        self.parts = (mine, *(flip(mine, "ctx", d) for d in (2, 4, 6)))
        return mine

    def stack(self, *after):
        (every,) = fuse(stack_kernel, self.place, [(4,) + self.shape], self.parts, after)
        self.parts = (every, flip(every, "ctx", 1))
        return every


def send_down(x, levels):
    n = lax.axis_size("ctx")
    return lax.ppermute(x, "ctx", [(i, i - 2 * levels) for i in range(2 * levels, n)])


def local(
    tokens,
    cotangent,
    attn_gain,
    w_query,
    w_key,
    w_value,
    w_out,
    mlp_gain,
    w_gate,
    w_up,
    w_down,
    seq_lengths,
    seq_starts,
):
    seqs, rows, dim = tokens.shape
    n = seqs * rows
    n_ctx = lax.axis_size("ctx")
    me = lax.axis_index("ctx")
    index = lax.axis_index("fsdp").reshape(1).astype(jnp.int32)
    fs = w_query.shape[0]
    cot = jnp.transpose(cotangent, (0, 2, 1))

    used = KV_HEADS * LANES + HEADS * HEAD_DIM + 2
    width = used - used % -LANES
    vm = pl.BlockSpec(memory_space=pltpu.VMEM)
    first = call(pack_kernel, sds((fs, width), BF16), [vm] * 5, cost=1.5, out_specs=vm)(
        w_query, w_key, w_value, attn_gain, mlp_gain
    )
    first_shards = gather_shards(first)
    places = me * rows + jnp.arange(rows, dtype=jnp.int32)
    positions = (places[None, :] - seq_starts[:, None]).astype(F32)
    frequency = THETA ** (-(2.0 * jnp.arange(HEAD_DIM // 2, dtype=F32)) / HEAD_DIM)
    angles = (positions[:, :, None] * frequency).reshape(n, HEAD_DIM // 2)
    cos, sin = jnp.cos(angles), jnp.sin(angles)
    cosines = jnp.concatenate([cos] * 4, axis=1)
    sines = jnp.concatenate([-sin, sin] * 2, axis=1)

    ff, fd = w_gate.shape[1], w_down.shape[0]
    hbm = pl.BlockSpec(memory_space=pl.ANY)
    tiles = seqs * KV_HEADS
    weights, normed, queries, kv, gain_two, x = call(
        qkv_kernel,
        (
            sds((dim, width), BF16),
            sds((n, dim), BF16),
            sds((tiles, GROUP * rows, LANES), BF16),
            sds((tiles, rows, LANES), BF16),
            sds((1, dim), F32),
            sds((n, dim), BF16),
        ),
        [pl.BlockSpec(memory_space=pltpu.SMEM)] + [vm] * 7,
        cost=4.0,
        out_specs=(vm,) * 6,
    )(index, jnp.transpose(tokens, (0, 2, 1)), *first_shards, cosines, sines)

    gu_own, do_own = call(
        rest_pack_kernel,
        (sds((fs, 2 * ff), BF16), sds((fd + fs, dim), BF16)),
        [vm] * 4,
        cost=3.0,
        out_specs=(vm, vm),
    )(w_gate, w_up, w_down.T, w_out)
    gu_shards = gather_shards(gu_own)
    do_shards = gather_shards(do_own)

    spans = [seq_starts.astype(jnp.int32), (seq_starts + seq_lengths).astype(jnp.int32)]

    def info_of(bases):
        return jnp.concatenate([me.reshape(1).astype(jnp.int32), bases.astype(jnp.int32)] + spans)

    x_bit = me % 2
    if n_ctx <= 8 and n_ctx % 2 == 0:
        levels = n_ctx // 2
        up = [(i, i + 2) for i in range(n_ctx - 2)]
        down = [(i + 2, i) for i in range(n_ctx - 2)]
        pieces = []
        piece = kv
        for k in range(levels):
            other = flip(piece, "ctx", 1)
            pair = (me // 2 - k) * 2
            bases = jnp.stack([pair + x_bit, pair + 1 - x_bit]) * rows
            bases = jnp.where(pair >= 0, bases, FAR)
            pieces.append((bases, piece[None], other[None]))
            if k + 1 < levels:
                piece = lax.ppermute(piece, "ctx", up)
        carry = None
        for k in range(levels - 1):
            bases, a, b = pieces[k]
            carry = attend(info_of(bases), queries, a, b, carry, k == 0)
        bases, a, b = pieces[-1]
        last_piece = (info_of(bases), queries, a, b, True)
    else:
        every = lax.all_gather(kv, "ctx", axis=0)
        info = info_of(jnp.arange(n_ctx, dtype=jnp.int32) * rows)
        carry = attend(info, queries, every[0::2], every[1::2], None, True)
        last_piece = (info, queries, every[:1], every[:1], False)

    result, d_mid, d_out, stats, keep_mlp, send_mlp = middle(
        index, x, cot, gain_two, carry[0], carry[1], gu_shards, do_shards, *last_piece
    )

    place = jnp.stack([me & 1, (me >> 1) & 3, index[0]]).astype(jnp.int32)
    mlp = Sum(place, keep_mlp, send_mlp)
    if n_ctx <= 8 and n_ctx % 2 == 0:
        dq, last = None, ()
        dkv, partials = [], []
        for k in reversed(range(levels)):
            bases, a, b = pieces[k]
            extra = partials[0][1:] if k < levels - 2 else ()
            dq, da, db, *both = attend_back(
                info_of(bases),
                queries,
                d_out,
                stats,
                a,
                b,
                dq,
                k == 0,
                last,
                extra,
            )
            if extra:
                dkv.append(send_down(both[0], partials.pop(0)[0]))
            partials.append((k, da[0], flip(db[0], "ctx", 1)))
            last = (mlp.core(dq),) if k == levels - 1 else ()
        while len(partials) > 1:
            far, near, other = partials.pop(0)
            (both,) = fuse(add_kernel, place, [near.shape], (near, other), (dq,))
            dkv.append(send_down(both, far))
            last = (both,)
        dkv = [partials[0][1], partials[0][2]] + dkv
        last = (mlp.y(*last),)
    else:
        dq, da, db = attend_back(
            info, queries, d_out, stats, every[0::2], every[1::2], None, True
        )
        partial = jnp.stack([da, db], axis=1).reshape((n_ctx,) + da.shape[1:])
        dkv = [lax.psum_scatter(partial, "ctx", scatter_dimension=0, tiled=False)]
        mlp.core(dq)
        last = (mlp.y(dq),)

    input_grad, keep_q, send_q = finish(
        index, x, normed, weights, cosines, sines, dq, dkv, d_mid, last
    )
    qkv = Sum(place, keep_q, send_q)
    step = mlp.x(keep_q)
    step = qkv.core(step)
    step = mlp.z(step)
    step = qkv.y(step)
    step = qkv.x(step)
    step = mlp.stack(step)
    step = qkv.z(step)
    step = qkv.stack(step)
    grad_gate, grad_up, grad_down, grad_out, gain_two_grad = own(
        own_kernel,
        place,
        [(fs, ff), (fs, ff), (dim, fd), (fs, dim), (1, fs)],
        mlp.parts,
        (dim, dim),
    )
    grad_down = grad_down.T
    kv_width = KV_HEADS * HEAD_DIM
    grad_query, grad_key, grad_value, gain_one_grad = own(
        own_q_kernel,
        place,
        [(fs, HEADS * HEAD_DIM), (fs, kv_width), (fs, kv_width), (1, fs)],
        qkv.parts,
        (fs, width),
        (grad_gate,),
    )
    grad_mlp_gain = gain_two_grad.reshape(fs)
    grad_attn_gain = gain_one_grad.reshape(fs)
    return (
        jnp.transpose(result, (0, 2, 1)),
        jnp.transpose(input_grad, (0, 2, 1)),
        grad_attn_gain,
        grad_query,
        grad_key,
        grad_value,
        grad_out,
        grad_mlp_gain,
        grad_gate,
        grad_up,
        grad_down,
    )


def solution(mesh):
    rows3 = P("fsdp", "ctx", None)
    mat = P("fsdp", None)
    vec = P("fsdp")
    return jax.shard_map(
        local,
        mesh=mesh,
        in_specs=(rows3, rows3, vec, mat, mat, mat, mat, vec, mat, mat, mat, vec, vec),
        out_specs=(rows3, rows3, vec, mat, mat, mat, mat, vec, mat, mat, mat),
        check_vma=False,
    )
```
